256 devices in a mesh: row: 128 (over z, y, x_lo, core), col: 2 (over x_hi).
Axes of the slice: x: 4 (x_hi: 2, x_lo: 2; x = x_hi * 2 + x_lo), y: 4, z: 8, core: 2. Of those that a mesh axis runs over, the one named last changes fastest.
Arguments:
- tall_panel_array: float32 [128, 1048576], P('col', 'row')
- row_signs: int32 [1048576], P('row'), may hold values from -1 to 1, as said below
- sample_rows: int32 [4096], replicated, may hold values from 0 to 1048575, as said below
Outputs:
- orthobasis: float32 [128, 4096], P('col', 'row')
- triangular: float32 [128, 128], P('col')
The draws below stay inside these ranges and needn't reach their ends.
Inputs may be any that keep to these rules, and one draw needn't show every extreme that they name: `row_signs`: each entry is -1 or +1. `sample_rows`: sketch row s keeps a panel row of the block from (s // 32) * 8192 to (s // 32 + 1) * 8192 - 1; a panel row may be kept more than once.
All inputs are finite; a program needn't handle non-finite values.
Results may differ from the reference program's by a relative error of at most 0.00016.
Values sent between devices are 32-bit elements; how exact they have to be, the bound alone decides.
A program may use at most 64 MiB of HBM per device.

```python
import jax
import jax.numpy as jnp
from jax import lax

COLS = 128
SAMP_DEV = 32
ROWS = 1048576
SAMPLES = 4096
N_ROW = 128


def draw_tall_panel_array(key, part):
    key = jax.random.fold_in(key, 2)
    keys = jax.random.split(key, 3)
    base = jax.random.normal(keys[0], (COLS, ROWS), jnp.float32)
    colscale = jnp.exp(jax.random.uniform(keys[1], (COLS, 1), jnp.float32, jnp.log(0.3), jnp.log(3.0)))
    rowscale = jnp.exp(jax.random.uniform(keys[2], (1, ROWS), jnp.float32, jnp.log(0.3), jnp.log(3.0)))
    return base * colscale * rowscale


def draw_row_signs(key, part):
    key = jax.random.fold_in(key, 5)
    return 2 * jax.random.randint(key, (ROWS,), 0, 2, jnp.int32) - 1


def draw_sample_rows(key, part):
    key = jax.random.fold_in(key, 7)
    block_rows = ROWS // N_ROW
    offsets = jax.random.randint(key, (SAMPLES,), 0, block_rows, jnp.int32)
    sample_iota = jnp.arange(SAMPLES, dtype=jnp.int32)
    offsets = jnp.where(sample_iota == 0, 0, offsets)
    offsets = jnp.where(sample_iota == SAMPLES - 1, block_rows - 1, offsets)
    return sample_iota // SAMP_DEV * block_rows + offsets


def setup_inputs(seed: int = 0) -> dict:
    seeds = jax.random.split(jax.random.key(seed), 4)
    return {
        "tall_panel_array": draw_tall_panel_array(jax.random.fold_in(seeds[3], 71), 0),
        "row_signs": draw_row_signs(jax.random.fold_in(seeds[3], 71), 0),
        "sample_rows": draw_sample_rows(jax.random.fold_in(seeds[3], 71), 0),
    }


def parity_sign(first, second, nbits):
    total = jnp.zeros_like(first + second)
    for bit_index in range(nbits):
        total = total + jnp.bitwise_and(jnp.right_shift(first, bit_index), 1) * jnp.bitwise_and(jnp.right_shift(second, bit_index), 1)
    return 1 - 2 * (total % 2)

def walsh_last(values):
    length = values.shape[-1]
    leading = values.shape[:-1]
    stride = 1
    while stride < length:
        reshaped_panel = values.reshape(leading + (length // (2 * stride), 2, stride))
        first_half = reshaped_panel[..., 0, :]
        second_half = reshaped_panel[..., 1, :]
        values = jnp.stack([first_half + second_half, first_half - second_half], axis=-2).reshape(leading + (length,))
        stride = stride * 2
    return values

def reference(tall_panel_array, row_signs, sample_rows):
    columns, total_rows = tall_panel_array.shape
    row_count = N_ROW
    local_rows = total_rows // row_count
    sign_flipped_rows = tall_panel_array * row_signs.astype(jnp.float32)[None, :]
    device_local_part = walsh_last(sign_flipped_rows.reshape(columns, row_count, local_rows))
    owner_device = (sample_rows // local_rows).astype(jnp.int32)
    local_spot = (sample_rows % local_rows).astype(jnp.int32)
    selected_rows = device_local_part[:, :, local_spot]
    devices_iota = jnp.arange(row_count, dtype=jnp.int32)
    signing = parity_sign(devices_iota[:, None], owner_device[None, :], row_count.bit_length() - 1).astype(jnp.float32)
    sketch = lax.optimization_barrier(jnp.sum(selected_rows * signing[None, :, :], axis=1)) / jnp.sqrt(jnp.float32(total_rows))
    sample_indices = sketch.shape[1]
    gram_matrix = jnp.dot(sketch.astype(jnp.float32), sketch.T.astype(jnp.float32), preferred_element_type=jnp.float32, precision=lax.Precision.HIGHEST) / jnp.float32(sample_indices)
    lower_factor = jnp.linalg.cholesky(gram_matrix)
    orthobasis = jax.scipy.linalg.solve_triangular(lower_factor, sketch, lower=True)
    return (orthobasis, lower_factor.T)
```

```python
import functools

import jax
import jax.numpy as jnp
import numpy as np
from jax import lax
from jax.experimental import pallas as pl
from jax.experimental.pallas import tpu as pltpu
from jax.sharding import PartitionSpec as P

F32 = jnp.float32
BF16 = jnp.bfloat16
MESH = pl.DeviceIdType.MESH
LO = 256
ORDER = (4, 3, 5, 2, 6, 1, 7, 0)


def hadamard(n):
    h = np.ones((1, 1), np.float32)
    while h.shape[0] < n:
        h = np.block([[h, h], [h, -h]])
    return h


def local_kernel(x_ref, sg_ref, h_ref, idx_ref, out_ref, y_ref, t_ref):
    p = lax.axis_index("row")
    nu = x_ref.shape[1] // LO

    def butterfly(ct, carry):
        rows = pl.ds(pl.multiple_of(ct * 8, 8), 8)
        for bt in range(LO // 128):
            v = []
            for u in range(nu):
                at = u * LO + bt * 128
                sign = sg_ref[pl.ds(at // 128, 1), :].astype(F32)
                v.append(x_ref[rows, at : at + 128] * sign)
            step = 1
            while step < nu:
                for u in range(nu):
                    if not u & step:
                        v[u], v[u + step] = v[u] + v[u + step], v[u] - v[u + step]
                step *= 2
            for u in range(nu):
                at = u * LO + bt * 128
                y_ref[rows, at : at + 128] = v[u]
        return carry

    lax.fori_loop(0, x_ref.shape[0] // 8, butterfly, 0)

    h = h_ref[...]
    for g in range(nu // 2):
        parts = []
        for u in (2 * g, 2 * g + 1):
            v = y_ref[:, u * LO : (u + 1) * LO]
            hi = v.astype(BF16)
            rest = v - hi.astype(F32)
            mid = rest.astype(BF16)
            low = (rest - mid.astype(F32)).astype(BF16)
            w = jnp.concatenate([hi, mid, low], axis=1)
            parts += [w, w]
        w = jnp.concatenate(parts, axis=0)
        o = lax.dot_general(h, w, (((1,), (1,)), ((), ())), preferred_element_type=F32)
        t_ref[2 * g * LO : (2 * g + 1) * LO, :] = o[:, :128]
        t_ref[(2 * g + 1) * LO : (2 * g + 2) * LO, :] = o[:, 128:]

    left = lax.broadcasted_iota(jnp.int32, (1, 128), 1) < 64
    mask = t_ref.shape[0] - 1

    def gather(q, carry):
        bits = p & q
        bits = bits ^ (bits >> 4)
        bits = bits ^ (bits >> 2)
        bits = bits ^ (bits >> 1)
        sign = (1 - 2 * (bits & 1)).astype(F32)
        base = ((q & 1) * 64 + (q >> 1)) * 16
        for i in range(16):
            a = t_ref[pl.ds(idx_ref[q * 32 + i] & mask, 1), :]
            b = t_ref[pl.ds(idx_ref[q * 32 + 16 + i] & mask, 1), :]
            out_ref[pl.ds(base + i, 1), :] = jnp.where(left, a, b) * sign
        return carry

    lax.fori_loop(0, 128, gather, 0)


def local_part(panel, signs, rows):
    n = panel.shape[1]
    h = jnp.asarray(np.tile(hadamard(LO) / 1024.0, (1, 3)), BF16)
    vm = pl.BlockSpec(memory_space=pltpu.VMEM)
    return pl.pallas_call(
        local_kernel,
        out_shape=jax.ShapeDtypeStruct((2048, 128), F32),
        in_specs=[vm, vm, vm, pl.BlockSpec(memory_space=pltpu.SMEM)],
        out_specs=vm,
        scratch_shapes=[pltpu.VMEM((64, n), F32), pltpu.VMEM((n, 128), F32)],
        compiler_params=pltpu.CompilerParams(vmem_limit_bytes=40 << 20),
        name="local_mix",
    )(panel, signs.reshape(n // 128, 128), h, rows)


def exchange_kernel(
    z_ref, g_out, m_out, rc, acc, ry, sz, rz, rx, ms, gp, rgc, gz, gy, gf,
    cs, cr, ys, yr, zs, zr, xs, xr, gcs, gcr, gzs, gzr, gys, gyr, gfs, gfr,
):
    row, col = lax.axis_index("row"), lax.axis_index("col")
    c = row % 2
    y = (row // 4) % 4
    z = row // 16
    xl = (row // 2) % 2
    x = col * 2 + xl

    def dev(z_, y_, x_, c_):
        return {"row": z_ * 16 + y_ * 4 + (x_ % 2) * 2 + c_, "col": x_ // 2}

    core_dev = dev(z, y, x, 1 - c)
    y_dev = [dev(z, (y + d) % 4, x, c) for d in range(1, 4)]
    z_dev = [dev((z + d) % 8, y, x, c) for d in range(1, 8)]
    x_dev = [dev(z, y, (x + d) % 4, c) for d in range(1, 4)]
    xo_dev = [dev(z, y, (x + d) % 4, 1 - c) for d in range(1, 4)]
    everyone = [core_dev] + y_dev + z_dev + x_dev + xo_dev

    barrier = pltpu.get_barrier_semaphore()
    for d in everyone:
        pl.semaphore_signal(barrier, inc=1, device_id=d, device_id_type=MESH)
    pl.semaphore_wait(barrier, len(everyone))

    def send(src, dst, ss, rs, device):
        copy = pltpu.make_async_remote_copy(
            src_ref=src, dst_ref=dst, send_sem=ss, recv_sem=rs,
            device_id=device, device_id_type=MESH,
        )
        copy.start()
        return copy

    started = []
    to_core = []
    for k, off in enumerate(ORDER):
        to_core.append(send(z_ref.at[1 - c, (z + off) % 8], rc.at[k], cs.at[k], cr.at[k], core_dev))
    started += to_core
    to_y = {}
    to_z = [None] * 7

    def stage_y(k):
        to_core[k].wait_recv()
        acc[k] = z_ref[c, (z + ORDER[k]) % 8] + rc[k]
        to_y[k] = [
            send(acc.at[k, (y + d) % 4], ry.at[k, d - 1], ys.at[k, d - 1], yr.at[k, d - 1], y_dev[d - 1])
            for d in (2, 1, 3)
        ]

    def stage_z(k):
        for copy in to_y[k]:
            copy.wait_recv()
        sz[k] = (acc[k, y] + ry[k, 0]) + (ry[k, 1] + ry[k, 2])
        off = ORDER[k]
        if off:
            to_z[off - 1] = send(sz.at[k], rz.at[off - 1], zs.at[off - 1], zr.at[off - 1], z_dev[off - 1])

    for k in range(8):
        stage_y(k)
        if k >= 2:
            stage_z(k - 2)
    stage_z(6)
    stage_z(7)
    for k in range(8):
        started += to_y[k]
    started += to_z
    for copy in to_z:
        copy.wait_recv()
    r = [rz[i] for i in range(7)]
    rx[x] = ((sz[7] + r[0]) + (r[1] + r[2])) + ((r[3] + r[4]) + (r[5] + r[6]))

    to_x = [send(rx.at[x], rx.at[x], xs.at[d], xr.at[d], x_dev[d]) for d in (1, 0, 2)]
    started += to_x
    for copy in to_x:
        copy.wait_recv()
    a0 = rx[0] + rx[1]
    a1 = rx[2] + rx[3]
    first = jnp.concatenate([a0[:, :64], a1[:, :64]], axis=1)
    second = jnp.concatenate([a0[:, 64:], a1[:, 64:]], axis=1)
    ms[0, 0], ms[0, 1] = first[:16], first[16:]
    ms[1, 0], ms[1, 1] = second[:16], second[16:]
    m = jnp.concatenate([first, second], axis=0)
    g = lax.dot_general(
        m.T, m, (((1,), (0,)), ((), ())), preferred_element_type=F32, precision=lax.Precision.HIGHEST
    )
    for e in range(8):
        gp[e] = g[e * 16 : (e + 1) * 16]
    to_gc = send(gp.at[x * 2 + 1 - c], rgc, gcs, gcr, core_dev)
    m_out[0:16, :] = ms[0, xl]
    m_out[16:32, :] = ms[1, xl]
    to_gc.wait_recv()
    gz[z] = gp[x * 2 + c] + rgc[...]
    to_gz = [send(gz.at[z], gz.at[z], gzs.at[d - 1], gzr.at[d - 1], z_dev[d - 1]) for d in (4, 3, 5, 2, 6, 1, 7)]
    for copy in to_gz:
        copy.wait_recv()
    gy[y] = ((gz[0] + gz[1]) + (gz[2] + gz[3])) + ((gz[4] + gz[5]) + (gz[6] + gz[7]))
    to_gy = [send(gy.at[y], gy.at[y], gys.at[d - 1], gyr.at[d - 1], y_dev[d - 1]) for d in (2, 1, 3)]
    for copy in to_gy:
        copy.wait_recv()
    mine = x * 2 + c
    gf[mine] = ((gy[0] + gy[1]) + (gy[2] + gy[3])) * (1.0 / 4096.0)
    peers = [x_dev[1], xo_dev[1], x_dev[0], xo_dev[0], x_dev[2], xo_dev[2], core_dev]
    to_gf = [send(gf.at[mine], gf.at[mine], gfs.at[i], gfr.at[i], d) for i, d in enumerate(peers)]
    for copy in to_gf:
        copy.wait_recv()
    for e in range(8):
        g_out[e * 16 : (e + 1) * 16, :] = gf[e]
    started += [to_gc] + to_gz + to_gy + to_gf
    for copy in started:
        copy.wait_send()


def exchange(zs):
    vm = pl.BlockSpec(memory_space=pltpu.VMEM)
    V = pltpu.VMEM
    D = pltpu.SemaphoreType.DMA
    return pl.pallas_call(
        exchange_kernel,
        out_shape=(jax.ShapeDtypeStruct((128, 128), F32), jax.ShapeDtypeStruct((32, 128), F32)),
        in_specs=[vm],
        out_specs=(vm, vm),
        scratch_shapes=[
            V((8, 4, 32, 128), F32),
            V((8, 4, 32, 128), F32),
            V((8, 3, 32, 128), F32),
            V((8, 32, 128), F32),
            V((7, 32, 128), F32),
            V((4, 32, 128), F32),
            V((2, 2, 16, 128), F32),
            V((8, 16, 128), F32),
            V((16, 128), F32),
            V((8, 16, 128), F32),
            V((4, 16, 128), F32),
            V((8, 16, 128), F32),
            D((8,)), D((8,)), D((8, 3)), D((8, 3)), D((7,)), D((7,)), D((3,)), D((3,)),
            D, D, D((7,)), D((7,)), D((3,)), D((3,)), D((7,)), D((7,)),
        ],
        compiler_params=pltpu.CompilerParams(
            collective_id=0, has_side_effects=True, vmem_limit_bytes=24 << 20
        ),
        name="exchange",
    )(zs.reshape(2, 8, 4, 32, 128))


def rows_const(v, j):
    return jnp.broadcast_to(v[:, j : j + 1], (8, 128))


def factor_kernel(g_ref, m_ref, basis_ref, tri_ref, a_ref, u_ref):
    n, width = 128, 32
    col = lax.axis_index("col")
    a_ref[:, :128] = g_ref[...]
    mt = jnp.concatenate([m_ref[...], jnp.zeros((96, 128), F32)], axis=0)
    a_ref[:, 128:] = mt.T
    lane = lax.broadcasted_iota(jnp.int32, (8, 128), 1)
    for panel in range(n // width):
        top = panel * width
        nb = width // 8
        blocks = [
            [a_ref[top + 8 * i : top + 8 * i + 8, 128 * t : 128 * t + 128] for t in range(2)]
            for i in range(nb)
        ]
        for j in range(nb):
            at = top + 8 * j
            rows = [
                [jnp.broadcast_to(blocks[j][t][k : k + 1, :], (8, 128)) for t in range(2)]
                for k in range(8)
            ]
            d = {(i, k): rows_const(rows[i][0], at + k) for i in range(8) for k in range(i + 1)}
            below = [[rows_const(blocks[i][0], at + k) for k in range(8)] for i in range(j + 1, nb)]
            for k in range(8):
                r = lax.rsqrt(d[k, k])
                for i in range(k + 1, 8):
                    d[i, k] = d[i, k] * r
                for i in range(k + 1, 8):
                    for q in range(k + 1, i + 1):
                        d[i, q] = d[i, q] - d[i, k] * d[q, k]
                for t in range(2):
                    rows[k][t] = rows[k][t] * r
                    for q in range(k + 1, 8):
                        rows[q][t] = rows[q][t] - d[q, k] * rows[k][t]
                for b in below:
                    b[k] = b[k] * r
                    for q in range(k + 1, 8):
                        b[q] = b[q] - d[q, k] * b[k]
            for k in range(8):
                keep = lane >= at + k
                u_ref[at + k : at + k + 1, :128] = jnp.where(keep, rows[k][0], 0.0)[:1]
                u_ref[at + k : at + k + 1, 128:] = rows[k][1][:1]
            for i in range(j + 1, nb):
                b = below[i - j - 1]
                for t in range(2):
                    v = blocks[i][t]
                    for k in range(8):
                        v = v - b[k] * rows[k][t]
                    blocks[i][t] = v
        if top + width < n:
            rest = top + width
            u = u_ref[top:rest, :]
            left = u[:, :128].T[rest:, :]
            upd = jnp.dot(left, u, preferred_element_type=F32, precision=lax.Precision.HIGHEST)
            a_ref[rest:, :] = a_ref[rest:, :] - upd
    half = pl.ds(pl.multiple_of(col * 64, 64), 64)
    tri_ref[...] = u_ref[half, :128]
    basis_ref[...] = u_ref[half, 128:][:, :32]


def factor(gram, samples):
    vm = pl.BlockSpec(memory_space=pltpu.VMEM)
    return pl.pallas_call(
        factor_kernel,
        out_shape=(jax.ShapeDtypeStruct((64, 32), F32), jax.ShapeDtypeStruct((64, 128), F32)),
        in_specs=[vm, vm],
        out_specs=(vm, vm),
        scratch_shapes=[pltpu.VMEM((128, 256), F32), pltpu.VMEM((128, 256), F32)],
        compiler_params=pltpu.CompilerParams(vmem_limit_bytes=16 << 20),
        name="factor",
    )(gram, samples)


def shards(tall_panel_array, row_signs, sample_rows):
    picked = local_part(tall_panel_array, row_signs, sample_rows)
    gram, samples = exchange(picked)
    return factor(gram, samples)


def solution(mesh):
    return jax.shard_map(
        shards,
        mesh=mesh,
        in_specs=(P("col", "row"), P("row"), P()),
        out_specs=(P("col", "row"), P("col", None)),
        check_vma=False,
    )
```

```python
import jax
import jax.numpy as jnp
from jax import lax
from jax.experimental import pallas as pl
from jax.experimental.pallas import tpu as pltpu
from jax.sharding import PartitionSpec as P

F32 = jnp.float32
BF16 = jnp.bfloat16
MESH = pl.DeviceIdType.MESH
LO = 256
NU = 32
LOCAL = LO * NU
ORDER = (4, 3, 5, 2, 6, 1, 7, 0)


def parity(bits):
    bits = bits ^ (bits >> 4)
    bits = bits ^ (bits >> 2)
    bits = bits ^ (bits >> 1)
    return bits & 1


def mix_kernel(
    x_hbm, sg_hbm, idx_hbm, g_out, m_out,
    xv, sgv, idx, t, zo, acc, rc, y1p, y1m, y2p, y2m, zp, zm, rx, ms, mt, gs, gr, gz, gf,
    in_sem, cs, cr, ys, yr, zs, zr, xs, xr, gss, gsr, gzs, gzr, gfs, gfr,
):
    row, col = lax.axis_index("row"), lax.axis_index("col")
    c = row % 2
    xl = (row // 2) % 2
    y = (row // 4) % 4
    z = row // 16
    x = col * 2 + xl

    def dev(z_, y_, x_, c_):
        return {"row": z_ * 16 + y_ * 4 + (x_ % 2) * 2 + c_, "col": x_ // 2}

    def near(dy, dx, dc):
        return dev(z, (y + dy) % 4, (x + dx) % 4, c + dc - 2 * c * dc)

    core_dev = near(0, 0, 1)
    z_dev = [dev((z + d) % 8, y, x, c) for d in range(1, 8)]
    plane = [(dy, dx, dc) for dy in (2, 1, 3, 0) for dx in (2, 1, 3, 0) for dc in (0, 1) if dy or dx or dc]

    barrier = pltpu.get_barrier_semaphore()
    for at in plane:
        pl.semaphore_signal(barrier, inc=1, device_id=near(*at), device_id_type=MESH)
    for d in z_dev:
        pl.semaphore_signal(barrier, inc=1, device_id=d, device_id_type=MESH)

    fetch_signs = pltpu.make_async_copy(sg_hbm, sgv, in_sem.at[8])
    fetch_rows = pltpu.make_async_copy(idx_hbm, idx, in_sem.at[9])

    def fetch(i):
        at = pl.ds(i * 8, 8)
        return pltpu.make_async_copy(x_hbm.at[at], xv.at[at], in_sem.at[i])

    fetch_signs.start()
    for i in range(8):
        fetch(i).start()
    fetch_rows.start()
    ri = lax.broadcasted_iota(jnp.int32, (LO, LO), 0)
    ci = lax.broadcasted_iota(jnp.int32, (LO, LO), 1)
    h = ((1 - 2 * parity(ri & ci)).astype(F32) * (1.0 / 1024.0)).astype(BF16)
    h = jnp.concatenate([h, h, h], axis=1)
    fetch_signs.wait()

    def butterfly(i, carry):
        fetch(i).wait()
        rows = pl.ds(pl.multiple_of(i * 8, 8), 8)
        for bt in range(LO // 128):
            v = []
            for u in range(NU):
                at = u * LO + bt * 128
                v.append(xv[rows, at : at + 128] * sgv[at // 128 : at // 128 + 1, :].astype(F32))
            step = 1
            while step < NU:
                for u in range(NU):
                    if not u & step:
                        v[u], v[u + step] = v[u] + v[u + step], v[u] - v[u + step]
                step *= 2
            for u in range(NU):
                at = u * LO + bt * 128
                xv[rows, at : at + 128] = v[u]
        return carry

    lax.fori_loop(0, 8, butterfly, 0)

    for g in range(NU // 4):
        parts = []
        for u in (2 * g, 2 * g + NU // 2, 2 * g + 1, 2 * g + 1 + NU // 2):
            v = xv[:, u * LO : (u + 1) * LO]
            hi = v.astype(BF16)
            rest = v - hi.astype(F32)
            mid = rest.astype(BF16)
            low = (rest - mid.astype(F32)).astype(BF16)
            parts.append(jnp.concatenate([hi, mid, low], axis=1))
        w = jnp.concatenate(parts, axis=0)
        o = lax.dot_general(h, w, (((1,), (1,)), ((), ())), preferred_element_type=F32)
        for i in range(2):
            part = o[:, 128 * i : 128 * i + 128]
            at = (2 * g + i) * LO
            t[at : at + LO, :] = part
            t[LOCAL // 2 + at : LOCAL // 2 + at + LO, :] = pltpu.roll(part, 64, 1)

    fetch_rows.wait()
    pl.semaphore_wait(barrier, len(plane) + 7)

    left = lax.broadcasted_iota(jnp.int32, (1, 128), 1) < 64

    def pick(out, k, zq, cq):
        def body(i, carry):
            q = zq * 16 + i * 2 + cq
            sign = (1 - 2 * parity(row & q)).astype(F32)
            for j in range(16):
                a = t[pl.ds(idx[q * 32 + j] & (LOCAL - 1), 1), :]
                b = t[pl.ds((idx[q * 32 + 16 + j] & (LOCAL - 1)) ^ (LOCAL // 2), 1), :]
                out[k, pl.ds(i * 16 + j, 1), :] = jnp.where(left, a, b) * sign
            return carry

        lax.fori_loop(0, 8, body, 0)

    started = []

    def send(src, dst, ss, rs, device):
        copy = pltpu.make_async_remote_copy(
            src_ref=src, dst_ref=dst, send_sem=ss, recv_sem=rs,
            device_id=device, device_id_type=MESH,
        )
        copy.start()
        started.append(copy)
        return copy

    up, down, opposite = (y + 1) % 4, (y + 3) % 4, (y + 2) % 4
    y_up, y_down = near(1, 0, 0), near(3, 0, 0)
    to_core, to_y1, to_y2, to_z = {}, {}, {}, {}

    def block(i, first, n):
        return pl.ds(pl.multiple_of(i * 32 + first, 8), n)

    def stage_a(k):
        to_core[k].wait_recv()
        acc[k] = acc[k] + rc[k]
        to_y1[k] = [
            send(acc.at[k, block(opposite, 0, 16)], y1p.at[k], ys.at[k, 0], yr.at[k, 0], y_up),
            send(acc.at[k, block(opposite, 16, 16)], y1m.at[k], ys.at[k, 1], yr.at[k, 1], y_down),
        ]

    def stage_b(k):
        for copy in to_y1[k]:
            copy.wait_recv()
        half = block(up, 0, 16)
        acc[k, half] = acc[k, half] + y1p[k]
        half = block(down, 16, 16)
        acc[k, half] = acc[k, half] + y1m[k]
        to_y2[k] = [
            send(acc.at[k, block(up, 0, 32)], y2p.at[k], ys.at[k, 2], yr.at[k, 2], y_up),
            send(acc.at[k, block(down, 0, 32)], y2m.at[k], ys.at[k, 3], yr.at[k, 3], y_down),
        ]

    def stage_c(k):
        for copy in to_y2[k]:
            copy.wait_recv()
        mine = block(y, 0, 32)
        s = acc[k, mine] + (y2p[k] + y2m[k])
        off = ORDER[k]
        if off == 4:
            acc[k, mine] = s
            to_z["p", 0] = send(acc.at[k, block(y, 0, 16)], zp.at[0, 0:16], zs.at[0, 0], zr.at[0, 0], z_dev[0])
            to_z["m", 0] = send(acc.at[k, block(y, 16, 16)], zm.at[0, 16:32], zs.at[1, 0], zr.at[1, 0], z_dev[6])
        elif off:
            way, n, got, line, nxt = ("p", 4 - off, zp, 0, z_dev[0]) if off < 4 else ("m", off - 4, zm, 1, z_dev[6])
            to_z[way, n - 1].wait_recv()
            if n == 1:
                lo = 0 if way == "p" else 16
                acc[k, mine] = s
                half = block(y, lo, 16)
                acc[k, half] = acc[k, half] + got[0, lo : lo + 16]
            else:
                acc[k, mine] = s + got[n - 1]
            to_z[way, n] = send(acc.at[k, mine], got.at[n], zs.at[line, n], zr.at[line, n], nxt)
        else:
            to_z["p", 3].wait_recv()
            to_z["m", 3].wait_recv()
            rx[x] = s + (zp[3] + zm[3])

    for k in range(12):
        if k < 8:
            zq = (z + ORDER[k]) % 8
            pick(zo, k, zq, 1 - c)
            to_core[k] = send(zo.at[k], rc.at[k], cs.at[k], cr.at[k], core_dev)
            pick(acc, k, zq, c)
            if k >= 2:
                stage_a(k - 2)
            if k >= 4:
                stage_b(k - 4)
            if k >= 6:
                stage_c(k - 6)
        elif k < 10:
            stage_a(k - 2)
            stage_b(k - 4)
            stage_c(k - 6)
        else:
            stage_b(k - 4)
            stage_c(k - 6)
    stage_c(6)
    stage_c(7)

    to_x = [send(rx.at[x], rx.at[x], xs.at[d], xr.at[d], near(0, d + 1, 0)) for d in (1, 0, 2)]
    for copy in to_x:
        copy.wait_recv()
    a0 = rx[0] + rx[1]
    a1 = rx[2] + rx[3]
    first = jnp.concatenate([a0[:, :64], a1[:, :64]], axis=1)
    second = jnp.concatenate([a0[:, 64:], a1[:, 64:]], axis=1)
    m = jnp.concatenate([first, second], axis=0)
    mt[...] = m.T
    g = jnp.dot(
        mt[pl.ds(pl.multiple_of(x * 32, 32), 32), :], m,
        preferred_element_type=F32, precision=lax.Precision.HIGHEST,
    )
    for e in range(8):
        gs[e] = g[4 * e : 4 * e + 4]

    part = [(dy, 0, dc) for dy in (2, 1, 3, 0) for dc in (0, 1) if dy or dc]
    to_gs = []
    for i, (dy, dx, dc) in enumerate(part):
        e = ((y + dy) % 4) * 2 + (c + dc - 2 * c * dc)
        to_gs.append(send(gs.at[e], gr.at[i], gss.at[i], gsr.at[i], near(dy, dx, dc)))
    ms[0, 0], ms[0, 1] = first[:16], first[16:]
    ms[1, 0], ms[1, 1] = second[:16], second[16:]
    m_out[0:16, :] = ms[0, xl]
    m_out[16:32, :] = ms[1, xl]
    own = y * 2 + c
    for copy in to_gs:
        copy.wait_recv()
    gz[z] = ((gs[own] + gr[0]) + (gr[1] + gr[2])) + ((gr[3] + gr[4]) + (gr[5] + gr[6]))
    to_gz = [send(gz.at[z], gz.at[z], gzs.at[d - 1], gzr.at[d - 1], z_dev[d - 1]) for d in (4, 3, 5, 2, 6, 1, 7)]
    for copy in to_gz:
        copy.wait_recv()
    e = x * 8 + own
    gf[e] = (((gz[0] + gz[1]) + (gz[2] + gz[3])) + ((gz[4] + gz[5]) + (gz[6] + gz[7]))) * (1.0 / 4096.0)
    to_gf = [send(gf.at[e], gf.at[e], gfs.at[i], gfr.at[i], near(*at)) for i, at in enumerate(plane)]
    for copy in to_gf:
        copy.wait_recv()
    for e in range(32):
        g_out[e * 4 : (e + 1) * 4, :] = gf[e]
    for copy in started:
        copy.wait_send()


def mix(panel, signs, rows):
    vm = pl.BlockSpec(memory_space=pltpu.VMEM)
    hbm = pl.BlockSpec(memory_space=pltpu.HBM)
    V = pltpu.VMEM
    D = pltpu.SemaphoreType.DMA
    return pl.pallas_call(
        mix_kernel,
        out_shape=(jax.ShapeDtypeStruct((128, 128), F32), jax.ShapeDtypeStruct((32, 128), F32)),
        in_specs=[hbm, hbm, hbm],
        out_specs=(vm, vm),
        scratch_shapes=[
            V((64, LOCAL), F32),
            V((LOCAL // 128, 128), jnp.int32),
            pltpu.SMEM((4096,), jnp.int32),
            V((LOCAL, 128), F32),
            V((8, 128, 128), F32),
            V((8, 128, 128), F32),
            V((8, 128, 128), F32),
            V((8, 16, 128), F32),
            V((8, 16, 128), F32),
            V((8, 32, 128), F32),
            V((8, 32, 128), F32),
            V((4, 32, 128), F32),
            V((4, 32, 128), F32),
            V((4, 32, 128), F32),
            V((2, 2, 16, 128), F32),
            V((128, 64), F32),
            V((8, 4, 128), F32),
            V((7, 4, 128), F32),
            V((8, 4, 128), F32),
            V((32, 4, 128), F32),
            D((10,)),
            D((8,)), D((8,)), D((8, 4)), D((8, 4)), D((2, 4)), D((2, 4)), D((3,)), D((3,)),
            D((7,)), D((7,)), D((7,)), D((7,)), D((31,)), D((31,)),
        ],
        compiler_params=pltpu.CompilerParams(
            collective_id=0, has_side_effects=True, vmem_limit_bytes=40 << 20
        ),
        name="mix",
    )(panel, signs.reshape(LOCAL // 128, 128), rows)


def rows_const(v, j):
    return jnp.broadcast_to(v[:, j : j + 1], (8, 128))


def factor_kernel(g_ref, m_ref, basis_ref, tri_ref, a_ref, u_ref):
    n, width = 128, 32
    col = lax.axis_index("col")
    a_ref[:, :128] = g_ref[...]
    mt = jnp.concatenate([m_ref[...], jnp.zeros((96, 128), F32)], axis=0)
    a_ref[:, 128:] = mt.T
    lane = lax.broadcasted_iota(jnp.int32, (8, 128), 1)
    for panel in range(n // width):
        top = panel * width
        nb = width // 8
        blocks = [
            [a_ref[top + 8 * i : top + 8 * i + 8, 128 * t : 128 * t + 128] for t in range(2)]
            for i in range(nb)
        ]
        for j in range(nb):
            at = top + 8 * j
            rows = [
                [jnp.broadcast_to(blocks[j][t][k : k + 1, :], (8, 128)) for t in range(2)]
                for k in range(8)
            ]
            d = {(i, k): rows_const(rows[i][0], at + k) for i in range(8) for k in range(i + 1)}
            below = [[rows_const(blocks[i][0], at + k) for k in range(8)] for i in range(j + 1, nb)]
            for k in range(8):
                r = lax.rsqrt(d[k, k])
                for i in range(k + 1, 8):
                    d[i, k] = d[i, k] * r
                for i in range(k + 1, 8):
                    for q in range(k + 1, i + 1):
                        d[i, q] = d[i, q] - d[i, k] * d[q, k]
                for t in range(2):
                    rows[k][t] = rows[k][t] * r
                    for q in range(k + 1, 8):
                        rows[q][t] = rows[q][t] - d[q, k] * rows[k][t]
                for b in below:
                    b[k] = b[k] * r
                    for q in range(k + 1, 8):
                        b[q] = b[q] - d[q, k] * b[k]
            for k in range(8):
                keep = lane >= at + k
                u_ref[at + k : at + k + 1, :128] = jnp.where(keep, rows[k][0], 0.0)[:1]
                u_ref[at + k : at + k + 1, 128:] = rows[k][1][:1]
            for i in range(j + 1, nb):
                b = below[i - j - 1]
                for t in range(2):
                    v = blocks[i][t]
                    for k in range(8):
                        v = v - b[k] * rows[k][t]
                    blocks[i][t] = v
        if top + width < n:
            rest = top + width
            u = u_ref[top:rest, :]
            left = u[:, :128].T[rest:, :]
            upd = jnp.dot(left, u, preferred_element_type=F32, precision=lax.Precision.HIGHEST)
            a_ref[rest:, :] = a_ref[rest:, :] - upd
    half = pl.ds(pl.multiple_of(col * 64, 64), 64)
    tri_ref[...] = u_ref[half, :128]
    basis_ref[...] = u_ref[half, 128:].T[:32]


def factor(gram, samples):
    vm = pl.BlockSpec(memory_space=pltpu.VMEM)
    return pl.pallas_call(
        factor_kernel,
        out_shape=(jax.ShapeDtypeStruct((32, 64), F32), jax.ShapeDtypeStruct((64, 128), F32)),
        in_specs=[vm, vm],
        out_specs=(vm, vm),
        scratch_shapes=[pltpu.VMEM((128, 256), F32), pltpu.VMEM((128, 256), F32)],
        compiler_params=pltpu.CompilerParams(vmem_limit_bytes=16 << 20),
        name="factor",
    )(gram, samples)


def shards(tall_panel_array, row_signs, sample_rows):
    gram, samples = mix(tall_panel_array, row_signs, sample_rows)
    basis, upper = factor(gram, samples)
    return basis.T, upper


def solution(mesh):
    return jax.shard_map(
        shards,
        mesh=mesh,
        in_specs=(P("col", "row"), P("row"), P()),
        out_specs=(P("col", "row"), P("col", None)),
        check_vma=False,
    )
```

```python
import jax
import jax.numpy as jnp
from jax import lax
from jax.experimental import pallas as pl
from jax.experimental.pallas import tpu as pltpu
from jax.sharding import PartitionSpec as P

F32 = jnp.float32
BF16 = jnp.bfloat16
MESH = pl.DeviceIdType.MESH
LO = 256
NU = 32
LOCAL = LO * NU
ORDER = (4, 3, 5, 2, 6, 1, 7, 0)


def rows_const(v, j):
    return jnp.broadcast_to(v[:, j : j + 1], (8, 128))


def factor(a_ref, u_ref):
    n, width = 128, 32
    lane = lax.broadcasted_iota(jnp.int32, (8, 128), 1)
    for panel in range(n // width):
        top = panel * width
        nb = width // 8
        blocks = [
            [a_ref[top + 8 * i : top + 8 * i + 8, 128 * t : 128 * t + 128] for t in range(2)]
            for i in range(nb)
        ]
        for j in range(nb):
            at = top + 8 * j
            rows = [
                [jnp.broadcast_to(blocks[j][t][k : k + 1, :], (8, 128)) for t in range(2)]
                for k in range(8)
            ]
            d = {(i, k): rows_const(rows[i][0], at + k) for i in range(8) for k in range(i + 1)}
            below = [[rows_const(blocks[i][0], at + k) for k in range(8)] for i in range(j + 1, nb)]
            for k in range(8):
                r = lax.rsqrt(d[k, k])
                for i in range(k + 1, 8):
                    d[i, k] = d[i, k] * r
                for i in range(k + 1, 8):
                    for q in range(k + 1, i + 1):
                        d[i, q] = d[i, q] - d[i, k] * d[q, k]
                for t in range(2):
                    rows[k][t] = rows[k][t] * r
                    for q in range(k + 1, 8):
                        rows[q][t] = rows[q][t] - d[q, k] * rows[k][t]
                for b in below:
                    b[k] = b[k] * r
                    for q in range(k + 1, 8):
                        b[q] = b[q] - d[q, k] * b[k]
            for k in range(8):
                keep = lane >= at + k
                u_ref[at + k : at + k + 1, :128] = jnp.where(keep, rows[k][0], 0.0)[:1]
                u_ref[at + k : at + k + 1, 128:] = rows[k][1][:1]
            for i in range(j + 1, nb):
                b = below[i - j - 1]
                for t in range(2):
                    v = blocks[i][t]
                    for k in range(8):
                        v = v - b[k] * rows[k][t]
                    blocks[i][t] = v
        if top + width < n:
            rest = top + width
            u = u_ref[top:rest, :]
            left = u[:, :128].T[rest:, :]
            upd = jnp.dot(left, u, preferred_element_type=F32, precision=lax.Precision.HIGHEST)
            a_ref[rest:, :] = a_ref[rest:, :] - upd


def parity(bits):
    bits = bits ^ (bits >> 4)
    bits = bits ^ (bits >> 2)
    bits = bits ^ (bits >> 1)
    return bits & 1


def mix_kernel(
    x_hbm, sg_hbm, idx_hbm, basis_out, tri_out,
    xv, sgv, idx, t, zo, acc, rc, ry, rz, rx, ms, mt, gs, gr, gz, gf, aug, fac,
    in_sem, cs, cr, ys, yr, zs, zr, xs, xr, gss, gsr, gzs, gzr, gfs, gfr,
):
    row, col = lax.axis_index("row"), lax.axis_index("col")
    c = row % 2
    xl = (row // 2) % 2
    y = (row // 4) % 4
    z = row // 16
    x = col * 2 + xl

    def dev(z_, y_, x_, c_):
        return {"row": z_ * 16 + y_ * 4 + (x_ % 2) * 2 + c_, "col": x_ // 2}

    def near(dy, dx, dc):
        return dev(z, (y + dy) % 4, (x + dx) % 4, c + dc - 2 * c * dc)

    core_dev = near(0, 0, 1)
    z_dev = [dev((z + d) % 8, y, x, c) for d in range(1, 8)]
    plane = [(dy, dx, dc) for dy in (2, 1, 3, 0) for dx in (2, 1, 3, 0) for dc in (0, 1) if dy or dx or dc]

    barrier = pltpu.get_barrier_semaphore()
    for at in plane:
        pl.semaphore_signal(barrier, inc=1, device_id=near(*at), device_id_type=MESH)
    for d in z_dev:
        pl.semaphore_signal(barrier, inc=1, device_id=d, device_id_type=MESH)

    fetch_signs = pltpu.make_async_copy(sg_hbm, sgv, in_sem.at[8])
    fetch_rows = pltpu.make_async_copy(idx_hbm, idx, in_sem.at[9])

    def fetch(i):
        at = pl.ds(i * 8, 8)
        return pltpu.make_async_copy(x_hbm.at[at], xv.at[at], in_sem.at[i])

    fetch_signs.start()
    for i in range(8):
        fetch(i).start()
    fetch_rows.start()
    ri = lax.broadcasted_iota(jnp.int32, (LO, LO), 0)
    ci = lax.broadcasted_iota(jnp.int32, (LO, LO), 1)
    h = ((1 - 2 * parity(ri & ci)).astype(F32) * (1.0 / 1024.0)).astype(BF16)
    h = jnp.concatenate([h, h, h], axis=1)
    fetch_signs.wait()

    def butterfly(i, carry):
        fetch(i).wait()
        rows = pl.ds(pl.multiple_of(i * 8, 8), 8)
        for bt in range(LO // 128):
            v = []
            for u in range(NU):
                at = u * LO + bt * 128
                v.append(xv[rows, at : at + 128] * sgv[at // 128 : at // 128 + 1, :].astype(F32))
            step = 1
            while step < NU:
                for u in range(NU):
                    if not u & step:
                        v[u], v[u + step] = v[u] + v[u + step], v[u] - v[u + step]
                step *= 2
            for u in range(NU):
                at = u * LO + bt * 128
                xv[rows, at : at + 128] = v[u]
        return carry

    lax.fori_loop(0, 8, butterfly, 0)

    for g in range(NU // 4):
        parts = []
        for u in (2 * g, 2 * g + NU // 2, 2 * g + 1, 2 * g + 1 + NU // 2):
            v = xv[:, u * LO : (u + 1) * LO]
            hi = v.astype(BF16)
            rest = v - hi.astype(F32)
            mid = rest.astype(BF16)
            low = (rest - mid.astype(F32)).astype(BF16)
            parts.append(jnp.concatenate([hi, mid, low], axis=1))
        w = jnp.concatenate(parts, axis=0)
        o = lax.dot_general(h, w, (((1,), (1,)), ((), ())), preferred_element_type=F32)
        for i in range(2):
            part = o[:, 128 * i : 128 * i + 128]
            at = (2 * g + i) * LO
            t[at : at + LO, :] = part
            t[LOCAL // 2 + at : LOCAL // 2 + at + LO, :] = pltpu.roll(part, 64, 1)

    fetch_rows.wait()
    pl.semaphore_wait(barrier, len(plane) + 7)

    left = lax.broadcasted_iota(jnp.int32, (1, 128), 1) < 64

    def pick(out, k, zq, cq):
        def body(i, carry):
            q = zq * 16 + i * 2 + cq
            sign = (1 - 2 * parity(row & q)).astype(F32)
            for j in range(16):
                a = t[pl.ds(idx[q * 32 + j] & (LOCAL - 1), 1), :]
                b = t[pl.ds((idx[q * 32 + 16 + j] & (LOCAL - 1)) ^ (LOCAL // 2), 1), :]
                out[k, pl.ds(i * 16 + j, 1), :] = jnp.where(left, a, b) * sign
            return carry

        lax.fori_loop(0, 8, body, 0)

    started = []

    def send(src, dst, ss, rs, device):
        copy = pltpu.make_async_remote_copy(
            src_ref=src, dst_ref=dst, send_sem=ss, recv_sem=rs,
            device_id=device, device_id_type=MESH,
        )
        copy.start()
        started.append(copy)
        return copy

    y_dev = [near(d, 0, 0) for d in range(1, 4)]
    to_core, to_y, to_z = {}, {}, {}

    def block(i):
        return pl.ds(pl.multiple_of(i * 32, 32), 32)

    def stage_y(k):
        to_core[k].wait_recv()
        acc[k] = acc[k] + rc[k]
        to_y[k] = [
            send(acc.at[k, block((y + d) % 4)], ry.at[k, d - 1], ys.at[k, d - 1], yr.at[k, d - 1], y_dev[d - 1])
            for d in (2, 1, 3)
        ]

    def stage_z(k):
        for copy in to_y[k]:
            copy.wait_recv()
        mine = block(y)
        acc[k, mine] = (acc[k, mine] + ry[k, 0]) + (ry[k, 1] + ry[k, 2])
        off = ORDER[k]
        if off:
            to_z[off] = send(acc.at[k, mine], rz.at[off - 1], zs.at[off - 1], zr.at[off - 1], z_dev[off - 1])

    for k in range(8):
        pick(zo, k, (z + ORDER[k]) % 8, 1 - c)
        to_core[k] = send(zo.at[k], rc.at[k], cs.at[k], cr.at[k], core_dev)
    for k in range(8):
        pick(acc, k, (z + ORDER[k]) % 8, c)
        stage_y(k)
    for k in range(8):
        stage_z(k)
    for off in range(1, 8):
        to_z[off].wait_recv()
    r = [rz[i] for i in range(7)]
    rx[x] = ((acc[7, block(y)] + r[0]) + (r[1] + r[2])) + ((r[3] + r[4]) + (r[5] + r[6]))

    to_x = [send(rx.at[x], rx.at[x], xs.at[d], xr.at[d], near(0, d + 1, 0)) for d in (1, 0, 2)]
    for copy in to_x:
        copy.wait_recv()
    a0 = rx[0] + rx[1]
    a1 = rx[2] + rx[3]
    first = jnp.concatenate([a0[:, :64], a1[:, :64]], axis=1)
    second = jnp.concatenate([a0[:, 64:], a1[:, 64:]], axis=1)
    m = jnp.concatenate([first, second], axis=0)
    mt[...] = m.T
    g = jnp.dot(
        mt[pl.ds(pl.multiple_of(x * 32, 32), 32), :], m,
        preferred_element_type=F32, precision=lax.Precision.HIGHEST,
    )
    for e in range(8):
        gs[e] = g[4 * e : 4 * e + 4]

    part = [(dy, 0, dc) for dy in (2, 1, 3, 0) for dc in (0, 1) if dy or dc]
    to_gs = []
    for i, (dy, dx, dc) in enumerate(part):
        e = ((y + dy) % 4) * 2 + (c + dc - 2 * c * dc)
        to_gs.append(send(gs.at[e], gr.at[i], gss.at[i], gsr.at[i], near(dy, dx, dc)))
    ms[0, 0], ms[0, 1] = first[:16], first[16:]
    ms[1, 0], ms[1, 1] = second[:16], second[16:]
    own = jnp.concatenate([ms[0, xl], ms[1, xl], jnp.zeros((96, 128), F32)], axis=0)
    aug[:, 128:] = own.T
    own = y * 2 + c
    for copy in to_gs:
        copy.wait_recv()
    gz[z] = ((gs[own] + gr[0]) + (gr[1] + gr[2])) + ((gr[3] + gr[4]) + (gr[5] + gr[6]))
    to_gz = [send(gz.at[z], gz.at[z], gzs.at[d - 1], gzr.at[d - 1], z_dev[d - 1]) for d in (4, 3, 5, 2, 6, 1, 7)]
    for copy in to_gz:
        copy.wait_recv()
    e = x * 8 + own
    gf[e] = (((gz[0] + gz[1]) + (gz[2] + gz[3])) + ((gz[4] + gz[5]) + (gz[6] + gz[7]))) * (1.0 / 4096.0)
    to_gf = [send(gf.at[e], gf.at[e], gfs.at[i], gfr.at[i], near(*at)) for i, at in enumerate(plane)]
    for copy in to_gf:
        copy.wait_recv()
    for e in range(32):
        aug[e * 4 : (e + 1) * 4, :128] = gf[e]
    factor(aug, fac)
    half = pl.ds(pl.multiple_of(col * 64, 64), 64)
    tri_out[...] = fac[half, :128]
    basis_out[...] = fac[half, 128:].T[:32]
    for copy in started:
        copy.wait_send()


def mix(panel, signs, rows):
    vm = pl.BlockSpec(memory_space=pltpu.VMEM)
    hbm = pl.BlockSpec(memory_space=pltpu.HBM)
    V = pltpu.VMEM
    D = pltpu.SemaphoreType.DMA
    return pl.pallas_call(
        mix_kernel,
        out_shape=(jax.ShapeDtypeStruct((32, 64), F32), jax.ShapeDtypeStruct((64, 128), F32)),
        in_specs=[hbm, hbm, hbm],
        out_specs=(vm, vm),
        scratch_shapes=[
            V((64, LOCAL), F32),
            V((LOCAL // 128, 128), jnp.int32),
            pltpu.SMEM((4096,), jnp.int32),
            V((LOCAL, 128), F32),
            V((8, 128, 128), F32),
            V((8, 128, 128), F32),
            V((8, 128, 128), F32),
            V((8, 3, 32, 128), F32),
            V((7, 32, 128), F32),
            V((4, 32, 128), F32),
            V((2, 2, 16, 128), F32),
            V((128, 64), F32),
            V((8, 4, 128), F32),
            V((7, 4, 128), F32),
            V((8, 4, 128), F32),
            V((32, 4, 128), F32),
            V((128, 256), F32),
            V((128, 256), F32),
            D((10,)),
            D((8,)), D((8,)), D((8, 3)), D((8, 3)), D((7,)), D((7,)), D((3,)), D((3,)),
            D((7,)), D((7,)), D((7,)), D((7,)), D((31,)), D((31,)),
        ],
        compiler_params=pltpu.CompilerParams(
            collective_id=0, has_side_effects=True, vmem_limit_bytes=62 << 20
        ),
        name="mix",
    )(panel, signs.reshape(LOCAL // 128, 128), rows)


def shards(tall_panel_array, row_signs, sample_rows):
    basis, upper = mix(tall_panel_array, row_signs, sample_rows)
    return basis.T, upper


def solution(mesh):
    return jax.shard_map(
        shards,
        mesh=mesh,
        in_specs=(P("col", "row"), P("row"), P()),
        out_specs=(P("col", "row"), P("col", None)),
        check_vma=False,
    )
```

```python
import jax
import jax.numpy as jnp
from jax import lax
from jax.experimental import pallas as pl
from jax.experimental.pallas import tpu as pltpu
from jax.sharding import PartitionSpec as P

F32 = jnp.float32
BF16 = jnp.bfloat16
MESH = pl.DeviceIdType.MESH
LO = 256
NU = 32
LOCAL = LO * NU
ORDER = (4, 3, 5, 2, 6, 1, 7, 0)


def parity(bits):
    bits = bits ^ (bits >> 4)
    bits = bits ^ (bits >> 2)
    bits = bits ^ (bits >> 1)
    return bits & 1


def mix_kernel(
    x_hbm, sg_hbm, idx_hbm, both_out,
    xv, sgv, idxv, idx, t, zo, acc, rc, ry, rz, rx, ms, mt, gs, gr, gz, gf,
    in_sem, cs, cr, ys, yr, zs, zr, xs, xr, gss, gsr, gzs, gzr, gfs, gfr,
):
    row, col = lax.axis_index("row"), lax.axis_index("col")
    c = row % 2
    xl = (row // 2) % 2
    y = (row // 4) % 4
    z = row // 16
    x = col * 2 + xl

    def dev(z_, y_, x_, c_):
        return {"row": z_ * 16 + y_ * 4 + (x_ % 2) * 2 + c_, "col": x_ // 2}

    def near(dy, dx, dc):
        return dev(z, (y + dy) % 4, (x + dx) % 4, c + dc - 2 * c * dc)

    core_dev = near(0, 0, 1)
    z_dev = [dev((z + d) % 8, y, x, c) for d in range(1, 8)]
    plane = [(dy, dx, dc) for dy in (2, 1, 3, 0) for dx in (2, 1, 3, 0) for dc in (0, 1) if dy or dx or dc]

    fetch_signs = pltpu.make_async_copy(sg_hbm, sgv, in_sem.at[8])
    fetch_rows = pltpu.make_async_copy(idx_hbm, idxv, in_sem.at[9])
    place_rows = pltpu.make_async_copy(idxv, idx, in_sem.at[10])

    def fetch(i):
        at = pl.ds(i * 8, 8)
        return pltpu.make_async_copy(x_hbm.at[at], xv.at[at], in_sem.at[i])

    fetch_rows.start()
    fetch_signs.start()
    for i in range(8):
        fetch(i).start()
    barrier = pltpu.get_barrier_semaphore()
    for at in plane:
        pl.semaphore_signal(barrier, inc=1, device_id=near(*at), device_id_type=MESH)
    for d in z_dev:
        pl.semaphore_signal(barrier, inc=1, device_id=d, device_id_type=MESH)

    ri = lax.broadcasted_iota(jnp.int32, (LO, LO), 0)
    ci = lax.broadcasted_iota(jnp.int32, (LO, LO), 1)
    h = ((1 - 2 * parity(ri & ci)).astype(F32) * (1.0 / 1024.0)).astype(BF16)
    h = jnp.concatenate([h, h, h], axis=1)
    fetch_rows.wait()
    lane = lax.broadcasted_iota(jnp.int32, (32, 128), 1)
    idxv[...] = (idxv[...] & (LOCAL - 1)) ^ ((lane // 16 % 2) * (LOCAL // 2))
    place_rows.start()
    fetch_signs.wait()

    def butterfly(i, carry):
        fetch(i).wait()
        rows = pl.ds(pl.multiple_of(i * 8, 8), 8)
        for bt in range(LO // 128):
            v = []
            for u in range(NU):
                at = u * LO + bt * 128
                v.append(xv[rows, at : at + 128] * sgv[at // 128 : at // 128 + 1, :].astype(F32))
            step = 1
            while step < NU:
                for u in range(NU):
                    if not u & step:
                        v[u], v[u + step] = v[u] + v[u + step], v[u] - v[u + step]
                step *= 2
            for u in range(NU):
                at = u * LO + bt * 128
                xv[rows, at : at + 128] = v[u]
        return carry

    lax.fori_loop(0, 8, butterfly, 0)

    for g in range(NU // 4):
        parts = []
        for u in (2 * g, 2 * g + NU // 2, 2 * g + 1, 2 * g + 1 + NU // 2):
            v = xv[:, u * LO : (u + 1) * LO]
            hi = v.astype(BF16)
            rest = v - hi.astype(F32)
            mid = rest.astype(BF16)
            low = (rest - mid.astype(F32)).astype(BF16)
            parts.append(jnp.concatenate([hi, mid, low], axis=1))
        w = jnp.concatenate(parts, axis=0)
        o = lax.dot_general(h, w, (((1,), (1,)), ((), ())), preferred_element_type=F32)
        for i in range(2):
            part = o[:, 128 * i : 128 * i + 128]
            at = (2 * g + i) * LO
            t[at : at + LO, :] = part
            t[LOCAL // 2 + at : LOCAL // 2 + at + LO, :] = pltpu.roll(part, 64, 1)

    place_rows.wait()
    pl.semaphore_wait(barrier, len(plane) + 7)

    left = lax.broadcasted_iota(jnp.int32, (1, 128), 1) < 64

    def pick(out, k, zq, cq):
        def body(i, carry):
            q = zq * 16 + i * 2 + cq
            sign = (1 - 2 * parity(row & q)).astype(F32)
            first = (q % 4) * 32
            for j in range(16):
                a = t[pl.ds(idx[q // 4, first + j], 1), :]
                b = t[pl.ds(idx[q // 4, first + 16 + j], 1), :]
                out[k, pl.ds(i * 16 + j, 1), :] = jnp.where(left, a, b) * sign
            return carry

        lax.fori_loop(0, 8, body, 0)

    started = []

    def send(src, dst, ss, rs, device):
        copy = pltpu.make_async_remote_copy(
            src_ref=src, dst_ref=dst, send_sem=ss, recv_sem=rs,
            device_id=device, device_id_type=MESH,
        )
        copy.start()
        started.append(copy)
        return copy

    y_dev = [near(d, 0, 0) for d in range(1, 4)]
    to_core, to_y, to_z = {}, {}, {}

    def block(i):
        return pl.ds(pl.multiple_of(i * 32, 32), 32)

    def stage_y(k):
        to_core[k].wait_recv()
        acc[k] = acc[k] + rc[k]
        to_y[k] = [
            send(acc.at[k, block((y + d) % 4)], ry.at[k, d - 1], ys.at[k, d - 1], yr.at[k, d - 1], y_dev[d - 1])
            for d in (2, 1, 3)
        ]

    def stage_z(k):
        for copy in to_y[k]:
            copy.wait_recv()
        mine = block(y)
        acc[k, mine] = (acc[k, mine] + ry[k, 0]) + (ry[k, 1] + ry[k, 2])
        off = ORDER[k]
        if off:
            to_z[off] = send(acc.at[k, mine], rz.at[off - 1], zs.at[off - 1], zr.at[off - 1], z_dev[off - 1])

    for k in range(8):
        pick(zo, k, (z + ORDER[k]) % 8, 1 - c)
        to_core[k] = send(zo.at[k], rc.at[k], cs.at[k], cr.at[k], core_dev)
    for k in range(8):
        pick(acc, k, (z + ORDER[k]) % 8, c)
        stage_y(k)
    for k in range(8):
        stage_z(k)
    for off in range(1, 8):
        to_z[off].wait_recv()
    r = [rz[i] for i in range(7)]
    rx[x] = ((acc[7, block(y)] + r[0]) + (r[1] + r[2])) + ((r[3] + r[4]) + (r[5] + r[6]))

    to_x = [send(rx.at[x], rx.at[x], xs.at[d], xr.at[d], near(0, d + 1, 0)) for d in (1, 0, 2)]
    for copy in started[:-3]:
        copy.wait_send()
    del started[:-3]
    for copy in to_x:
        copy.wait_recv()
    a0 = rx[0] + rx[1]
    a1 = rx[2] + rx[3]
    first = jnp.concatenate([a0[:, :64], a1[:, :64]], axis=1)
    second = jnp.concatenate([a0[:, 64:], a1[:, 64:]], axis=1)
    m = jnp.concatenate([first, second], axis=0)
    mt[...] = m.T
    g = jnp.dot(
        mt[pl.ds(pl.multiple_of(x * 32, 32), 32), :], m,
        preferred_element_type=F32, precision=lax.Precision.HIGHEST,
    )
    for e in range(8):
        gs[e] = g[4 * e : 4 * e + 4]

    part = [(dy, 0, dc) for dy in (2, 1, 3, 0) for dc in (0, 1) if dy or dc]
    to_gs = []
    for i, (dy, dx, dc) in enumerate(part):
        e = ((y + dy) % 4) * 2 + (c + dc - 2 * c * dc)
        to_gs.append(send(gs.at[e], gr.at[i], gss.at[i], gsr.at[i], near(dy, dx, dc)))
    ms[0, 0], ms[0, 1] = first[:16], first[16:]
    ms[1, 0], ms[1, 1] = second[:16], second[16:]
    both_out[128:144, :] = ms[0, xl]
    both_out[144:160, :] = ms[1, xl]
    own = y * 2 + c
    for copy in to_gs:
        copy.wait_recv()
    gz[z] = ((gs[own] + gr[0]) + (gr[1] + gr[2])) + ((gr[3] + gr[4]) + (gr[5] + gr[6]))
    to_gz = [send(gz.at[z], gz.at[z], gzs.at[d - 1], gzr.at[d - 1], z_dev[d - 1]) for d in (4, 3, 5, 2, 6, 1, 7)]
    for copy in to_gz:
        copy.wait_recv()
    e = x * 8 + own
    gf[e] = (((gz[0] + gz[1]) + (gz[2] + gz[3])) + ((gz[4] + gz[5]) + (gz[6] + gz[7]))) * (1.0 / 4096.0)
    to_gf = [send(gf.at[e], gf.at[e], gfs.at[i], gfr.at[i], near(*at)) for i, at in enumerate(plane)]
    for copy in to_gf:
        copy.wait_recv()
    for e in range(32):
        both_out[e * 4 : (e + 1) * 4, :] = gf[e]
    for copy in started:
        copy.wait_send()


def mix(panel, signs, rows):
    vm = pl.BlockSpec(memory_space=pltpu.VMEM)
    hbm = pl.BlockSpec(memory_space=pltpu.HBM)
    V = pltpu.VMEM
    D = pltpu.SemaphoreType.DMA
    return pl.pallas_call(
        mix_kernel,
        out_shape=jax.ShapeDtypeStruct((160, 128), F32),
        in_specs=[hbm, hbm, hbm],
        out_specs=vm,
        scratch_shapes=[
            V((64, LOCAL), F32),
            V((LOCAL // 128, 128), jnp.int32),
            V((32, 128), jnp.int32),
            pltpu.SMEM((32, 128), jnp.int32),
            V((LOCAL, 128), F32),
            V((8, 128, 128), F32),
            V((8, 128, 128), F32),
            V((8, 128, 128), F32),
            V((8, 3, 32, 128), F32),
            V((7, 32, 128), F32),
            V((4, 32, 128), F32),
            V((2, 2, 16, 128), F32),
            V((128, 64), F32),
            V((8, 4, 128), F32),
            V((7, 4, 128), F32),
            V((8, 4, 128), F32),
            V((32, 4, 128), F32),
            D((11,)),
            D((8,)), D((8,)), D((8, 3)), D((8, 3)), D((7,)), D((7,)), D((3,)), D((3,)),
            D((7,)), D((7,)), D((7,)), D((7,)), D((31,)), D((31,)),
        ],
        compiler_params=pltpu.CompilerParams(
            collective_id=0, has_side_effects=True, vmem_limit_bytes=62 << 20
        ),
        name="mix",
    )(panel, signs.reshape(LOCAL // 128, 128), rows.reshape(32, 128))


def rows_const(v, j):
    return jnp.broadcast_to(v[:, j : j + 1], (8, 128))


def factor_kernel(both_ref, basis_ref, tri_ref, a_ref, u_ref):
    n, width = 128, 32
    col = lax.axis_index("col")
    a_ref[:, :128] = both_ref[:128, :]
    samples = jnp.concatenate([both_ref[128:, :], jnp.zeros((96, 128), F32)], axis=0)
    a_ref[:, 128:] = samples.T
    lane = lax.broadcasted_iota(jnp.int32, (8, 128), 1)
    for panel in range(n // width):
        top = panel * width
        nb = width // 8
        blocks = [
            [a_ref[top + 8 * i : top + 8 * i + 8, 128 * t : 128 * t + 128] for t in range(2)]
            for i in range(nb)
        ]
        for j in range(nb):
            at = top + 8 * j
            rows = [
                [jnp.broadcast_to(blocks[j][t][k : k + 1, :], (8, 128)) for t in range(2)]
                for k in range(8)
            ]
            d = {(i, k): rows_const(rows[i][0], at + k) for i in range(8) for k in range(i + 1)}
            below = [[rows_const(blocks[i][0], at + k) for k in range(8)] for i in range(j + 1, nb)]
            for k in range(8):
                r = lax.rsqrt(d[k, k])
                for i in range(k + 1, 8):
                    d[i, k] = d[i, k] * r
                for i in range(k + 1, 8):
                    for q in range(k + 1, i + 1):
                        d[i, q] = d[i, q] - d[i, k] * d[q, k]
                for t in range(2):
                    rows[k][t] = rows[k][t] * r
                    for q in range(k + 1, 8):
                        rows[q][t] = rows[q][t] - d[q, k] * rows[k][t]
                for b in below:
                    b[k] = b[k] * r
                    for q in range(k + 1, 8):
                        b[q] = b[q] - d[q, k] * b[k]
            for k in range(8):
                keep = lane >= at + k
                u_ref[at + k : at + k + 1, :128] = jnp.where(keep, rows[k][0], 0.0)[:1]
                u_ref[at + k : at + k + 1, 128:] = rows[k][1][:1]
            for i in range(j + 1, nb):
                b = below[i - j - 1]
                for t in range(2):
                    v = blocks[i][t]
                    for k in range(8):
                        v = v - b[k] * rows[k][t]
                    blocks[i][t] = v
        if top + width < n:
            rest = top + width
            u = u_ref[top:rest, :]
            left = u[:, :128].T[rest:, :]
            upd = jnp.dot(left, u, preferred_element_type=F32, precision=lax.Precision.HIGHEST)
            a_ref[rest:, :] = a_ref[rest:, :] - upd
    half = pl.ds(pl.multiple_of(col * 64, 64), 64)
    tri_ref[...] = u_ref[half, :128]
    basis_ref[...] = u_ref[half, 128:].T[:32]


def factor(both):
    vm = pl.BlockSpec(memory_space=pltpu.VMEM)
    return pl.pallas_call(
        factor_kernel,
        out_shape=(jax.ShapeDtypeStruct((32, 64), F32), jax.ShapeDtypeStruct((64, 128), F32)),
        in_specs=[vm],
        out_specs=(vm, vm),
        scratch_shapes=[pltpu.VMEM((128, 256), F32), pltpu.VMEM((128, 256), F32)],
        compiler_params=pltpu.CompilerParams(vmem_limit_bytes=16 << 20),
        name="factor",
    )(both)


def shards(tall_panel_array, row_signs, sample_rows):
    basis, upper = factor(mix(tall_panel_array, row_signs, sample_rows))
    return basis.T, upper


def solution(mesh):
    return jax.shard_map(
        shards,
        mesh=mesh,
        in_specs=(P("col", "row"), P("row"), P()),
        out_specs=(P("col", "row"), P("col", None)),
        check_vma=False,
    )
```

```python
import jax
import jax.numpy as jnp
from jax import lax
from jax.experimental import pallas as pl
from jax.experimental.pallas import tpu as pltpu
from jax.sharding import PartitionSpec as P

F32 = jnp.float32
BF16 = jnp.bfloat16
MESH = pl.DeviceIdType.MESH
LO = 256
NU = 32
LOCAL = LO * NU
HALF = LOCAL // 2


def parity(bits):
    bits = bits ^ (bits >> 4)
    bits = bits ^ (bits >> 2)
    bits = bits ^ (bits >> 1)
    return bits & 1


def away(k):
    return 4 + (k // 2) * (1 - 2 * (k % 2)) - k % 2


def mix_kernel(
    x_hbm, sg_hbm, idx_hbm, both_out,
    xv, sgv, idxv, idx, t, zo, acc, rc, ry, rz, rx, ms, mt, gs, gr, gz, gf,
    in_sem, cs, cr, ys, yr, zs, zr, xs, xr, gss, gsr, gzs, gzr, gfs, gfr,
):
    row, col = lax.axis_index("row"), lax.axis_index("col")
    c = row % 2
    xl = (row // 2) % 2
    y = (row // 4) % 4
    z = row // 16
    x = col * 2 + xl

    def dev(z_, y_, x_, c_):
        return {"row": z_ * 16 + y_ * 4 + (x_ % 2) * 2 + c_, "col": x_ // 2}

    def near(dy, dx, dc):
        return dev(z, (y + dy) % 4, (x + dx) % 4, (c + dc) % 2)

    def plane(i):
        return near(i // 8, (i // 2) % 4, i % 2)

    def along_z(d):
        return dev((z + d) % 8, y, x, c)

    def loop(first, last, body):
        def step(i, carry):
            body(i)
            return carry

        lax.fori_loop(first, last, step, 0)

    fetch_rows = pltpu.make_async_copy(idx_hbm, idxv, in_sem.at[8])
    fetch_signs = pltpu.make_async_copy(sg_hbm, sgv, in_sem.at[9])
    place_rows = pltpu.make_async_copy(idxv, idx, in_sem.at[10])

    def fetch(i):
        at = pl.ds(pl.multiple_of(i * 8, 8), 8)
        return pltpu.make_async_copy(x_hbm.at[at], xv.at[at], in_sem.at[i])

    fetch_rows.start()
    fetch_signs.start()
    loop(0, 8, lambda i: fetch(i).start())

    barrier = pltpu.get_barrier_semaphore()
    loop(1, 32, lambda i: pl.semaphore_signal(barrier, inc=1, device_id=plane(i), device_id_type=MESH))
    loop(1, 8, lambda d: pl.semaphore_signal(barrier, inc=1, device_id=along_z(d), device_id_type=MESH))

    ri = lax.broadcasted_iota(jnp.int32, (LO, LO), 0)
    ci = lax.broadcasted_iota(jnp.int32, (LO, LO), 1)
    h = ((1 - 2 * parity(ri & ci)).astype(F32) * (1.0 / 1024.0)).astype(BF16)
    h = jnp.concatenate([h, h, h], axis=1)
    fetch_rows.wait()
    idxv[...] = idxv[...] & (LOCAL - 1)
    place_rows.start()
    fetch_signs.wait()

    def butterfly(i):
        fetch(i).wait()
        rows = pl.ds(pl.multiple_of(i * 8, 8), 8)
        for bt in range(LO // 128):
            v = []
            for u in range(NU):
                at = u * LO + bt * 128
                v.append(xv[rows, at : at + 128] * sgv[at // 128 : at // 128 + 1, :].astype(F32))
            step = 1
            while step < NU:
                for u in range(NU):
                    if not u & step:
                        v[u], v[u + step] = v[u] + v[u + step], v[u] - v[u + step]
                step *= 2
            for u in range(NU):
                at = u * LO + bt * 128
                xv[rows, at : at + 128] = v[u]

    loop(0, 8, butterfly)

    def lower(g):
        parts = []
        for i in range(2):
            for top in (0, NU // 2):
                at = pl.multiple_of((2 * g + i + top) * LO, LO)
                v = xv[:, pl.ds(at, LO)]
                hi = v.astype(BF16)
                rest = v - hi.astype(F32)
                mid = rest.astype(BF16)
                low = (rest - mid.astype(F32)).astype(BF16)
                parts.append(jnp.concatenate([hi, mid, low], axis=1))
        w = jnp.concatenate(parts, axis=0)
        o = lax.dot_general(h, w, (((1,), (1,)), ((), ())), preferred_element_type=F32)
        for i in range(2):
            part = o[:, 128 * i : 128 * i + 128]
            at = pl.multiple_of((2 * g + i) * LO, LO)
            t[pl.ds(at, LO), :] = part
            t[pl.ds(at + LOCAL, LO), :] = part
            t[pl.ds(at + HALF, LO), :] = pltpu.roll(part, 64, 1)

    loop(0, NU // 4, lower)

    place_rows.wait()
    pl.semaphore_wait(barrier, 38)

    left = lax.broadcasted_iota(jnp.int32, (8, 128), 1) < 64
    sub = lax.broadcasted_iota(jnp.int32, (8, 128), 0)
    shifted = t.at[pl.ds(HALF, LOCAL)]

    def pick(out, k, cq):
        zq = (z + away(k)) % 8

        def body(i, carry):
            q = zq * 16 + i * 2 + cq
            sign = (1 - 2 * parity(row & q)).astype(F32)
            for top in (0, 8):
                v = None
                for j in range(8):
                    a = jnp.broadcast_to(t[pl.ds(idx[q * 32 + top + j], 1), :], (8, 128))
                    b = jnp.broadcast_to(shifted[pl.ds(idx[q * 32 + 16 + top + j], 1), :], (8, 128))
                    r = jnp.where(left, a, b)
                    v = r if v is None else jnp.where(sub == j, r, v)
                out[k, pl.ds(pl.multiple_of(i * 16, 16) + top, 8), :] = v * sign
            return carry

        lax.fori_loop(0, 8, body, 0, unroll=4)

    def remote(src, dst, ss, rs, device):
        return pltpu.make_async_remote_copy(
            src_ref=src, dst_ref=dst, send_sem=ss, recv_sem=rs,
            device_id=device, device_id_type=MESH,
        )

    def block(i):
        return pl.ds(pl.multiple_of(i * 32, 32), 32)

    def to_core(k):
        return remote(zo.at[k], rc.at[k], cs.at[k], cr.at[k], near(0, 0, 1))

    def to_y(k, d):
        return remote(acc.at[k, block((y + d) % 4)], ry.at[k, d - 1], ys.at[k, d - 1], yr.at[k, d - 1], near(d, 0, 0))

    def to_z(k):
        return remote(acc.at[k, block(y)], rz.at[k], zs.at[k], zr.at[k], along_z(away(k)))

    def pick_other(k):
        pick(zo, k, 1 - c)
        to_core(k).start()

    def pick_own(k):
        pick(acc, k, c)
        to_core(k).wait_recv()
        acc[k] = acc[k] + rc[k]
        for d in (2, 1, 3):
            to_y(k, d).start()

    def add_y(k):
        for d in (2, 1, 3):
            to_y(k, d).wait_recv()
        mine = block(y)
        acc[k, mine] = (acc[k, mine] + ry[k, 0]) + (ry[k, 1] + ry[k, 2])

    def pass_z(k):
        add_y(k)
        to_z(k).start()

    loop(0, 8, pick_other)
    loop(0, 8, pick_own)
    loop(0, 7, pass_z)
    add_y(7)
    loop(0, 7, lambda k: to_z(k).wait_recv())
    r = [rz[i] for i in range(7)]
    rx[x] = ((acc[7, block(y)] + r[0]) + (r[1] + r[2])) + ((r[3] + r[4]) + (r[5] + r[6]))

    def to_x(d):
        return remote(rx.at[x], rx.at[x], xs.at[d - 1], xr.at[d - 1], near(0, d, 0))

    for d in (2, 1, 3):
        to_x(d).start()

    def sent(k):
        to_core(k).wait_send()
        for d in (2, 1, 3):
            to_y(k, d).wait_send()

    loop(0, 8, sent)
    for d in (2, 1, 3):
        to_x(d).wait_recv()
    a0 = rx[0] + rx[1]
    a1 = rx[2] + rx[3]
    first = jnp.concatenate([a0[:, :64], a1[:, :64]], axis=1)
    second = jnp.concatenate([a0[:, 64:], a1[:, 64:]], axis=1)
    m = jnp.concatenate([first, second], axis=0)
    mt[...] = m.T
    g = jnp.dot(
        mt[pl.ds(pl.multiple_of(x * 32, 32), 32), :], m,
        preferred_element_type=F32, precision=lax.Precision.HIGHEST,
    )
    for e in range(8):
        gs[e] = g[4 * e : 4 * e + 4]

    own = y * 2 + c

    def to_gs(i):
        dy, dc = i // 2, i % 2
        e = ((y + dy) % 4) * 2 + (c + dc) % 2
        return remote(gs.at[e], gr.at[i - 1], gss.at[i - 1], gsr.at[i - 1], near(dy, 0, dc))

    def to_gz(d):
        return remote(gz.at[z], gz.at[z], gzs.at[d - 1], gzr.at[d - 1], along_z(d))

    place = x * 8 + own

    def to_gf(i):
        return remote(gf.at[place], gf.at[place], gfs.at[i - 1], gfr.at[i - 1], plane(i))

    loop(1, 8, lambda i: to_gs(i).start())
    ms[0, 0], ms[0, 1] = first[:16], first[16:]
    ms[1, 0], ms[1, 1] = second[:16], second[16:]
    both_out[128:144, :] = ms[0, xl]
    both_out[144:160, :] = ms[1, xl]
    loop(0, 7, lambda k: to_z(k).wait_send())
    loop(1, 8, lambda i: to_gs(i).wait_recv())
    gz[z] = ((gs[own] + gr[0]) + (gr[1] + gr[2])) + ((gr[3] + gr[4]) + (gr[5] + gr[6]))
    loop(1, 8, lambda d: to_gz(d).start())
    for d in (2, 1, 3):
        to_x(d).wait_send()
    loop(1, 8, lambda i: to_gs(i).wait_send())
    loop(1, 8, lambda d: to_gz(d).wait_recv())
    gf[place] = (((gz[0] + gz[1]) + (gz[2] + gz[3])) + ((gz[4] + gz[5]) + (gz[6] + gz[7]))) * (1.0 / 4096.0)
    loop(1, 32, lambda i: to_gf(i).start())
    loop(1, 8, lambda d: to_gz(d).wait_send())

    def land(i):
        to_gf(i).wait_recv()
        to_gf(i).wait_send()

    loop(1, 32, land)
    for e in range(32):
        both_out[e * 4 : (e + 1) * 4, :] = gf[e]


def mix(panel, signs, rows):
    vm = pl.BlockSpec(memory_space=pltpu.VMEM)
    hbm = pl.BlockSpec(memory_space=pltpu.HBM)
    V = pltpu.VMEM
    D = pltpu.SemaphoreType.DMA
    return pl.pallas_call(
        mix_kernel,
        out_shape=jax.ShapeDtypeStruct((160, 128), F32),
        in_specs=[hbm, hbm, hbm],
        out_specs=vm,
        scratch_shapes=[
            V((64, LOCAL), F32),
            V((LOCAL // 128, 128), jnp.int32),
            V((4096,), jnp.int32),
            pltpu.SMEM((4096,), jnp.int32),
            V((LOCAL + HALF, 128), F32),
            V((8, 128, 128), F32),
            V((8, 128, 128), F32),
            V((8, 128, 128), F32),
            V((8, 3, 32, 128), F32),
            V((7, 32, 128), F32),
            V((4, 32, 128), F32),
            V((2, 2, 16, 128), F32),
            V((128, 64), F32),
            V((8, 4, 128), F32),
            V((7, 4, 128), F32),
            V((8, 4, 128), F32),
            V((32, 4, 128), F32),
            D((11,)),
            D((8,)), D((8,)), D((8, 3)), D((8, 3)), D((7,)), D((7,)), D((3,)), D((3,)),
            D((7,)), D((7,)), D((7,)), D((7,)), D((31,)), D((31,)),
        ],
        compiler_params=pltpu.CompilerParams(
            collective_id=0, has_side_effects=True, vmem_limit_bytes=62 << 20
        ),
        name="mix",
    )(panel, signs.reshape(LOCAL // 128, 128), rows)


def rows_const(v, j):
    return jnp.broadcast_to(v[:, j : j + 1], (8, 128))


def factor_kernel(both_ref, basis_ref, tri_ref, a_ref, u_ref):
    n, width = 128, 32
    col = lax.axis_index("col")
    a_ref[:, :128] = both_ref[:128, :]
    samples = jnp.concatenate([both_ref[128:, :], jnp.zeros((96, 128), F32)], axis=0)
    a_ref[:, 128:] = samples.T
    lane = lax.broadcasted_iota(jnp.int32, (8, 128), 1)
    for panel in range(n // width):
        top = panel * width
        nb = width // 8
        blocks = [
            [a_ref[top + 8 * i : top + 8 * i + 8, 128 * t : 128 * t + 128] for t in range(2)]
            for i in range(nb)
        ]
        for j in range(nb):
            at = top + 8 * j
            rows = [
                [jnp.broadcast_to(blocks[j][t][k : k + 1, :], (8, 128)) for t in range(2)]
                for k in range(8)
            ]
            d = {(i, k): rows_const(rows[i][0], at + k) for i in range(8) for k in range(i + 1)}
            below = [[rows_const(blocks[i][0], at + k) for k in range(8)] for i in range(j + 1, nb)]
            for k in range(8):
                r = lax.rsqrt(d[k, k])
                for i in range(k + 1, 8):
                    d[i, k] = d[i, k] * r
                for i in range(k + 1, 8):
                    for q in range(k + 1, i + 1):
                        d[i, q] = d[i, q] - d[i, k] * d[q, k]
                for t in range(2):
                    rows[k][t] = rows[k][t] * r
                    for q in range(k + 1, 8):
                        rows[q][t] = rows[q][t] - d[q, k] * rows[k][t]
                for b in below:
                    b[k] = b[k] * r
                    for q in range(k + 1, 8):
                        b[q] = b[q] - d[q, k] * b[k]
            for k in range(8):
                keep = lane >= at + k
                u_ref[at + k : at + k + 1, :128] = jnp.where(keep, rows[k][0], 0.0)[:1]
                u_ref[at + k : at + k + 1, 128:] = rows[k][1][:1]
            for i in range(j + 1, nb):
                b = below[i - j - 1]
                for t in range(2):
                    v = blocks[i][t]
                    for k in range(8):
                        v = v - b[k] * rows[k][t]
                    blocks[i][t] = v
        if top + width < n:
            rest = top + width
            u = u_ref[top:rest, :]
            left = u[:, :128].T[rest:, :]
            upd = jnp.dot(left, u, preferred_element_type=F32, precision=lax.Precision.HIGHEST)
            a_ref[rest:, :] = a_ref[rest:, :] - upd
    half = pl.ds(pl.multiple_of(col * 64, 64), 64)
    tri_ref[...] = u_ref[half, :128]
    basis_ref[...] = u_ref[half, 128:].T[:32]


def factor(both):
    vm = pl.BlockSpec(memory_space=pltpu.VMEM)
    return pl.pallas_call(
        factor_kernel,
        out_shape=(jax.ShapeDtypeStruct((32, 64), F32), jax.ShapeDtypeStruct((64, 128), F32)),
        in_specs=[vm],
        out_specs=(vm, vm),
        scratch_shapes=[pltpu.VMEM((128, 256), F32), pltpu.VMEM((128, 256), F32)],
        compiler_params=pltpu.CompilerParams(vmem_limit_bytes=16 << 20),
        name="factor",
    )(both)


def shards(tall_panel_array, row_signs, sample_rows):
    basis, upper = factor(mix(tall_panel_array, row_signs, sample_rows))
    return basis.T, upper


def solution(mesh):
    return jax.shard_map(
        shards,
        mesh=mesh,
        in_specs=(P("col", "row"), P("row"), P()),
        out_specs=(P("col", "row"), P("col", None)),
        check_vma=False,
    )
```

```python
import jax
import jax.numpy as jnp
from jax import lax
from jax.experimental import pallas as pl
from jax.experimental.pallas import tpu as pltpu
from jax.sharding import PartitionSpec as P

F32 = jnp.float32
BF16 = jnp.bfloat16
MESH = pl.DeviceIdType.MESH
LO = 256
NU = 32
LOCAL = LO * NU
HALF = LOCAL // 2


def parity(bits):
    bits = bits ^ (bits >> 4)
    bits = bits ^ (bits >> 2)
    bits = bits ^ (bits >> 1)
    return bits & 1


def away(k):
    return 4 + (k // 2) * (1 - 2 * (k % 2)) - k % 2


def mix_kernel(
    x_hbm, sg_hbm, idx_hbm, both_out,
    xv, sgv, idxv, idx, t, zo, acc, rc, ry, rz, rx, ms, mt, gs, gr, gz, gf,
    in_sem, cs, cr, ys, yr, zs, zr, xs, xr, gss, gsr, gzs, gzr, gfs, gfr,
):
    row, col = lax.axis_index("row"), lax.axis_index("col")
    c = row % 2
    xl = (row // 2) % 2
    y = (row // 4) % 4
    z = row // 16
    x = col * 2 + xl

    def dev(z_, y_, x_, c_):
        return {"row": z_ * 16 + y_ * 4 + (x_ % 2) * 2 + c_, "col": x_ // 2}

    def near(dy, dx, dc):
        return dev(z, (y + dy) % 4, (x + dx) % 4, (c + dc) % 2)

    def along_z(d):
        return dev((z + d) % 8, y, x, c)

    def loop(first, last, body):
        def step(i, carry):
            body(i)
            return carry

        lax.fori_loop(first, last, step, 0)

    fetch_rows = pltpu.make_async_copy(idx_hbm, idxv, in_sem.at[8])
    fetch_signs = pltpu.make_async_copy(sg_hbm, sgv, in_sem.at[9])
    place_rows = pltpu.make_async_copy(idxv, idx, in_sem.at[10])

    def fetch(i):
        at = pl.ds(pl.multiple_of(i * 8, 8), 8)
        return pltpu.make_async_copy(x_hbm.at[at], xv.at[at], in_sem.at[i])

    fetch_rows.start()
    fetch_signs.start()
    loop(0, 8, lambda i: fetch(i).start())

    barrier = pltpu.get_barrier_semaphore()
    loop(1, 8, lambda i: pl.semaphore_signal(barrier, inc=1, device_id=near(i // 2, 0, i % 2), device_id_type=MESH))
    loop(2, 8, lambda i: pl.semaphore_signal(barrier, inc=1, device_id=near(0, i // 2, i % 2), device_id_type=MESH))
    loop(1, 8, lambda d: pl.semaphore_signal(barrier, inc=1, device_id=along_z(d), device_id_type=MESH))

    ri = lax.broadcasted_iota(jnp.int32, (LO, LO), 0)
    ci = lax.broadcasted_iota(jnp.int32, (LO, LO), 1)
    h = ((1 - 2 * parity(ri & ci)).astype(F32) * (1.0 / 1024.0)).astype(BF16)
    h = jnp.concatenate([h, h, h], axis=1)
    fetch_rows.wait()
    idxv[...] = idxv[...] & (LOCAL - 1)
    place_rows.start()
    fetch_signs.wait()

    def butterfly(i):
        fetch(i).wait()
        rows = pl.ds(pl.multiple_of(i * 8, 8), 8)
        for bt in range(LO // 128):
            v = []
            for u in range(NU):
                at = u * LO + bt * 128
                v.append(xv[rows, at : at + 128] * sgv[at // 128 : at // 128 + 1, :].astype(F32))
            step = 1
            while step < NU:
                for u in range(NU):
                    if not u & step:
                        v[u], v[u + step] = v[u] + v[u + step], v[u] - v[u + step]
                step *= 2
            for u in range(NU):
                at = u * LO + bt * 128
                xv[rows, at : at + 128] = v[u]

    loop(0, 8, butterfly)

    def lower(g):
        parts = []
        for i in range(2):
            for top in (0, NU // 2):
                at = pl.multiple_of((2 * g + i + top) * LO, LO)
                v = xv[:, pl.ds(at, LO)]
                hi = v.astype(BF16)
                rest = v - hi.astype(F32)
                mid = rest.astype(BF16)
                low = (rest - mid.astype(F32)).astype(BF16)
                parts.append(jnp.concatenate([hi, mid, low], axis=1))
        w = jnp.concatenate(parts, axis=0)
        o = lax.dot_general(h, w, (((1,), (1,)), ((), ())), preferred_element_type=F32)
        for i in range(2):
            part = o[:, 128 * i : 128 * i + 128]
            at = pl.multiple_of((2 * g + i) * LO, LO)
            t[pl.ds(at, LO), :] = part
            t[pl.ds(at + LOCAL, LO), :] = part
            t[pl.ds(at + HALF, LO), :] = pltpu.roll(part, 64, 1)

    loop(0, NU // 4, lower)

    place_rows.wait()
    pl.semaphore_wait(barrier, 20)

    left = lax.broadcasted_iota(jnp.int32, (8, 128), 1) < 64
    sub = lax.broadcasted_iota(jnp.int32, (8, 128), 0)
    shifted = t.at[pl.ds(HALF, LOCAL)]

    def pick(out, k, cq):
        zq = (z + away(k)) % 8

        def body(i, carry):
            q = zq * 16 + i * 2 + cq
            sign = (1 - 2 * parity(row & q)).astype(F32)
            for top in (0, 8):
                v = None
                for j in range(8):
                    a = jnp.broadcast_to(t[pl.ds(idx[q * 32 + top + j], 1), :], (8, 128))
                    b = jnp.broadcast_to(shifted[pl.ds(idx[q * 32 + 16 + top + j], 1), :], (8, 128))
                    r = jnp.where(left, a, b)
                    v = r if v is None else jnp.where(sub == j, r, v)
                out[k, pl.ds(pl.multiple_of(i * 16, 16) + top, 8), :] = v * sign
            return carry

        lax.fori_loop(0, 8, body, 0, unroll=4)

    def remote(src, dst, ss, rs, device):
        return pltpu.make_async_remote_copy(
            src_ref=src, dst_ref=dst, send_sem=ss, recv_sem=rs,
            device_id=device, device_id_type=MESH,
        )

    def block(i):
        return pl.ds(pl.multiple_of(i * 32, 32), 32)

    def to_core(k):
        return remote(zo.at[k], rc.at[k], cs.at[k], cr.at[k], near(0, 0, 1))

    def to_y(k, d):
        return remote(acc.at[k, block((y + d) % 4)], ry.at[k, d - 1], ys.at[k, d - 1], yr.at[k, d - 1], near(d, 0, 0))

    def to_z(k):
        return remote(acc.at[k, block(y)], rz.at[k], zs.at[k], zr.at[k], along_z(away(k)))

    def pick_other(k):
        pick(zo, k, 1 - c)
        to_core(k).start()

    def pick_own(k):
        pick(acc, k, c)
        to_core(k).wait_recv()
        acc[k] = acc[k] + rc[k]
        for d in (2, 1, 3):
            to_y(k, d).start()

    def add_y(k):
        for d in (2, 1, 3):
            to_y(k, d).wait_recv()
        mine = block(y)
        acc[k, mine] = (acc[k, mine] + ry[k, 0]) + (ry[k, 1] + ry[k, 2])

    def pass_z(k):
        add_y(k)
        to_z(k).start()

    loop(0, 8, pick_other)
    loop(0, 8, pick_own)
    loop(0, 7, pass_z)
    add_y(7)
    loop(0, 7, lambda k: to_z(k).wait_recv())
    r = [rz[i] for i in range(7)]
    rx[x] = ((acc[7, block(y)] + r[0]) + (r[1] + r[2])) + ((r[3] + r[4]) + (r[5] + r[6]))

    def to_x(d):
        return remote(rx.at[x], rx.at[x], xs.at[d - 1], xr.at[d - 1], near(0, d, 0))

    for d in (2, 1, 3):
        to_x(d).start()

    def sent(k):
        to_core(k).wait_send()
        for d in (2, 1, 3):
            to_y(k, d).wait_send()

    loop(0, 8, sent)
    for d in (2, 1, 3):
        to_x(d).wait_recv()
    a0 = rx[0] + rx[1]
    a1 = rx[2] + rx[3]
    first = jnp.concatenate([a0[:, :64], a1[:, :64]], axis=1)
    second = jnp.concatenate([a0[:, 64:], a1[:, 64:]], axis=1)
    m = jnp.concatenate([first, second], axis=0)
    mt[...] = m.T
    g = jnp.dot(
        mt[pl.ds(pl.multiple_of(x * 32, 32), 32), :], m,
        preferred_element_type=F32, precision=lax.Precision.HIGHEST,
    )
    for e in range(8):
        gs[e] = g[4 * e : 4 * e + 4]

    own = c * 4 + y

    def to_gs(i):
        dy, dc = i // 2, i % 2
        e = ((c + dc) % 2) * 4 + (y + dy) % 4
        return remote(gs.at[e], gr.at[i - 1], gss.at[i - 1], gsr.at[i - 1], near(dy, 0, dc))

    def to_gz(d):
        return remote(gz.at[z], gz.at[z], gzs.at[d - 1], gzr.at[d - 1], along_z(d))

    place = x * 8 + own

    def to_gy(d):
        return remote(gf.at[place], gf.at[place], gfs.at[d - 1], gfr.at[d - 1], near(d, 0, 0))

    def to_gf(i):
        four = pl.ds(pl.multiple_of(x * 8 + c * 4, 4), 4)
        return remote(gf.at[four], gf.at[four], gfs.at[i + 2], gfr.at[i + 2], near(0, i // 2, i % 2))

    loop(1, 8, lambda i: to_gs(i).start())
    ms[0, 0], ms[0, 1] = first[:16], first[16:]
    ms[1, 0], ms[1, 1] = second[:16], second[16:]
    both_out[128:144, :] = ms[0, xl]
    both_out[144:160, :] = ms[1, xl]
    loop(0, 7, lambda k: to_z(k).wait_send())
    loop(1, 8, lambda i: to_gs(i).wait_recv())
    gz[z] = ((gs[own] + gr[0]) + (gr[1] + gr[2])) + ((gr[3] + gr[4]) + (gr[5] + gr[6]))
    loop(1, 8, lambda d: to_gz(d).start())
    for d in (2, 1, 3):
        to_x(d).wait_send()
    loop(1, 8, lambda i: to_gs(i).wait_send())
    loop(1, 8, lambda d: to_gz(d).wait_recv())
    gf[place] = (((gz[0] + gz[1]) + (gz[2] + gz[3])) + ((gz[4] + gz[5]) + (gz[6] + gz[7]))) * (1.0 / 4096.0)
    for d in (2, 1, 3):
        to_gy(d).start()
    loop(1, 8, lambda d: to_gz(d).wait_send())
    for d in (2, 1, 3):
        to_gy(d).wait_recv()
    loop(1, 8, lambda i: to_gf(i).start())
    for d in (2, 1, 3):
        to_gy(d).wait_send()

    def land(i):
        to_gf(i).wait_recv()
        to_gf(i).wait_send()

    loop(1, 8, land)
    for e in range(32):
        both_out[e * 4 : (e + 1) * 4, :] = gf[e]


def mix(panel, signs, rows):
    vm = pl.BlockSpec(memory_space=pltpu.VMEM)
    hbm = pl.BlockSpec(memory_space=pltpu.HBM)
    V = pltpu.VMEM
    D = pltpu.SemaphoreType.DMA
    return pl.pallas_call(
        mix_kernel,
        out_shape=jax.ShapeDtypeStruct((160, 128), F32),
        in_specs=[hbm, hbm, hbm],
        out_specs=vm,
        scratch_shapes=[
            V((64, LOCAL), F32),
            V((LOCAL // 128, 128), jnp.int32),
            V((4096,), jnp.int32),
            pltpu.SMEM((4096,), jnp.int32),
            V((LOCAL + HALF, 128), F32),
            V((8, 128, 128), F32),
            V((8, 128, 128), F32),
            V((8, 128, 128), F32),
            V((8, 3, 32, 128), F32),
            V((7, 32, 128), F32),
            V((4, 32, 128), F32),
            V((2, 2, 16, 128), F32),
            V((128, 64), F32),
            V((8, 4, 128), F32),
            V((7, 4, 128), F32),
            V((8, 4, 128), F32),
            V((32, 4, 128), F32),
            D((11,)),
            D((8,)), D((8,)), D((8, 3)), D((8, 3)), D((7,)), D((7,)), D((3,)), D((3,)),
            D((7,)), D((7,)), D((7,)), D((7,)), D((10,)), D((10,)),
        ],
        compiler_params=pltpu.CompilerParams(
            collective_id=0, has_side_effects=True, vmem_limit_bytes=62 << 20
        ),
        name="mix",
    )(panel, signs.reshape(LOCAL // 128, 128), rows)


def rows_const(v, j):
    return jnp.broadcast_to(v[:, j : j + 1], (8, 128))


def factor_kernel(both_ref, basis_ref, tri_ref, a_ref, u_ref):
    n, width = 128, 32
    col = lax.axis_index("col")
    a_ref[:, :128] = both_ref[:128, :]
    samples = jnp.concatenate([both_ref[128:, :], jnp.zeros((96, 128), F32)], axis=0)
    a_ref[:, 128:] = samples.T
    lane = lax.broadcasted_iota(jnp.int32, (8, 128), 1)
    for panel in range(n // width):
        top = panel * width
        nb = width // 8
        blocks = [
            [a_ref[top + 8 * i : top + 8 * i + 8, 128 * t : 128 * t + 128] for t in range(2)]
            for i in range(nb)
        ]
        for j in range(nb):
            at = top + 8 * j
            rows = [
                [jnp.broadcast_to(blocks[j][t][k : k + 1, :], (8, 128)) for t in range(2)]
                for k in range(8)
            ]
            d = {(i, k): rows_const(rows[i][0], at + k) for i in range(8) for k in range(i + 1)}
            below = [[rows_const(blocks[i][0], at + k) for k in range(8)] for i in range(j + 1, nb)]
            for k in range(8):
                r = lax.rsqrt(d[k, k])
                for i in range(k + 1, 8):
                    d[i, k] = d[i, k] * r
                for i in range(k + 1, 8):
                    for q in range(k + 1, i + 1):
                        d[i, q] = d[i, q] - d[i, k] * d[q, k]
                for t in range(2):
                    rows[k][t] = rows[k][t] * r
                    for q in range(k + 1, 8):
                        rows[q][t] = rows[q][t] - d[q, k] * rows[k][t]
                for b in below:
                    b[k] = b[k] * r
                    for q in range(k + 1, 8):
                        b[q] = b[q] - d[q, k] * b[k]
            for k in range(8):
                keep = lane >= at + k
                u_ref[at + k : at + k + 1, :128] = jnp.where(keep, rows[k][0], 0.0)[:1]
                u_ref[at + k : at + k + 1, 128:] = rows[k][1][:1]
            for i in range(j + 1, nb):
                b = below[i - j - 1]
                for t in range(2):
                    v = blocks[i][t]
                    for k in range(8):
                        v = v - b[k] * rows[k][t]
                    blocks[i][t] = v
        if top + width < n:
            rest = top + width
            u = u_ref[top:rest, :]
            left = u[:, :128].T[rest:, :]
            upd = jnp.dot(left, u, preferred_element_type=F32, precision=lax.Precision.HIGHEST)
            a_ref[rest:, :] = a_ref[rest:, :] - upd
    half = pl.ds(pl.multiple_of(col * 64, 64), 64)
    tri_ref[...] = u_ref[half, :128]
    basis_ref[...] = u_ref[half, 128:].T[:32]


def factor(both):
    vm = pl.BlockSpec(memory_space=pltpu.VMEM)
    return pl.pallas_call(
        factor_kernel,
        out_shape=(jax.ShapeDtypeStruct((32, 64), F32), jax.ShapeDtypeStruct((64, 128), F32)),
        in_specs=[vm],
        out_specs=(vm, vm),
        scratch_shapes=[pltpu.VMEM((128, 256), F32), pltpu.VMEM((128, 256), F32)],
        compiler_params=pltpu.CompilerParams(vmem_limit_bytes=16 << 20),
        name="factor",
    )(both)


def shards(tall_panel_array, row_signs, sample_rows):
    basis, upper = factor(mix(tall_panel_array, row_signs, sample_rows))
    return basis.T, upper


def solution(mesh):
    return jax.shard_map(
        shards,
        mesh=mesh,
        in_specs=(P("col", "row"), P("row"), P()),
        out_specs=(P("col", "row"), P("col", None)),
        check_vma=False,
    )
```

```python
import jax
import jax.numpy as jnp
from jax import lax
from jax.experimental import pallas as pl
from jax.experimental.pallas import tpu as pltpu
from jax.sharding import PartitionSpec as P

F32 = jnp.float32
BF16 = jnp.bfloat16
MESH = pl.DeviceIdType.MESH
LO = 256
NU = 32
LOCAL = LO * NU
HALF = LOCAL // 2


def parity(bits):
    bits = bits ^ (bits >> 4)
    bits = bits ^ (bits >> 2)
    bits = bits ^ (bits >> 1)
    return bits & 1


def away(k):
    return 4 + (k // 2) * (1 - 2 * (k % 2)) - k % 2


def mix_kernel(
    x_hbm, sg_hbm, idx_hbm, both_out,
    xv, sgv, idxv, idx, t, zo, acc, rc, ry, rz, rx, ms, mt, gs, gr, gz, gf,
    in_sem, cs, cr, ys, yr, zs, zr, xs, xr, gss, gsr, gzs, gzr, gfs, gfr,
):
    row, col = lax.axis_index("row"), lax.axis_index("col")
    c = row % 2
    xl = (row // 2) % 2
    y = (row // 4) % 4
    z = row // 16
    x = col * 2 + xl

    def dev(z_, y_, x_, c_):
        return {"row": z_ * 16 + y_ * 4 + (x_ % 2) * 2 + c_, "col": x_ // 2}

    def near(dy, dx, dc):
        return dev(z, (y + dy) % 4, (x + dx) % 4, (c + dc) % 2)

    def plane(i):
        return near(i // 8, (i // 2) % 4, i % 2)

    def along_z(d):
        return dev((z + d) % 8, y, x, c)

    def loop(first, last, body):
        def step(i, carry):
            body(i)
            return carry

        lax.fori_loop(first, last, step, 0)

    fetch_rows = pltpu.make_async_copy(idx_hbm, idxv, in_sem.at[8])
    fetch_signs = pltpu.make_async_copy(sg_hbm, sgv, in_sem.at[9])
    place_rows = pltpu.make_async_copy(idxv, idx, in_sem.at[10])

    def fetch(i):
        at = pl.ds(pl.multiple_of(i * 8, 8), 8)
        return pltpu.make_async_copy(x_hbm.at[at], xv.at[at], in_sem.at[i])

    fetch_rows.start()
    fetch_signs.start()
    loop(0, 8, lambda i: fetch(i).start())

    barrier = pltpu.get_barrier_semaphore()
    loop(1, 32, lambda i: pl.semaphore_signal(barrier, inc=1, device_id=plane(i), device_id_type=MESH))
    loop(1, 8, lambda d: pl.semaphore_signal(barrier, inc=1, device_id=along_z(d), device_id_type=MESH))

    ri = lax.broadcasted_iota(jnp.int32, (LO, LO), 0)
    ci = lax.broadcasted_iota(jnp.int32, (LO, LO), 1)
    h = ((1 - 2 * parity(ri & ci)).astype(F32) * (1.0 / 1024.0)).astype(BF16)
    h = jnp.concatenate([h, h, h], axis=1)
    fetch_rows.wait()
    idxv[...] = idxv[...] & (LOCAL - 1)
    place_rows.start()
    fetch_signs.wait()

    def butterfly(i):
        fetch(i).wait()
        rows = pl.ds(pl.multiple_of(i * 8, 8), 8)
        for bt in range(LO // 128):
            v = []
            for u in range(NU):
                at = u * LO + bt * 128
                v.append(xv[rows, at : at + 128] * sgv[at // 128 : at // 128 + 1, :].astype(F32))
            step = 1
            while step < NU:
                for u in range(NU):
                    if not u & step:
                        v[u], v[u + step] = v[u] + v[u + step], v[u] - v[u + step]
                step *= 2
            for u in range(NU):
                at = u * LO + bt * 128
                xv[rows, at : at + 128] = v[u]

    loop(0, 8, butterfly)

    def lower(g):
        parts = []
        for i in range(2):
            for top in (0, NU // 2):
                at = pl.multiple_of((2 * g + i + top) * LO, LO)
                v = xv[:, pl.ds(at, LO)]
                hi = v.astype(BF16)
                rest = v - hi.astype(F32)
                mid = rest.astype(BF16)
                low = (rest - mid.astype(F32)).astype(BF16)
                parts.append(jnp.concatenate([hi, mid, low], axis=1))
        w = jnp.concatenate(parts, axis=0)
        o = lax.dot_general(h, w, (((1,), (1,)), ((), ())), preferred_element_type=F32)
        for i in range(2):
            part = o[:, 128 * i : 128 * i + 128]
            at = pl.multiple_of((2 * g + i) * LO, LO)
            t[pl.ds(at, LO), :] = part
            t[pl.ds(at + LOCAL, LO), :] = part
            t[pl.ds(at + HALF, LO), :] = pltpu.roll(part, 64, 1)

    loop(0, NU // 4, lower)

    place_rows.wait()
    pl.semaphore_wait(barrier, 38)

    left = lax.broadcasted_iota(jnp.int32, (8, 128), 1) < 64
    sub = lax.broadcasted_iota(jnp.int32, (8, 128), 0)
    shifted = t.at[pl.ds(HALF, LOCAL)]

    def pick(out, k, cq):
        zq = (z + away(k)) % 8

        def body(i, carry):
            q = zq * 16 + i * 2 + cq
            sign = (1 - 2 * parity(row & q)).astype(F32)
            for top in (0, 8):
                v = None
                for j in range(8):
                    a = jnp.broadcast_to(t[pl.ds(idx[q * 32 + top + j], 1), :], (8, 128))
                    b = jnp.broadcast_to(shifted[pl.ds(idx[q * 32 + 16 + top + j], 1), :], (8, 128))
                    r = jnp.where(left, a, b)
                    v = r if v is None else jnp.where(sub == j, r, v)
                out[k, pl.ds(pl.multiple_of(i * 16, 16) + top, 8), :] = v * sign
            return carry

        lax.fori_loop(0, 8, body, 0, unroll=4)

    def remote(src, dst, ss, rs, device):
        return pltpu.make_async_remote_copy(
            src_ref=src, dst_ref=dst, send_sem=ss, recv_sem=rs,
            device_id=device, device_id_type=MESH,
        )

    def all_of(ref, ss, rs):
        return remote(ref, ref, ss, rs, near(0, 0, 1))

    def block(i):
        return pl.ds(pl.multiple_of(i * 32, 32), 32)

    def to_core(k):
        return remote(zo.at[k], rc.at[k], cs, cr.at[k], near(0, 0, 1))

    def to_y(k, d):
        return remote(acc.at[k, block((y + d) % 4)], ry.at[k, d - 1], ys, yr.at[k], near(d, 0, 0))

    def to_z(k):
        return remote(acc.at[k, block(y)], rz.at[k], zs, zr, along_z(away(k)))

    def pick_other(k):
        pick(zo, k, 1 - c)
        to_core(k).start()

    def pick_own(k):
        pick(acc, k, c)
        to_core(k).wait_recv()
        acc[k] = acc[k] + rc[k]
        for d in (2, 1, 3):
            to_y(k, d).start()

    def add_y(k):
        all_of(ry.at[k], ys, yr.at[k]).wait_recv()
        mine = block(y)
        acc[k, mine] = (acc[k, mine] + ry[k, 0]) + (ry[k, 1] + ry[k, 2])

    def pass_z(k):
        add_y(k)
        to_z(k).start()

    loop(0, 8, pick_other)
    loop(0, 8, pick_own)
    loop(0, 7, pass_z)
    add_y(7)
    all_of(rz, zs, zr).wait_recv()
    r = [rz[i] for i in range(7)]
    rx[x] = ((acc[7, block(y)] + r[0]) + (r[1] + r[2])) + ((r[3] + r[4]) + (r[5] + r[6]))

    def to_x(d):
        return remote(rx.at[x], rx.at[x], xs, xr, near(0, d, 0))

    for d in (2, 1, 3):
        to_x(d).start()

    all_of(zo, cs, cr.at[0]).wait_send()
    all_of(ry, ys, yr.at[0]).wait_send()
    all_of(rx.at[pl.ds(0, 3)], xs, xr).wait_recv()
    a0 = rx[0] + rx[1]
    a1 = rx[2] + rx[3]
    first = jnp.concatenate([a0[:, :64], a1[:, :64]], axis=1)
    second = jnp.concatenate([a0[:, 64:], a1[:, 64:]], axis=1)
    m = jnp.concatenate([first, second], axis=0)
    mt[...] = m.T
    g = jnp.dot(
        mt[pl.ds(pl.multiple_of(x * 32, 32), 32), :], m,
        preferred_element_type=F32, precision=lax.Precision.HIGHEST,
    )
    for e in range(8):
        gs[e] = g[4 * e : 4 * e + 4]

    own = y * 2 + c

    def to_gs(i):
        dy, dc = i // 2, i % 2
        e = ((y + dy) % 4) * 2 + (c + dc) % 2
        return remote(gs.at[e], gr.at[i - 1], gss, gsr, near(dy, 0, dc))

    def to_gz(d):
        return remote(gz.at[z], gz.at[z], gzs, gzr, along_z(d))

    place = x * 8 + own

    def to_gf(i):
        return remote(gf.at[place], gf.at[place], gfs, gfr, plane(i))

    loop(1, 8, lambda i: to_gs(i).start())
    ms[0, 0], ms[0, 1] = first[:16], first[16:]
    ms[1, 0], ms[1, 1] = second[:16], second[16:]
    both_out[128:144, :] = ms[0, xl]
    both_out[144:160, :] = ms[1, xl]
    all_of(rz, zs, zr).wait_send()
    all_of(rx.at[pl.ds(0, 3)], xs, xr).wait_send()
    all_of(gr, gss, gsr).wait_recv()
    gz[z] = ((gs[own] + gr[0]) + (gr[1] + gr[2])) + ((gr[3] + gr[4]) + (gr[5] + gr[6]))
    loop(1, 8, lambda d: to_gz(d).start())
    all_of(gr, gss, gsr).wait_send()
    all_of(gz.at[pl.ds(0, 7)], gzs, gzr).wait_recv()
    gf[place] = (((gz[0] + gz[1]) + (gz[2] + gz[3])) + ((gz[4] + gz[5]) + (gz[6] + gz[7]))) * (1.0 / 4096.0)
    loop(0, 31, lambda i: to_gf((i + 19) % 31 + 1).start())
    all_of(gz.at[pl.ds(0, 7)], gzs, gzr).wait_send()
    all_of(gf.at[pl.ds(0, 31)], gfs, gfr).wait_recv()
    for e in range(32):
        both_out[e * 4 : (e + 1) * 4, :] = gf[e]
    all_of(gf.at[pl.ds(0, 31)], gfs, gfr).wait_send()


def mix(panel, signs, rows):
    vm = pl.BlockSpec(memory_space=pltpu.VMEM)
    hbm = pl.BlockSpec(memory_space=pltpu.HBM)
    V = pltpu.VMEM
    D = pltpu.SemaphoreType.DMA
    return pl.pallas_call(
        mix_kernel,
        out_shape=jax.ShapeDtypeStruct((160, 128), F32),
        in_specs=[hbm, hbm, hbm],
        out_specs=vm,
        scratch_shapes=[
            V((64, LOCAL), F32),
            V((LOCAL // 128, 128), jnp.int32),
            V((4096,), jnp.int32),
            pltpu.SMEM((4096,), jnp.int32),
            V((LOCAL + HALF, 128), F32),
            V((8, 128, 128), F32),
            V((8, 128, 128), F32),
            V((8, 128, 128), F32),
            V((8, 3, 32, 128), F32),
            V((7, 32, 128), F32),
            V((4, 32, 128), F32),
            V((2, 2, 16, 128), F32),
            V((128, 64), F32),
            V((8, 4, 128), F32),
            V((7, 4, 128), F32),
            V((8, 4, 128), F32),
            V((32, 4, 128), F32),
            D((11,)),
            D, D((8,)), D, D((8,)), D, D, D, D, D, D, D, D, D, D,
        ],
        compiler_params=pltpu.CompilerParams(
            collective_id=0, has_side_effects=True, vmem_limit_bytes=62 << 20
        ),
        name="mix",
    )(panel, signs.reshape(LOCAL // 128, 128), rows)


def rows_const(v, j):
    return jnp.broadcast_to(v[:, j : j + 1], (8, 128))


def factor_kernel(both_ref, basis_ref, tri_ref, a_ref, u_ref):
    n, width = 128, 32
    col = lax.axis_index("col")
    a_ref[:, :128] = both_ref[:128, :]
    samples = jnp.concatenate([both_ref[128:, :], jnp.zeros((96, 128), F32)], axis=0)
    a_ref[:, 128:] = samples.T
    lane = lax.broadcasted_iota(jnp.int32, (8, 128), 1)
    for panel in range(n // width):
        top = panel * width
        nb = width // 8
        blocks = [
            [a_ref[top + 8 * i : top + 8 * i + 8, 128 * t : 128 * t + 128] for t in range(2)]
            for i in range(nb)
        ]
        for j in range(nb):
            at = top + 8 * j
            rows = [
                [jnp.broadcast_to(blocks[j][t][k : k + 1, :], (8, 128)) for t in range(2)]
                for k in range(8)
            ]
            d = {(i, k): rows_const(rows[i][0], at + k) for i in range(8) for k in range(i + 1)}
            below = [[rows_const(blocks[i][0], at + k) for k in range(8)] for i in range(j + 1, nb)]
            for k in range(8):
                r = lax.rsqrt(d[k, k])
                for i in range(k + 1, 8):
                    d[i, k] = d[i, k] * r
                for i in range(k + 1, 8):
                    for q in range(k + 1, i + 1):
                        d[i, q] = d[i, q] - d[i, k] * d[q, k]
                for t in range(2):
                    rows[k][t] = rows[k][t] * r
                    for q in range(k + 1, 8):
                        rows[q][t] = rows[q][t] - d[q, k] * rows[k][t]
                for b in below:
                    b[k] = b[k] * r
                    for q in range(k + 1, 8):
                        b[q] = b[q] - d[q, k] * b[k]
            for k in range(8):
                keep = lane >= at + k
                u_ref[at + k : at + k + 1, :128] = jnp.where(keep, rows[k][0], 0.0)[:1]
                u_ref[at + k : at + k + 1, 128:] = rows[k][1][:1]
            for i in range(j + 1, nb):
                b = below[i - j - 1]
                for t in range(2):
                    v = blocks[i][t]
                    for k in range(8):
                        v = v - b[k] * rows[k][t]
                    blocks[i][t] = v
        if top + width < n:
            rest = top + width
            u = u_ref[top:rest, :]
            left = u[:, :128].T[rest:, :]
            upd = jnp.dot(left, u, preferred_element_type=F32, precision=lax.Precision.HIGHEST)
            a_ref[rest:, :] = a_ref[rest:, :] - upd
    half = pl.ds(pl.multiple_of(col * 64, 64), 64)
    tri_ref[...] = u_ref[half, :128]
    basis_ref[...] = u_ref[half, 128:].T[:32]


def factor(both):
    vm = pl.BlockSpec(memory_space=pltpu.VMEM)
    return pl.pallas_call(
        factor_kernel,
        out_shape=(jax.ShapeDtypeStruct((32, 64), F32), jax.ShapeDtypeStruct((64, 128), F32)),
        in_specs=[vm],
        out_specs=(vm, vm),
        scratch_shapes=[pltpu.VMEM((128, 256), F32), pltpu.VMEM((128, 256), F32)],
        compiler_params=pltpu.CompilerParams(vmem_limit_bytes=16 << 20),
        name="factor",
    )(both)


def shards(tall_panel_array, row_signs, sample_rows):
    basis, upper = factor(mix(tall_panel_array, row_signs, sample_rows))
    return basis.T, upper


def solution(mesh):
    return jax.shard_map(
        shards,
        mesh=mesh,
        in_specs=(P("col", "row"), P("row"), P()),
        out_specs=(P("col", "row"), P("col", None)),
        check_vma=False,
    )
```

```python
import jax
import jax.numpy as jnp
from jax import lax
from jax.experimental import pallas as pl
from jax.experimental.pallas import tpu as pltpu
from jax.sharding import PartitionSpec as P

F32 = jnp.float32
BF16 = jnp.bfloat16
MESH = pl.DeviceIdType.MESH
LO = 256
NU = 32
LOCAL = LO * NU
HALF = LOCAL // 2


def parity(bits):
    bits = bits ^ (bits >> 4)
    bits = bits ^ (bits >> 2)
    bits = bits ^ (bits >> 1)
    return bits & 1


def away(k):
    return 4 + (k // 2) * (1 - 2 * (k % 2)) - k % 2


def mix_kernel(
    x_hbm, sg_hbm, idx_hbm, both_out,
    xv, sgv, idxv, idx, t, zo, acc, rc, ry, rz, rx, ms, mt, gs, gr, gz, gf,
    in_sem, cs, cr, ys, yr, zs, zr, xs, xr, gss, gsr, gzs, gzr, gfs, gfr,
):
    row, col = lax.axis_index("row"), lax.axis_index("col")
    c = row % 2
    xl = (row // 2) % 2
    y = (row // 4) % 4
    z = row // 16
    x = col * 2 + xl

    def dev(z_, y_, x_, c_):
        return {"row": z_ * 16 + y_ * 4 + (x_ % 2) * 2 + c_, "col": x_ // 2}

    def near(dy, dx, dc):
        return dev(z, (y + dy) % 4, (x + dx) % 4, (c + dc) % 2)

    def plane(i):
        return near(i // 8, (i // 2) % 4, i % 2)

    def along_z(d):
        return dev((z + d) % 8, y, x, c)

    def loop(first, last, body):
        def step(i, carry):
            body(i)
            return carry

        lax.fori_loop(first, last, step, 0)

    fetch_rows = pltpu.make_async_copy(idx_hbm, idxv, in_sem.at[8])
    fetch_signs = pltpu.make_async_copy(sg_hbm, sgv, in_sem.at[9])
    place_rows = pltpu.make_async_copy(idxv, idx, in_sem.at[10])

    def fetch(i):
        at = pl.ds(pl.multiple_of(i * 8, 8), 8)
        return pltpu.make_async_copy(x_hbm.at[at], xv.at[at], in_sem.at[i])

    fetch_rows.start()
    fetch_signs.start()
    loop(0, 8, lambda i: fetch(i).start())

    barrier = pltpu.get_barrier_semaphore()
    loop(1, 32, lambda i: pl.semaphore_signal(barrier, inc=1, device_id=plane(i), device_id_type=MESH))
    loop(1, 8, lambda d: pl.semaphore_signal(barrier, inc=1, device_id=along_z(d), device_id_type=MESH))

    ri = lax.broadcasted_iota(jnp.int32, (LO, LO), 0)
    ci = lax.broadcasted_iota(jnp.int32, (LO, LO), 1)
    h = ((1 - 2 * parity(ri & ci)).astype(F32) * (1.0 / 1024.0)).astype(BF16)
    h = jnp.concatenate([h, h, h], axis=1)
    fetch_rows.wait()
    idxv[...] = idxv[...] & (LOCAL - 1)
    place_rows.start()
    fetch_signs.wait()

    def butterfly(i):
        fetch(i).wait()
        rows = pl.ds(pl.multiple_of(i * 8, 8), 8)
        for bt in range(LO // 128):
            v = []
            for u in range(NU):
                at = u * LO + bt * 128
                v.append(xv[rows, at : at + 128] * sgv[at // 128 : at // 128 + 1, :].astype(F32))
            step = 1
            while step < NU:
                for u in range(NU):
                    if not u & step:
                        v[u], v[u + step] = v[u] + v[u + step], v[u] - v[u + step]
                step *= 2
            for u in range(NU):
                at = u * LO + bt * 128
                xv[rows, at : at + 128] = v[u]

    loop(0, 8, butterfly)

    def lower(g):
        parts = []
        for i in range(2):
            for top in (0, NU // 2):
                at = (2 * g + i + top) * LO
                v = xv[:, at : at + LO]
                hi = v.astype(BF16)
                rest = v - hi.astype(F32)
                mid = rest.astype(BF16)
                low = (rest - mid.astype(F32)).astype(BF16)
                parts.append(jnp.concatenate([hi, mid, low], axis=1))
        w = jnp.concatenate(parts, axis=0)
        o = lax.dot_general(h, w, (((1,), (1,)), ((), ())), preferred_element_type=F32)
        for i in range(2):
            part = o[:, 128 * i : 128 * i + 128]
            at = (2 * g + i) * LO
            t[at : at + LO, :] = part
            t[at + LOCAL : at + LOCAL + LO, :] = part
            t[at + HALF : at + HALF + LO, :] = pltpu.roll(part, 64, 1)

    for g in range(NU // 4):
        lower(g)

    place_rows.wait()
    pl.semaphore_wait(barrier, 38)

    left = lax.broadcasted_iota(jnp.int32, (8, 128), 1) < 64
    sub = lax.broadcasted_iota(jnp.int32, (8, 128), 0)
    shifted = t.at[pl.ds(HALF, LOCAL)]

    def pick(out, k, cq):
        zq = (z + away(k)) % 8

        def body(i, carry):
            q = zq * 16 + i * 2 + cq
            sign = (1 - 2 * parity(row & q)).astype(F32)
            for top in (0, 8):
                v = None
                for j in range(8):
                    a = jnp.broadcast_to(t[pl.ds(idx[q * 32 + top + j], 1), :], (8, 128))
                    b = jnp.broadcast_to(shifted[pl.ds(idx[q * 32 + 16 + top + j], 1), :], (8, 128))
                    r = jnp.where(left, a, b)
                    v = r if v is None else jnp.where(sub == j, r, v)
                out[k, pl.ds(pl.multiple_of(i * 16, 16) + top, 8), :] = v * sign
            return carry

        lax.fori_loop(0, 8, body, 0, unroll=8)

    def remote(src, dst, ss, rs, device):
        return pltpu.make_async_remote_copy(
            src_ref=src, dst_ref=dst, send_sem=ss, recv_sem=rs,
            device_id=device, device_id_type=MESH,
        )

    def all_of(ref, ss, rs):
        return remote(ref, ref, ss, rs, near(0, 0, 1))

    def block(i):
        return pl.ds(pl.multiple_of(i * 32, 32), 32)

    def to_core(k):
        return remote(zo.at[k], rc.at[k], cs, cr.at[k], near(0, 0, 1))

    def to_y(k, d):
        return remote(acc.at[k, block((y + d) % 4)], ry.at[k, d - 1], ys, yr.at[k], near(d, 0, 0))

    def to_z(k):
        return remote(acc.at[k, block(y)], rz.at[k], zs, zr, along_z(away(k)))

    def pick_other(k):
        pick(zo, k, 1 - c)
        to_core(k).start()

    def pick_own(k):
        pick(acc, k, c)
        to_core(k).wait_recv()
        acc[k] = acc[k] + rc[k]
        for d in (2, 1, 3):
            to_y(k, d).start()

    def add_y(k):
        all_of(ry.at[k], ys, yr.at[k]).wait_recv()
        mine = block(y)
        acc[k, mine] = (acc[k, mine] + ry[k, 0]) + (ry[k, 1] + ry[k, 2])

    def pass_z(k):
        add_y(k)
        to_z(k).start()

    loop(0, 8, pick_other)
    loop(0, 8, pick_own)
    loop(0, 7, pass_z)
    add_y(7)
    all_of(rz, zs, zr).wait_recv()
    r = [rz[i] for i in range(7)]
    rx[x] = ((acc[7, block(y)] + r[0]) + (r[1] + r[2])) + ((r[3] + r[4]) + (r[5] + r[6]))

    def to_x(d):
        return remote(rx.at[x], rx.at[x], xs, xr, near(0, d, 0))

    for d in (2, 1, 3):
        to_x(d).start()

    all_of(zo, cs, cr.at[0]).wait_send()
    all_of(ry, ys, yr.at[0]).wait_send()
    all_of(rx.at[pl.ds(0, 3)], xs, xr).wait_recv()
    a0 = rx[0] + rx[1]
    a1 = rx[2] + rx[3]
    first = jnp.concatenate([a0[:, :64], a1[:, :64]], axis=1)
    second = jnp.concatenate([a0[:, 64:], a1[:, 64:]], axis=1)
    m = jnp.concatenate([first, second], axis=0)
    mt[...] = m.T
    g = jnp.dot(
        mt[pl.ds(pl.multiple_of(x * 32, 32), 32), :], m,
        preferred_element_type=F32, precision=lax.Precision.HIGHEST,
    )
    for e in range(8):
        gs[e] = g[4 * e : 4 * e + 4]

    own = y * 2 + c

    def to_gs(i):
        dy, dc = i // 2, i % 2
        e = ((y + dy) % 4) * 2 + (c + dc) % 2
        return remote(gs.at[e], gr.at[i - 1], gss, gsr, near(dy, 0, dc))

    def to_gz(d):
        return remote(gz.at[z], gz.at[z], gzs, gzr, along_z(d))

    place = x * 8 + own

    def to_gf(i):
        return remote(gf.at[place], gf.at[place], gfs, gfr, plane(i))

    loop(1, 8, lambda i: to_gs(i).start())
    ms[0, 0], ms[0, 1] = first[:16], first[16:]
    ms[1, 0], ms[1, 1] = second[:16], second[16:]
    both_out[128:144, :] = ms[0, xl]
    both_out[144:160, :] = ms[1, xl]
    all_of(rz, zs, zr).wait_send()
    all_of(rx.at[pl.ds(0, 3)], xs, xr).wait_send()
    all_of(gr, gss, gsr).wait_recv()
    gz[z] = ((gs[own] + gr[0]) + (gr[1] + gr[2])) + ((gr[3] + gr[4]) + (gr[5] + gr[6]))
    loop(1, 8, lambda d: to_gz(d).start())
    all_of(gr, gss, gsr).wait_send()
    all_of(gz.at[pl.ds(0, 7)], gzs, gzr).wait_recv()
    gf[place] = (((gz[0] + gz[1]) + (gz[2] + gz[3])) + ((gz[4] + gz[5]) + (gz[6] + gz[7]))) * (1.0 / 4096.0)
    loop(0, 31, lambda i: to_gf((i + 19) % 31 + 1).start())
    all_of(gz.at[pl.ds(0, 7)], gzs, gzr).wait_send()
    all_of(gf.at[pl.ds(0, 31)], gfs, gfr).wait_recv()
    for e in range(32):
        both_out[e * 4 : (e + 1) * 4, :] = gf[e]
    all_of(gf.at[pl.ds(0, 31)], gfs, gfr).wait_send()


def mix(panel, signs, rows):
    vm = pl.BlockSpec(memory_space=pltpu.VMEM)
    hbm = pl.BlockSpec(memory_space=pltpu.HBM)
    V = pltpu.VMEM
    D = pltpu.SemaphoreType.DMA
    return pl.pallas_call(
        mix_kernel,
        out_shape=jax.ShapeDtypeStruct((160, 128), F32),
        in_specs=[hbm, hbm, hbm],
        out_specs=vm,
        scratch_shapes=[
            V((64, LOCAL), F32),
            V((LOCAL // 128, 128), jnp.int32),
            V((4096,), jnp.int32),
            pltpu.SMEM((4096,), jnp.int32),
            V((LOCAL + HALF, 128), F32),
            V((8, 128, 128), F32),
            V((8, 128, 128), F32),
            V((8, 128, 128), F32),
            V((8, 3, 32, 128), F32),
            V((7, 32, 128), F32),
            V((4, 32, 128), F32),
            V((2, 2, 16, 128), F32),
            V((128, 64), F32),
            V((8, 4, 128), F32),
            V((7, 4, 128), F32),
            V((8, 4, 128), F32),
            V((32, 4, 128), F32),
            D((11,)),
            D, D((8,)), D, D((8,)), D, D, D, D, D, D, D, D, D, D,
        ],
        compiler_params=pltpu.CompilerParams(
            collective_id=0, has_side_effects=True, vmem_limit_bytes=62 << 20
        ),
        name="mix",
    )(panel, signs.reshape(LOCAL // 128, 128), rows)


def rows_const(v, j):
    return jnp.broadcast_to(v[:, j : j + 1], (8, 128))


def factor_kernel(both_ref, basis_ref, tri_ref, a_ref, u_ref):
    n, width = 128, 32
    col = lax.axis_index("col")
    a_ref[:, :128] = both_ref[:128, :]
    samples = jnp.concatenate([both_ref[128:, :], jnp.zeros((96, 128), F32)], axis=0)
    a_ref[:, 128:] = samples.T
    lane = lax.broadcasted_iota(jnp.int32, (8, 128), 1)
    for panel in range(n // width):
        top = panel * width
        nb = width // 8
        blocks = [
            [a_ref[top + 8 * i : top + 8 * i + 8, 128 * t : 128 * t + 128] for t in range(2)]
            for i in range(nb)
        ]
        for j in range(nb):
            at = top + 8 * j
            rows = [
                [jnp.broadcast_to(blocks[j][t][k : k + 1, :], (8, 128)) for t in range(2)]
                for k in range(8)
            ]
            d = {(i, k): rows_const(rows[i][0], at + k) for i in range(8) for k in range(i + 1)}
            below = [[rows_const(blocks[i][0], at + k) for k in range(8)] for i in range(j + 1, nb)]
            for k in range(8):
                r = lax.rsqrt(d[k, k])
                for i in range(k + 1, 8):
                    d[i, k] = d[i, k] * r
                for i in range(k + 1, 8):
                    for q in range(k + 1, i + 1):
                        d[i, q] = d[i, q] - d[i, k] * d[q, k]
                for t in range(2):
                    rows[k][t] = rows[k][t] * r
                    for q in range(k + 1, 8):
                        rows[q][t] = rows[q][t] - d[q, k] * rows[k][t]
                for b in below:
                    b[k] = b[k] * r
                    for q in range(k + 1, 8):
                        b[q] = b[q] - d[q, k] * b[k]
            for k in range(8):
                keep = lane >= at + k
                u_ref[at + k : at + k + 1, :128] = jnp.where(keep, rows[k][0], 0.0)[:1]
                u_ref[at + k : at + k + 1, 128:] = rows[k][1][:1]
            for i in range(j + 1, nb):
                b = below[i - j - 1]
                for t in range(2):
                    v = blocks[i][t]
                    for k in range(8):
                        v = v - b[k] * rows[k][t]
                    blocks[i][t] = v
        if top + width < n:
            rest = top + width
            u = u_ref[top:rest, :]
            left = u[:, :128].T[rest:, :]
            upd = jnp.dot(left, u, preferred_element_type=F32, precision=lax.Precision.HIGHEST)
            a_ref[rest:, :] = a_ref[rest:, :] - upd
    half = pl.ds(pl.multiple_of(col * 64, 64), 64)
    tri_ref[...] = u_ref[half, :128]
    basis_ref[...] = u_ref[half, 128:].T[:32]


def factor(both):
    vm = pl.BlockSpec(memory_space=pltpu.VMEM)
    return pl.pallas_call(
        factor_kernel,
        out_shape=(jax.ShapeDtypeStruct((32, 64), F32), jax.ShapeDtypeStruct((64, 128), F32)),
        in_specs=[vm],
        out_specs=(vm, vm),
        scratch_shapes=[pltpu.VMEM((128, 256), F32), pltpu.VMEM((128, 256), F32)],
        compiler_params=pltpu.CompilerParams(vmem_limit_bytes=16 << 20),
        name="factor",
    )(both)


def shards(tall_panel_array, row_signs, sample_rows):
    basis, upper = factor(mix(tall_panel_array, row_signs, sample_rows))
    return basis.T, upper


def solution(mesh):
    return jax.shard_map(
        shards,
        mesh=mesh,
        in_specs=(P("col", "row"), P("row"), P()),
        out_specs=(P("col", "row"), P("col", None)),
        check_vma=False,
    )
```

```python
import jax
import jax.numpy as jnp
from jax import lax
from jax.experimental import pallas as pl
from jax.experimental.pallas import tpu as pltpu
from jax.sharding import PartitionSpec as P

F32 = jnp.float32
BF16 = jnp.bfloat16
MESH = pl.DeviceIdType.MESH
LO = 256
NU = 32
LOCAL = LO * NU
HALF = LOCAL // 2


def parity(bits):
    bits = bits ^ (bits >> 4)
    bits = bits ^ (bits >> 2)
    bits = bits ^ (bits >> 1)
    return bits & 1


def away(k):
    b = (k + 6) % 8
    return 4 + (b // 2) * (1 - 2 * (b % 2)) - b % 2 + b // 7 - k // 7


def mix_kernel(
    x_hbm, sg_hbm, idx_hbm, both_out,
    xv, sgv, idxv, idx, t, zo, acc, rc, rf, ry, rz, rx, ms, mt, gs, gr, gz, gf,
    in_sem, cs, cr, fs, fr, ys, yr, zs, zr, xs, xr, gss, gsr, gzs, gzr, gfs, gfr,
):
    row, col = lax.axis_index("row"), lax.axis_index("col")
    c = row % 2
    xl = (row // 2) % 2
    y = (row // 4) % 4
    z = row // 16
    x = col * 2 + xl

    def dev(z_, y_, x_, c_):
        return {"row": z_ * 16 + y_ * 4 + (x_ % 2) * 2 + c_, "col": x_ // 2}

    def near(dy, dx, dc):
        return dev(z, (y + dy) % 4, (x + dx) % 4, (c + dc) % 2)

    def plane(i):
        return near(i // 8, (i // 2) % 4, i % 2)

    def along_z(d):
        return dev((z + d) % 8, y, x, c)

    def loop(first, last, body):
        def step(i, carry):
            body(i)
            return carry

        lax.fori_loop(first, last, step, 0)

    fetch_rows = pltpu.make_async_copy(idx_hbm, idxv, in_sem.at[8])
    fetch_signs = pltpu.make_async_copy(sg_hbm, sgv, in_sem.at[9])
    place_rows = pltpu.make_async_copy(idxv, idx, in_sem.at[10])

    def fetch(i):
        at = pl.ds(pl.multiple_of(i * 8, 8), 8)
        return pltpu.make_async_copy(x_hbm.at[at], xv.at[at], in_sem.at[i])

    fetch_rows.start()
    fetch_signs.start()
    loop(0, 8, lambda i: fetch(i).start())

    barrier = pltpu.get_barrier_semaphore()
    loop(1, 32, lambda i: pl.semaphore_signal(barrier, inc=1, device_id=plane(i), device_id_type=MESH))
    loop(1, 8, lambda d: pl.semaphore_signal(barrier, inc=1, device_id=along_z(d), device_id_type=MESH))

    ri = lax.broadcasted_iota(jnp.int32, (LO, LO), 0)
    ci = lax.broadcasted_iota(jnp.int32, (LO, LO), 1)
    h = ((1 - 2 * parity(ri & ci)).astype(F32) * (1.0 / 1024.0)).astype(BF16)
    h = jnp.concatenate([h, h, h], axis=1)
    fetch_rows.wait()
    idxv[...] = idxv[...] & (LOCAL - 1)
    place_rows.start()
    fetch_signs.wait()

    def butterfly(i):
        fetch(i).wait()
        rows = pl.ds(pl.multiple_of(i * 8, 8), 8)
        for bt in range(LO // 128):
            v = []
            for u in range(NU):
                at = u * LO + bt * 128
                v.append(xv[rows, at : at + 128] * sgv[at // 128 : at // 128 + 1, :].astype(F32))
            step = 1
            while step < NU:
                for u in range(NU):
                    if not u & step:
                        v[u], v[u + step] = v[u] + v[u + step], v[u] - v[u + step]
                step *= 2
            for u in range(NU):
                at = u * LO + bt * 128
                xv[rows, at : at + 128] = v[u]

    loop(0, 8, butterfly)

    def lower(g):
        parts = []
        for i in range(2):
            for top in (0, NU // 2):
                at = (2 * g + i + top) * LO
                v = xv[:, at : at + LO]
                hi = v.astype(BF16)
                rest = v - hi.astype(F32)
                mid = rest.astype(BF16)
                low = (rest - mid.astype(F32)).astype(BF16)
                parts.append(jnp.concatenate([hi, mid, low], axis=1))
        w = jnp.concatenate(parts, axis=0)
        o = lax.dot_general(h, w, (((1,), (1,)), ((), ())), preferred_element_type=F32)
        for i in range(2):
            part = o[:, 128 * i : 128 * i + 128]
            at = (2 * g + i) * LO
            t[at : at + LO, :] = part
            t[at + LOCAL : at + LOCAL + LO, :] = part
            t[at + HALF : at + HALF + LO, :] = pltpu.roll(part, 64, 1)

    for g in range(NU // 4):
        lower(g)

    place_rows.wait()
    pl.semaphore_wait(barrier, 38)

    left = lax.broadcasted_iota(jnp.int32, (8, 128), 1) < 64
    sub = lax.broadcasted_iota(jnp.int32, (8, 128), 0)
    shifted = t.at[pl.ds(HALF, LOCAL)]

    def pick(out, k, cq):
        zq = (z + away(k)) % 8

        def body(i, carry):
            q = zq * 16 + i * 2 + cq
            sign = (1 - 2 * parity(row & q)).astype(F32)
            for top in (0, 8):
                v = None
                for j in range(8):
                    a = jnp.broadcast_to(t[pl.ds(idx[q * 32 + top + j], 1), :], (8, 128))
                    b = jnp.broadcast_to(shifted[pl.ds(idx[q * 32 + 16 + top + j], 1), :], (8, 128))
                    r = jnp.where(left, a, b)
                    v = r if v is None else jnp.where(sub == j, r, v)
                out[k, pl.ds(pl.multiple_of(i * 16, 16) + top, 8), :] = v * sign
            return carry

        lax.fori_loop(0, 8, body, 0, unroll=8)

    def remote(src, dst, ss, rs, device):
        return pltpu.make_async_remote_copy(
            src_ref=src, dst_ref=dst, send_sem=ss, recv_sem=rs,
            device_id=device, device_id_type=MESH,
        )

    def all_of(ref, ss, rs):
        return remote(ref, ref, ss, rs, near(0, 0, 1))

    def block(i):
        return pl.ds(pl.multiple_of(i * 32, 32), 32)

    def to_core(k):
        return remote(zo.at[k], rc.at[k], cs, cr.at[k], near(0, 0, 1))

    def to_y(k, d):
        return remote(acc.at[k, block((y + d) % 4)], ry.at[k - 2, d - 1], ys, yr.at[k - 2], near(d, 0, 0))

    def to_z(k):
        return remote(acc.at[k, block(y)], rz.at[k - 2], zs, zr, along_z(away(k)))

    def to_first(k):
        return remote(acc.at[k], rf.at[k], fs, fr, along_z(away(k)))

    def pick_other(k):
        pick(zo, k, 1 - c)
        to_core(k).start()

    def send_y(k):
        for d in (2, 1, 3):
            to_y(k, d).start()

    def pick_own(k):
        pick(acc, k, c)
        to_core(k).wait_recv()
        acc[k] = acc[k] + rc[k]
        pl.when(k < 2)(lambda: to_first(k).start())
        pl.when(k % 7 >= 2)(lambda: send_y(k))

    def add_y(k):
        all_of(ry.at[k - 2], ys, yr.at[k - 2]).wait_recv()
        mine = block(y)
        acc[k, mine] = (acc[k, mine] + ry[k - 2, 0]) + (ry[k - 2, 1] + ry[k - 2, 2])

    def pass_z(k):
        add_y(k)
        to_z(k).start()

    loop(0, 8, pick_other)
    loop(0, 8, pick_own)
    all_of(rf, fs, fr).wait_recv()
    acc[7] = acc[7] + (rf[0] + rf[1])
    send_y(7)
    loop(2, 7, pass_z)
    add_y(7)
    all_of(rz, zs, zr).wait_recv()
    rx[x] = (acc[7, block(y)] + rz[0]) + ((rz[1] + rz[2]) + (rz[3] + rz[4]))

    def to_x(d):
        return remote(rx.at[x], rx.at[x], xs, xr, near(0, d, 0))

    for d in (2, 1, 3):
        to_x(d).start()

    all_of(zo, cs, cr.at[0]).wait_send()
    all_of(rf, fs, fr).wait_send()
    all_of(ry, ys, yr.at[0]).wait_send()
    all_of(rx.at[pl.ds(0, 3)], xs, xr).wait_recv()
    a0 = rx[0] + rx[1]
    a1 = rx[2] + rx[3]
    first = jnp.concatenate([a0[:, :64], a1[:, :64]], axis=1)
    second = jnp.concatenate([a0[:, 64:], a1[:, 64:]], axis=1)
    m = jnp.concatenate([first, second], axis=0)
    mt[...] = m.T
    g = jnp.dot(
        mt[pl.ds(pl.multiple_of(x * 32, 32), 32), :], m,
        preferred_element_type=F32, precision=lax.Precision.HIGHEST,
    )
    for e in range(8):
        gs[e] = g[4 * e : 4 * e + 4]

    own = y * 2 + c

    def to_gs(i):
        dy, dc = i // 2, i % 2
        e = ((y + dy) % 4) * 2 + (c + dc) % 2
        return remote(gs.at[e], gr.at[i - 1], gss, gsr, near(dy, 0, dc))

    def to_gz(d):
        return remote(gz.at[z], gz.at[z], gzs, gzr, along_z(d))

    place = x * 8 + own

    def to_gf(i):
        return remote(gf.at[place], gf.at[place], gfs, gfr, plane(i))

    loop(1, 8, lambda i: to_gs(i).start())
    ms[0, 0], ms[0, 1] = first[:16], first[16:]
    ms[1, 0], ms[1, 1] = second[:16], second[16:]
    both_out[128:144, :] = ms[0, xl]
    both_out[144:160, :] = ms[1, xl]
    all_of(rz, zs, zr).wait_send()
    all_of(rx.at[pl.ds(0, 3)], xs, xr).wait_send()
    all_of(gr, gss, gsr).wait_recv()
    gz[z] = ((gs[own] + gr[0]) + (gr[1] + gr[2])) + ((gr[3] + gr[4]) + (gr[5] + gr[6]))
    loop(1, 8, lambda d: to_gz(d).start())
    all_of(gr, gss, gsr).wait_send()
    all_of(gz.at[pl.ds(0, 7)], gzs, gzr).wait_recv()
    gf[place] = (((gz[0] + gz[1]) + (gz[2] + gz[3])) + ((gz[4] + gz[5]) + (gz[6] + gz[7]))) * (1.0 / 4096.0)
    loop(0, 31, lambda i: to_gf((i + 19) % 31 + 1).start())
    all_of(gz.at[pl.ds(0, 7)], gzs, gzr).wait_send()
    all_of(gf.at[pl.ds(0, 31)], gfs, gfr).wait_recv()
    for e in range(32):
        both_out[e * 4 : (e + 1) * 4, :] = gf[e]
    all_of(gf.at[pl.ds(0, 31)], gfs, gfr).wait_send()


def mix(panel, signs, rows):
    vm = pl.BlockSpec(memory_space=pltpu.VMEM)
    hbm = pl.BlockSpec(memory_space=pltpu.HBM)
    V = pltpu.VMEM
    D = pltpu.SemaphoreType.DMA
    return pl.pallas_call(
        mix_kernel,
        out_shape=jax.ShapeDtypeStruct((160, 128), F32),
        in_specs=[hbm, hbm, hbm],
        out_specs=vm,
        scratch_shapes=[
            V((64, LOCAL), F32),
            V((LOCAL // 128, 128), jnp.int32),
            V((4096,), jnp.int32),
            pltpu.SMEM((4096,), jnp.int32),
            V((LOCAL + HALF, 128), F32),
            V((8, 128, 128), F32),
            V((8, 128, 128), F32),
            V((8, 128, 128), F32),
            V((2, 128, 128), F32),
            V((6, 3, 32, 128), F32),
            V((5, 32, 128), F32),
            V((4, 32, 128), F32),
            V((2, 2, 16, 128), F32),
            V((128, 64), F32),
            V((8, 4, 128), F32),
            V((7, 4, 128), F32),
            V((8, 4, 128), F32),
            V((32, 4, 128), F32),
            D((11,)),
            D, D((8,)), D, D, D, D((6,)), D, D, D, D, D, D, D, D, D, D,
        ],
        compiler_params=pltpu.CompilerParams(
            collective_id=0, has_side_effects=True, vmem_limit_bytes=62 << 20
        ),
        name="mix",
    )(panel, signs.reshape(LOCAL // 128, 128), rows)


def rows_const(v, j):
    return jnp.broadcast_to(v[:, j : j + 1], (8, 128))


def factor_kernel(both_ref, basis_ref, tri_ref, a_ref, u_ref):
    n, width = 128, 32
    col = lax.axis_index("col")
    a_ref[:, :128] = both_ref[:128, :]
    samples = jnp.concatenate([both_ref[128:, :], jnp.zeros((96, 128), F32)], axis=0)
    a_ref[:, 128:] = samples.T
    lane = lax.broadcasted_iota(jnp.int32, (8, 128), 1)
    for panel in range(n // width):
        top = panel * width
        nb = width // 8
        blocks = [
            [a_ref[top + 8 * i : top + 8 * i + 8, 128 * t : 128 * t + 128] for t in range(2)]
            for i in range(nb)
        ]
        for j in range(nb):
            at = top + 8 * j
            rows = [
                [jnp.broadcast_to(blocks[j][t][k : k + 1, :], (8, 128)) for t in range(2)]
                for k in range(8)
            ]
            d = {(i, k): rows_const(rows[i][0], at + k) for i in range(8) for k in range(i + 1)}
            below = [[rows_const(blocks[i][0], at + k) for k in range(8)] for i in range(j + 1, nb)]
            for k in range(8):
                r = lax.rsqrt(d[k, k])
                for i in range(k + 1, 8):
                    d[i, k] = d[i, k] * r
                for i in range(k + 1, 8):
                    for q in range(k + 1, i + 1):
                        d[i, q] = d[i, q] - d[i, k] * d[q, k]
                for t in range(2):
                    rows[k][t] = rows[k][t] * r
                    for q in range(k + 1, 8):
                        rows[q][t] = rows[q][t] - d[q, k] * rows[k][t]
                for b in below:
                    b[k] = b[k] * r
                    for q in range(k + 1, 8):
                        b[q] = b[q] - d[q, k] * b[k]
            for k in range(8):
                keep = lane >= at + k
                u_ref[at + k : at + k + 1, :128] = jnp.where(keep, rows[k][0], 0.0)[:1]
                u_ref[at + k : at + k + 1, 128:] = rows[k][1][:1]
            for i in range(j + 1, nb):
                b = below[i - j - 1]
                for t in range(2):
                    v = blocks[i][t]
                    for k in range(8):
                        v = v - b[k] * rows[k][t]
                    blocks[i][t] = v
        if top + width < n:
            rest = top + width
            u = u_ref[top:rest, :]
            left = u[:, :128].T[rest:, :]
            upd = jnp.dot(left, u, preferred_element_type=F32, precision=lax.Precision.HIGHEST)
            a_ref[rest:, :] = a_ref[rest:, :] - upd
    half = pl.ds(pl.multiple_of(col * 64, 64), 64)
    tri_ref[...] = u_ref[half, :128]
    basis_ref[...] = u_ref[half, 128:].T[:32]


def factor(both):
    vm = pl.BlockSpec(memory_space=pltpu.VMEM)
    return pl.pallas_call(
        factor_kernel,
        out_shape=(jax.ShapeDtypeStruct((32, 64), F32), jax.ShapeDtypeStruct((64, 128), F32)),
        in_specs=[vm],
        out_specs=(vm, vm),
        scratch_shapes=[pltpu.VMEM((128, 256), F32), pltpu.VMEM((128, 256), F32)],
        compiler_params=pltpu.CompilerParams(vmem_limit_bytes=16 << 20),
        name="factor",
    )(both)


def shards(tall_panel_array, row_signs, sample_rows):
    basis, upper = factor(mix(tall_panel_array, row_signs, sample_rows))
    return basis.T, upper


def solution(mesh):
    return jax.shard_map(
        shards,
        mesh=mesh,
        in_specs=(P("col", "row"), P("row"), P()),
        out_specs=(P("col", "row"), P("col", None)),
        check_vma=False,
    )
```

```python
import jax
import jax.numpy as jnp
from jax import lax
from jax.experimental import pallas as pl
from jax.experimental.pallas import tpu as pltpu
from jax.sharding import PartitionSpec as P

F32 = jnp.float32
BF16 = jnp.bfloat16
MESH = pl.DeviceIdType.MESH
LO = 256
NU = 32
LOCAL = LO * NU
HALF = LOCAL // 2


def parity(bits):
    bits = bits ^ (bits >> 4)
    bits = bits ^ (bits >> 2)
    bits = bits ^ (bits >> 1)
    return bits & 1


def away(k):
    b = (k + 6) % 8
    return 4 + (b // 2) * (1 - 2 * (b % 2)) - b % 2 + b // 7 - k // 7


def mix_kernel(
    x_hbm, sg_hbm, idx_hbm, both_out,
    xv, sgv, idxv, idx, t, zo, acc, rc, rf, ry, rz, mx, gs, gr, gz, gf,
    in_sem, cs, cr, fs, fr, ys, yr, zs, zr, xs, xr, gss, gsr, gzs, gzr, gfs, gfr,
):
    row, col = lax.axis_index("row"), lax.axis_index("col")
    c = row % 2
    xl = (row // 2) % 2
    y = (row // 4) % 4
    z = row // 16
    x = col * 2 + xl

    def dev(z_, y_, x_, c_):
        return {"row": z_ * 16 + y_ * 4 + (x_ % 2) * 2 + c_, "col": x_ // 2}

    def near(dy, dx, dc):
        return dev(z, (y + dy) % 4, (x + dx) % 4, (c + dc) % 2)

    def plane(i):
        return near(i // 8, (i // 2) % 4, i % 2)

    def along_z(d):
        return dev((z + d) % 8, y, x, c)

    def loop(first, last, body):
        def step(i, carry):
            body(i)
            return carry

        lax.fori_loop(first, last, step, 0)

    fetch_rows = pltpu.make_async_copy(idx_hbm, idxv, in_sem.at[8])
    fetch_signs = pltpu.make_async_copy(sg_hbm, sgv, in_sem.at[9])
    place_rows = pltpu.make_async_copy(idxv, idx, in_sem.at[10])

    def fetch(i):
        at = pl.ds(pl.multiple_of(i * 8, 8), 8)
        return pltpu.make_async_copy(x_hbm.at[at], xv.at[at], in_sem.at[i])

    fetch_rows.start()
    fetch_signs.start()
    loop(0, 8, lambda i: fetch(i).start())

    barrier = pltpu.get_barrier_semaphore()
    loop(1, 32, lambda i: pl.semaphore_signal(barrier, inc=1, device_id=plane(i), device_id_type=MESH))
    loop(1, 8, lambda d: pl.semaphore_signal(barrier, inc=1, device_id=along_z(d), device_id_type=MESH))

    def greet_line(i):
        d = dev((z + 2 + i // 3) % 8, y, (x + 1 + i % 3) % 4, c)
        pl.semaphore_signal(barrier, inc=1, device_id=d, device_id_type=MESH)

    loop(0, 15, greet_line)

    ri = lax.broadcasted_iota(jnp.int32, (LO, LO), 0)
    ci = lax.broadcasted_iota(jnp.int32, (LO, LO), 1)
    h = ((1 - 2 * parity(ri & ci)).astype(F32) * (1.0 / 1024.0)).astype(BF16)
    h = jnp.concatenate([h, h, h], axis=1)
    fetch_rows.wait()
    idxv[...] = idxv[...] & (LOCAL - 1)
    place_rows.start()
    fetch_signs.wait()

    def butterfly(i):
        fetch(i).wait()
        rows = pl.ds(pl.multiple_of(i * 8, 8), 8)
        for bt in range(LO // 128):
            v = []
            for u in range(NU):
                at = u * LO + bt * 128
                v.append(xv[rows, at : at + 128] * sgv[at // 128 : at // 128 + 1, :].astype(F32))
            step = 1
            while step < NU:
                for u in range(NU):
                    if not u & step:
                        v[u], v[u + step] = v[u] + v[u + step], v[u] - v[u + step]
                step *= 2
            for u in range(NU):
                at = u * LO + bt * 128
                xv[rows, at : at + 128] = v[u]

    loop(0, 8, butterfly)

    def lower(g):
        parts = []
        for i in range(2):
            for top in (0, NU // 2):
                at = (2 * g + i + top) * LO
                v = xv[:, at : at + LO]
                hi = v.astype(BF16)
                rest = v - hi.astype(F32)
                mid = rest.astype(BF16)
                low = (rest - mid.astype(F32)).astype(BF16)
                parts.append(jnp.concatenate([hi, mid, low], axis=1))
        w = jnp.concatenate(parts, axis=0)
        o = lax.dot_general(h, w, (((1,), (1,)), ((), ())), preferred_element_type=F32)
        for i in range(2):
            part = o[:, 128 * i : 128 * i + 128]
            at = (2 * g + i) * LO
            t[at : at + LO, :] = part
            t[at + LOCAL : at + LOCAL + LO, :] = part
            t[at + HALF : at + HALF + LO, :] = pltpu.roll(part, 64, 1)

    for g in range(NU // 4):
        lower(g)

    place_rows.wait()
    pl.semaphore_wait(barrier, 53)

    left = lax.broadcasted_iota(jnp.int32, (8, 128), 1) < 64
    sub = lax.broadcasted_iota(jnp.int32, (8, 128), 0)
    shifted = t.at[pl.ds(HALF, LOCAL)]

    def pick(out, k, cq):
        zq = (z + away(k)) % 8

        def body(i, carry):
            q = zq * 16 + i * 2 + cq
            sign = (1 - 2 * parity(row & q)).astype(F32)
            for top in (0, 8):
                v = None
                for j in range(8):
                    a = jnp.broadcast_to(t[pl.ds(idx[q * 32 + top + j], 1), :], (8, 128))
                    b = jnp.broadcast_to(shifted[pl.ds(idx[q * 32 + 16 + top + j], 1), :], (8, 128))
                    r = jnp.where(left, a, b)
                    v = r if v is None else jnp.where(sub == j, r, v)
                out[k, pl.ds(pl.multiple_of(i * 16, 16) + top, 8), :] = v * sign
            return carry

        lax.fori_loop(0, 8, body, 0, unroll=8)

    def remote(src, dst, ss, rs, device):
        return pltpu.make_async_remote_copy(
            src_ref=src, dst_ref=dst, send_sem=ss, recv_sem=rs,
            device_id=device, device_id_type=MESH,
        )

    def all_of(ref, ss, rs):
        return remote(ref, ref, ss, rs, near(0, 0, 1))

    def block(i):
        return pl.ds(pl.multiple_of(i * 32, 32), 32)

    def to_core(k):
        return remote(zo.at[k], rc.at[k], cs, cr.at[k], near(0, 0, 1))

    def to_y(k, d):
        return remote(acc.at[k, block((y + d) % 4)], ry.at[k - 2, d - 1], ys, yr.at[k - 2], near(d, 0, 0))

    def quarter(k, i):
        return acc.at[k, pl.ds(pl.multiple_of(y * 32 + (i % 2) * 16 + (i // 2) * 8, 8), 8)]

    def to_z(k, i):
        return remote(quarter(k, i), rz.at[(k - 2) * 4 + x], zs, zr, dev((z + away(k)) % 8, y, i, c))

    def to_first(k):
        return remote(acc.at[k], rf.at[k], fs, fr, along_z(away(k)))

    def pick_other(k):
        pick(zo, k, 1 - c)
        to_core(k).start()

    def send_y(k):
        for d in (2, 1, 3):
            to_y(k, d).start()

    def pick_own(k):
        pick(acc, k, c)
        to_core(k).wait_recv()
        acc[k] = acc[k] + rc[k]
        pl.when(k < 2)(lambda: to_first(k).start())
        pl.when(k % 7 >= 2)(lambda: send_y(k))

    def add_y(k):
        all_of(ry.at[k - 2], ys, yr.at[k - 2]).wait_recv()
        mine = block(y)
        acc[k, mine] = (acc[k, mine] + ry[k - 2, 0]) + (ry[k - 2, 1] + ry[k - 2, 2])

    def pass_z(k):
        add_y(k)
        for i in range(4):
            to_z(k, i).start()

    loop(0, 8, pick_other)
    loop(0, 8, pick_own)
    all_of(rf, fs, fr).wait_recv()
    acc[7] = acc[7] + (rf[0] + rf[1])
    send_y(7)
    loop(2, 7, pass_z)
    add_y(7)
    for d in (2, 1, 3):
        to_z(7, (x + d) % 4).start()
    rz[20 + x] = quarter(7, x)[...]
    all_of(zo, cs, cr.at[0]).wait_send()
    all_of(rf, fs, fr).wait_send()
    all_of(ry, ys, yr.at[0]).wait_send()
    others = all_of(rz.at[pl.ds(0, 23)], zs, zr)
    others.wait_recv()

    def total(i):
        v = [rz[4 * k + i] for k in range(6)] + [rz[4 * k + i + 1] for k in range(6)]
        while len(v) > 1:
            v = [v[j] + v[j + 1] if j + 1 < len(v) else v[j] for j in range(0, len(v), 2)]
        return v[0]

    a0, a1 = total(0), total(2)
    first = jnp.concatenate([a0[:, :64], a1[:, :64]], axis=1)
    second = jnp.concatenate([a0[:, 64:], a1[:, 64:]], axis=1)
    m = jnp.concatenate([first, second], axis=0)
    g = jnp.dot(m.T, m, preferred_element_type=F32, precision=lax.Precision.HIGHEST)
    for e in range(32):
        gs[e] = g[4 * e : 4 * e + 4]

    place = x * 8 + y * 2 + c

    def to_gs(i):
        e = ((x + (i // 2) % 4) % 4) * 8 + ((y + i // 8) % 4) * 2 + (c + i % 2) % 2
        return remote(gs.at[e], gr.at[i - 1], gss, gsr, plane(i))

    to_mate = remote(mx.at[x // 2], mx.at[x // 2], xs, xr, near(0, 2, 0))

    def to_gz(d):
        return remote(gz.at[z], gz.at[z], gzs, gzr, along_z(d))

    def to_gf(i):
        return remote(gf.at[place], gf.at[place], gfs, gfr, plane(i))

    loop(0, 31, lambda i: to_gs((i + 19) % 31 + 1).start())
    mx[x // 2] = m
    to_mate.start()
    others.wait_send()
    all_of(gr, gss, gsr).wait_recv()
    v = [gr[i] for i in range(31)] + [gs[place]]
    while len(v) > 1:
        v = [v[j] + v[j + 1] for j in range(0, len(v), 2)]
    gz[z] = v[0]
    loop(1, 8, lambda d: to_gz(d).start())
    all_of(gr, gss, gsr).wait_send()
    to_mate.wait()
    for i in range(2):
        for j in range(2):
            both_out[128 + 16 * j + 8 * i : 136 + 16 * j + 8 * i, :] = mx[i, 8 * j : 8 * j + 8]
    all_of(gz.at[pl.ds(0, 7)], gzs, gzr).wait_recv()
    gf[place] = (((gz[0] + gz[1]) + (gz[2] + gz[3])) + ((gz[4] + gz[5]) + (gz[6] + gz[7]))) * (1.0 / 4096.0)
    loop(0, 31, lambda i: to_gf((i + 19) % 31 + 1).start())
    all_of(gz.at[pl.ds(0, 7)], gzs, gzr).wait_send()
    all_of(gf.at[pl.ds(0, 31)], gfs, gfr).wait_recv()
    for e in range(32):
        both_out[e * 4 : (e + 1) * 4, :] = gf[e]
    all_of(gf.at[pl.ds(0, 31)], gfs, gfr).wait_send()


def mix(panel, signs, rows):
    vm = pl.BlockSpec(memory_space=pltpu.VMEM)
    hbm = pl.BlockSpec(memory_space=pltpu.HBM)
    V = pltpu.VMEM
    D = pltpu.SemaphoreType.DMA
    return pl.pallas_call(
        mix_kernel,
        out_shape=jax.ShapeDtypeStruct((160, 128), F32),
        in_specs=[hbm, hbm, hbm],
        out_specs=vm,
        scratch_shapes=[
            V((64, LOCAL), F32),
            V((LOCAL // 128, 128), jnp.int32),
            V((4096,), jnp.int32),
            pltpu.SMEM((4096,), jnp.int32),
            V((LOCAL + HALF, 128), F32),
            V((8, 128, 128), F32),
            V((8, 128, 128), F32),
            V((8, 128, 128), F32),
            V((2, 128, 128), F32),
            V((6, 3, 32, 128), F32),
            V((24, 8, 128), F32),
            V((2, 16, 128), F32),
            V((32, 4, 128), F32),
            V((31, 4, 128), F32),
            V((8, 4, 128), F32),
            V((32, 4, 128), F32),
            D((11,)),
            D, D((8,)), D, D, D, D((6,)), D, D, D, D, D, D, D, D, D, D,
        ],
        compiler_params=pltpu.CompilerParams(
            collective_id=0, has_side_effects=True, vmem_limit_bytes=62 << 20
        ),
        name="mix",
    )(panel, signs.reshape(LOCAL // 128, 128), rows)


def rows_const(v, j):
    return jnp.broadcast_to(v[:, j : j + 1], (8, 128))


def factor_kernel(both_ref, basis_ref, tri_ref, a_ref, u_ref):
    n, width = 128, 32
    col = lax.axis_index("col")
    a_ref[:, :128] = both_ref[:128, :]
    samples = jnp.concatenate([both_ref[128:, :], jnp.zeros((96, 128), F32)], axis=0)
    a_ref[:, 128:] = samples.T
    lane = lax.broadcasted_iota(jnp.int32, (8, 128), 1)
    for panel in range(n // width):
        top = panel * width
        nb = width // 8
        blocks = [
            [a_ref[top + 8 * i : top + 8 * i + 8, 128 * t : 128 * t + 128] for t in range(2)]
            for i in range(nb)
        ]
        for j in range(nb):
            at = top + 8 * j
            rows = [
                [jnp.broadcast_to(blocks[j][t][k : k + 1, :], (8, 128)) for t in range(2)]
                for k in range(8)
            ]
            d = {(i, k): rows_const(rows[i][0], at + k) for i in range(8) for k in range(i + 1)}
            below = [[rows_const(blocks[i][0], at + k) for k in range(8)] for i in range(j + 1, nb)]
            for k in range(8):
                r = lax.rsqrt(d[k, k])
                for i in range(k + 1, 8):
                    d[i, k] = d[i, k] * r
                for i in range(k + 1, 8):
                    for q in range(k + 1, i + 1):
                        d[i, q] = d[i, q] - d[i, k] * d[q, k]
                for t in range(2):
                    rows[k][t] = rows[k][t] * r
                    for q in range(k + 1, 8):
                        rows[q][t] = rows[q][t] - d[q, k] * rows[k][t]
                for b in below:
                    b[k] = b[k] * r
                    for q in range(k + 1, 8):
                        b[q] = b[q] - d[q, k] * b[k]
            for k in range(8):
                keep = lane >= at + k
                u_ref[at + k : at + k + 1, :128] = jnp.where(keep, rows[k][0], 0.0)[:1]
                u_ref[at + k : at + k + 1, 128:] = rows[k][1][:1]
            for i in range(j + 1, nb):
                b = below[i - j - 1]
                for t in range(2):
                    v = blocks[i][t]
                    for k in range(8):
                        v = v - b[k] * rows[k][t]
                    blocks[i][t] = v
        if top + width < n:
            rest = top + width
            u = u_ref[top:rest, :]
            left = u[:, :128].T[rest:, :]
            upd = jnp.dot(left, u, preferred_element_type=F32, precision=lax.Precision.HIGHEST)
            a_ref[rest:, :] = a_ref[rest:, :] - upd
    half = pl.ds(pl.multiple_of(col * 64, 64), 64)
    tri_ref[...] = u_ref[half, :128]
    basis_ref[...] = u_ref[half, 128:].T[:32]


def factor(both):
    vm = pl.BlockSpec(memory_space=pltpu.VMEM)
    return pl.pallas_call(
        factor_kernel,
        out_shape=(jax.ShapeDtypeStruct((32, 64), F32), jax.ShapeDtypeStruct((64, 128), F32)),
        in_specs=[vm],
        out_specs=(vm, vm),
        scratch_shapes=[pltpu.VMEM((128, 256), F32), pltpu.VMEM((128, 256), F32)],
        compiler_params=pltpu.CompilerParams(vmem_limit_bytes=16 << 20),
        name="factor",
    )(both)


def shards(tall_panel_array, row_signs, sample_rows):
    basis, upper = factor(mix(tall_panel_array, row_signs, sample_rows))
    return basis.T, upper


def solution(mesh):
    return jax.shard_map(
        shards,
        mesh=mesh,
        in_specs=(P("col", "row"), P("row"), P()),
        out_specs=(P("col", "row"), P("col", None)),
        check_vma=False,
    )
```

```python
import jax
import jax.numpy as jnp
from jax import lax
from jax.experimental import pallas as pl
from jax.experimental.pallas import tpu as pltpu
from jax.sharding import PartitionSpec as P

F32 = jnp.float32
BF16 = jnp.bfloat16
MESH = pl.DeviceIdType.MESH
LO = 256
NU = 32
LOCAL = LO * NU
HALF = LOCAL // 2


def parity(bits):
    bits = bits ^ (bits >> 4)
    bits = bits ^ (bits >> 2)
    bits = bits ^ (bits >> 1)
    return bits & 1


def away(k):
    b = (k + 6) % 8
    return 4 + (b // 2) * (1 - 2 * (b % 2)) - b % 2 + b // 7 - k // 7


def mix_kernel(
    x_hbm, sg_hbm, idx_hbm, both_out,
    xv, sgv, idxv, idx, t, zo, acc, rc, rf, ry, rz, rx, ms, mt, gs, gr, gz, gf,
    in_sem, cs, cr, fs, fr, ys, yr, zs, zr, xs, xr, gss, gsr, gzs, gzr, gfs, gfr,
):
    row, col = lax.axis_index("row"), lax.axis_index("col")
    c = row & 1
    xl = (row >> 1) & 1
    y = (row >> 2) & 3
    z = row >> 4
    x = col * 2 + xl

    y_at = [((y + d) & 3) * 4 for d in range(4)]
    x_at = [(((x + d) & 1) * 2, ((x + d) & 3) >> 1) for d in range(4)]
    c_at = [c, 1 - c]
    z_at = [((z + d) & 7) * 16 for d in range(8)]

    def near(dy, dx, dc, dz=0):
        return {"row": z_at[dz] + y_at[dy] + x_at[dx][0] + c_at[dc], "col": x_at[dx][1]}

    def along_z(d):
        return {"row": ((z + d) & 7) * 16 + (row & 15), "col": col}

    plane = [(dy, dx, dc) for dy in (2, 1, 3, 0) for dx in (2, 1, 3, 0) for dc in (1, 0) if dy or dx or dc]
    part = [(dy, 0, dc) for dy in (2, 1, 3, 0) for dc in (1, 0) if dy or dc]
    z_order = (4, 3, 5, 2, 6, 1, 7)

    def loop(first, last, body):
        def step(i, carry):
            body(i)
            return carry

        lax.fori_loop(first, last, step, 0)

    fetch_rows = pltpu.make_async_copy(idx_hbm, idxv, in_sem.at[8])
    fetch_signs = pltpu.make_async_copy(sg_hbm, sgv, in_sem.at[9])
    place_rows = pltpu.make_async_copy(idxv, idx, in_sem.at[10])

    def fetch(i):
        at = pl.ds(pl.multiple_of(i * 8, 8), 8)
        return pltpu.make_async_copy(x_hbm.at[at], xv.at[at], in_sem.at[i])

    fetch_rows.start()
    fetch_signs.start()
    loop(0, 8, lambda i: fetch(i).start())

    barrier = pltpu.get_barrier_semaphore()
    for d in [near(*i) for i in plane] + [near(0, 0, 0, d) for d in z_order]:
        pl.semaphore_signal(barrier, inc=1, device_id=d, device_id_type=MESH)

    ri = lax.broadcasted_iota(jnp.int32, (LO, LO), 0)
    ci = lax.broadcasted_iota(jnp.int32, (LO, LO), 1)
    h = ((1 - 2 * parity(ri & ci)).astype(F32) * (1.0 / 1024.0)).astype(BF16)
    h = jnp.concatenate([h, h, h], axis=1)
    fetch_rows.wait()
    idxv[...] = idxv[...] & (LOCAL - 1)
    place_rows.start()
    fetch_signs.wait()

    def butterfly(i):
        fetch(i).wait()
        rows = pl.ds(pl.multiple_of(i * 8, 8), 8)
        for bt in range(LO // 128):
            v = []
            for u in range(NU):
                at = u * LO + bt * 128
                v.append(xv[rows, at : at + 128] * sgv[at // 128 : at // 128 + 1, :].astype(F32))
            step = 1
            while step < NU:
                for u in range(NU):
                    if not u & step:
                        v[u], v[u + step] = v[u] + v[u + step], v[u] - v[u + step]
                step *= 2
            for u in range(NU):
                at = u * LO + bt * 128
                xv[rows, at : at + 128] = v[u]

    loop(0, 8, butterfly)

    def lower(g):
        parts = []
        for i in range(2):
            for top in (0, NU // 2):
                at = (2 * g + i + top) * LO
                v = xv[:, at : at + LO]
                hi = v.astype(BF16)
                rest = v - hi.astype(F32)
                mid = rest.astype(BF16)
                low = (rest - mid.astype(F32)).astype(BF16)
                parts.append(jnp.concatenate([hi, mid, low], axis=1))
        w = jnp.concatenate(parts, axis=0)
        o = lax.dot_general(h, w, (((1,), (1,)), ((), ())), preferred_element_type=F32)
        for i in range(2):
            part = o[:, 128 * i : 128 * i + 128]
            at = (2 * g + i) * LO
            t[at : at + LO, :] = part
            t[at + LOCAL : at + LOCAL + LO, :] = part
            t[at + HALF : at + HALF + LO, :] = pltpu.roll(part, 64, 1)

    for g in range(NU // 4):
        lower(g)

    place_rows.wait()
    pl.semaphore_wait(barrier, 38)

    left = lax.broadcasted_iota(jnp.int32, (8, 128), 1) < 64
    sub = lax.broadcasted_iota(jnp.int32, (8, 128), 0)
    shifted = t.at[pl.ds(HALF, LOCAL)]

    def pick(out, k, cq):
        zq = (z + away(k)) & 7

        def body(i, carry):
            q = zq * 16 + i * 2 + cq
            sign = (1 - 2 * parity(row & q)).astype(F32)
            for top in (0, 8):
                v = None
                for j in range(8):
                    a = jnp.broadcast_to(t[pl.ds(idx[q * 32 + top + j], 1), :], (8, 128))
                    b = jnp.broadcast_to(shifted[pl.ds(idx[q * 32 + 16 + top + j], 1), :], (8, 128))
                    r = jnp.where(left, a, b)
                    v = r if v is None else jnp.where(sub == j, r, v)
                out[k, pl.ds(pl.multiple_of(i * 16, 16) + top, 8), :] = v * sign
            return carry

        lax.fori_loop(0, 8, body, 0, unroll=8)

    def remote(src, dst, ss, rs, device):
        return pltpu.make_async_remote_copy(
            src_ref=src, dst_ref=dst, send_sem=ss, recv_sem=rs,
            device_id=device, device_id_type=MESH,
        )

    def all_of(ref, ss, rs):
        return remote(ref, ref, ss, rs, near(0, 0, 1))

    def block(i):
        return pl.ds(pl.multiple_of(i * 32, 32), 32)

    def to_core(k):
        return remote(zo.at[k], rc.at[k], cs, cr.at[k], near(0, 0, 1))

    def to_y(k, d):
        return remote(acc.at[k, block((y + d) & 3)], ry.at[k - 2, d - 1], ys, yr.at[k - 2], near(d, 0, 0))

    def to_z(k):
        return remote(acc.at[k, block(y)], rz.at[k - 2], zs, zr, along_z(away(k)))

    def to_first(k):
        return remote(acc.at[k], rf.at[k], fs, fr, along_z(away(k)))

    def pick_other(k):
        pick(zo, k, 1 - c)
        to_core(k).start()

    def send_y(k):
        for d in (2, 1, 3):
            to_y(k, d).start()

    def pick_own(k):
        pick(acc, k, c)
        to_core(k).wait_recv()
        acc[k] = acc[k] + rc[k]
        pl.when(k < 2)(lambda: to_first(k).start())
        pl.when(k % 7 >= 2)(lambda: send_y(k))

    def add_y(k):
        all_of(ry.at[k - 2], ys, yr.at[k - 2]).wait_recv()
        mine = block(y)
        acc[k, mine] = (acc[k, mine] + ry[k - 2, 0]) + (ry[k - 2, 1] + ry[k - 2, 2])

    def pass_z(k):
        add_y(k)
        to_z(k).start()

    loop(0, 8, pick_other)
    loop(0, 8, pick_own)
    all_of(rf, fs, fr).wait_recv()
    acc[7] = acc[7] + (rf[0] + rf[1])
    send_y(7)
    loop(2, 7, pass_z)
    add_y(7)
    all_of(rz, zs, zr).wait_recv()
    rx[x] = (acc[7, block(y)] + rz[0]) + ((rz[1] + rz[2]) + (rz[3] + rz[4]))

    def to_x(d):
        return remote(rx.at[x], rx.at[x], xs, xr, near(0, d, 0))

    for d in (2, 1, 3):
        to_x(d).start()

    all_of(zo, cs, cr.at[0]).wait_send()
    all_of(rf, fs, fr).wait_send()
    all_of(ry, ys, yr.at[0]).wait_send()
    all_of(rx.at[pl.ds(0, 3)], xs, xr).wait_recv()
    a0 = rx[0] + rx[1]
    a1 = rx[2] + rx[3]
    first = jnp.concatenate([a0[:, :64], a1[:, :64]], axis=1)
    second = jnp.concatenate([a0[:, 64:], a1[:, 64:]], axis=1)
    m = jnp.concatenate([first, second], axis=0)
    mt[...] = m.T
    g = jnp.dot(
        mt[pl.ds(pl.multiple_of(x * 32, 32), 32), :], m,
        preferred_element_type=F32, precision=lax.Precision.HIGHEST,
    )
    for e in range(8):
        gs[e] = g[4 * e : 4 * e + 4]

    own = y * 2 + c

    def to_gs(i):
        dy, _, dc = part[i]
        return remote(gs.at[((y + dy) & 3) * 2 + c_at[dc]], gr.at[i], gss, gsr, near(dy, 0, dc))

    def to_gz(d):
        return remote(gz.at[z], gz.at[z], gzs, gzr, near(0, 0, 0, d))

    place = x * 8 + own

    def to_gf(i):
        return remote(gf.at[place], gf.at[place], gfs, gfr, near(*plane[i]))

    for i in range(7):
        to_gs(i).start()
    ms[0, 0], ms[0, 1] = first[:16], first[16:]
    ms[1, 0], ms[1, 1] = second[:16], second[16:]
    both_out[128:144, :] = ms[0, xl]
    both_out[144:160, :] = ms[1, xl]
    all_of(rz, zs, zr).wait_send()
    all_of(rx.at[pl.ds(0, 3)], xs, xr).wait_send()
    all_of(gr, gss, gsr).wait_recv()
    gz[z] = ((gs[own] + gr[0]) + (gr[1] + gr[2])) + ((gr[3] + gr[4]) + (gr[5] + gr[6]))
    for d in z_order:
        to_gz(d).start()
    all_of(gr, gss, gsr).wait_send()
    all_of(gz.at[pl.ds(0, 7)], gzs, gzr).wait_recv()
    gf[place] = (((gz[0] + gz[1]) + (gz[2] + gz[3])) + ((gz[4] + gz[5]) + (gz[6] + gz[7]))) * (1.0 / 4096.0)
    for i in range(31):
        to_gf(i).start()
    all_of(gz.at[pl.ds(0, 7)], gzs, gzr).wait_send()
    all_of(gf.at[pl.ds(0, 31)], gfs, gfr).wait_recv()
    for e in range(32):
        both_out[e * 4 : (e + 1) * 4, :] = gf[e]
    all_of(gf.at[pl.ds(0, 31)], gfs, gfr).wait_send()


def mix(panel, signs, rows):
    vm = pl.BlockSpec(memory_space=pltpu.VMEM)
    hbm = pl.BlockSpec(memory_space=pltpu.HBM)
    V = pltpu.VMEM
    D = pltpu.SemaphoreType.DMA
    return pl.pallas_call(
        mix_kernel,
        out_shape=jax.ShapeDtypeStruct((160, 128), F32),
        in_specs=[hbm, hbm, hbm],
        out_specs=vm,
        scratch_shapes=[
            V((64, LOCAL), F32),
            V((LOCAL // 128, 128), jnp.int32),
            V((4096,), jnp.int32),
            pltpu.SMEM((4096,), jnp.int32),
            V((LOCAL + HALF, 128), F32),
            V((8, 128, 128), F32),
            V((8, 128, 128), F32),
            V((8, 128, 128), F32),
            V((2, 128, 128), F32),
            V((6, 3, 32, 128), F32),
            V((5, 32, 128), F32),
            V((4, 32, 128), F32),
            V((2, 2, 16, 128), F32),
            V((128, 64), F32),
            V((8, 4, 128), F32),
            V((7, 4, 128), F32),
            V((8, 4, 128), F32),
            V((32, 4, 128), F32),
            D((11,)),
            D, D((8,)), D, D, D, D((6,)), D, D, D, D, D, D, D, D, D, D,
        ],
        compiler_params=pltpu.CompilerParams(
            collective_id=0, has_side_effects=True, vmem_limit_bytes=62 << 20
        ),
        name="mix",
    )(panel, signs.reshape(LOCAL // 128, 128), rows)


def rows_const(v, j):
    return jnp.broadcast_to(v[:, j : j + 1], (8, 128))


def factor_kernel(both_ref, basis_ref, tri_ref, a_ref, u_ref):
    n, width = 128, 32
    col = lax.axis_index("col")
    a_ref[:, :128] = both_ref[:128, :]
    samples = jnp.concatenate([both_ref[128:, :], jnp.zeros((96, 128), F32)], axis=0)
    a_ref[:, 128:] = samples.T
    lane = lax.broadcasted_iota(jnp.int32, (8, 128), 1)
    for panel in range(n // width):
        top = panel * width
        nb = width // 8
        blocks = [
            [a_ref[top + 8 * i : top + 8 * i + 8, 128 * t : 128 * t + 128] for t in range(2)]
            for i in range(nb)
        ]
        for j in range(nb):
            at = top + 8 * j
            rows = [
                [jnp.broadcast_to(blocks[j][t][k : k + 1, :], (8, 128)) for t in range(2)]
                for k in range(8)
            ]
            d = {(i, k): rows_const(rows[i][0], at + k) for i in range(8) for k in range(i + 1)}
            below = [[rows_const(blocks[i][0], at + k) for k in range(8)] for i in range(j + 1, nb)]
            for k in range(8):
                r = lax.rsqrt(d[k, k])
                for i in range(k + 1, 8):
                    d[i, k] = d[i, k] * r
                for i in range(k + 1, 8):
                    for q in range(k + 1, i + 1):
                        d[i, q] = d[i, q] - d[i, k] * d[q, k]
                for t in range(2):
                    rows[k][t] = rows[k][t] * r
                    for q in range(k + 1, 8):
                        rows[q][t] = rows[q][t] - d[q, k] * rows[k][t]
                for b in below:
                    b[k] = b[k] * r
                    for q in range(k + 1, 8):
                        b[q] = b[q] - d[q, k] * b[k]
            for k in range(8):
                keep = lane >= at + k
                u_ref[at + k : at + k + 1, :128] = jnp.where(keep, rows[k][0], 0.0)[:1]
                u_ref[at + k : at + k + 1, 128:] = rows[k][1][:1]
            for i in range(j + 1, nb):
                b = below[i - j - 1]
                for t in range(2):
                    v = blocks[i][t]
                    for k in range(8):
                        v = v - b[k] * rows[k][t]
                    blocks[i][t] = v
        if top + width < n:
            rest = top + width
            u = u_ref[top:rest, :]
            left = u[:, :128].T[rest:, :]
            upd = jnp.dot(left, u, preferred_element_type=F32, precision=lax.Precision.HIGHEST)
            a_ref[rest:, :] = a_ref[rest:, :] - upd
    half = pl.ds(pl.multiple_of(col * 64, 64), 64)
    tri_ref[...] = u_ref[half, :128]
    basis_ref[...] = u_ref[half, 128:].T[:32]


def factor(both):
    vm = pl.BlockSpec(memory_space=pltpu.VMEM)
    return pl.pallas_call(
        factor_kernel,
        out_shape=(jax.ShapeDtypeStruct((32, 64), F32), jax.ShapeDtypeStruct((64, 128), F32)),
        in_specs=[vm],
        out_specs=(vm, vm),
        scratch_shapes=[pltpu.VMEM((128, 256), F32), pltpu.VMEM((128, 256), F32)],
        compiler_params=pltpu.CompilerParams(vmem_limit_bytes=16 << 20),
        name="factor",
    )(both)


def shards(tall_panel_array, row_signs, sample_rows):
    basis, upper = factor(mix(tall_panel_array, row_signs, sample_rows))
    return basis.T, upper


def solution(mesh):
    return jax.shard_map(
        shards,
        mesh=mesh,
        in_specs=(P("col", "row"), P("row"), P()),
        out_specs=(P("col", "row"), P("col", None)),
        check_vma=False,
    )
```

```python
import jax
import jax.numpy as jnp
from jax import lax
from jax.experimental import pallas as pl
from jax.experimental.pallas import tpu as pltpu
from jax.sharding import PartitionSpec as P

F32 = jnp.float32
BF16 = jnp.bfloat16
MESH = pl.DeviceIdType.MESH
LO = 256
NU = 32
LOCAL = LO * NU
HALF = LOCAL // 2


def parity(bits):
    bits = bits ^ (bits >> 4)
    bits = bits ^ (bits >> 2)
    bits = bits ^ (bits >> 1)
    return bits & 1


def away(k):
    b = (k + 6) & 7
    return 4 + (b >> 1) * (1 - 2 * (b & 1)) - (b & 1) + ((b + 1) >> 3) - ((k + 1) >> 3)


def mix_kernel(
    x_hbm, ints, both_out,
    xv, sgv, idxv, idx, t, zo, acc, rc, rf, ry, rz, rx, ms, mt, gs, gr, gz, gf,
    in_sem, cs, cr, fs, fr, ys, yr, zs, zr, xs, xr, gss, gsr, gzs, gzr, gfs, gfr,
):
    row, col = lax.axis_index("row"), lax.axis_index("col")
    c = row & 1
    xl = (row >> 1) & 1
    y = (row >> 2) & 3
    z = row >> 4
    x = col * 2 + xl

    y_at = [((y + d) & 3) * 4 for d in range(4)]
    x_at = [(((x + d) & 1) * 2, ((x + d) & 3) >> 1) for d in range(4)]
    c_at = [c, 1 - c]
    z_at = [((z + d) & 7) * 16 for d in range(8)]

    def near(dy, dx, dc, dz=0):
        return {"row": z_at[dz] + y_at[dy] + x_at[dx][0] + c_at[dc], "col": x_at[dx][1]}

    def along_z(d):
        return {"row": ((z + d) & 7) * 16 + (row & 15), "col": col}

    plane = [(dy, dx, dc) for dy in (2, 1, 3, 0) for dx in (2, 1, 3, 0) for dc in (1, 0) if dy or dx or dc]
    part = [(dy, 0, dc) for dy in (2, 1, 3, 0) for dc in (1, 0) if dy or dc]
    z_order = (4, 3, 5, 2, 6, 1, 7)

    def loop(first, last, body):
        def step(i, carry):
            body(i)
            return carry

        lax.fori_loop(first, last, step, 0)

    place_rows = pltpu.make_async_copy(idxv, idx, in_sem.at[8])

    def fetch(i):
        at = pl.ds(pl.multiple_of(i * 8, 8), 8)
        return pltpu.make_async_copy(x_hbm.at[at], xv.at[at], in_sem.at[i])

    loop(0, 8, lambda i: fetch(i).start())
    idxv[...] = ints[pl.ds(LOCAL, 4096)] & (LOCAL - 1)
    place_rows.start()
    sgv[...] = ints[pl.ds(0, LOCAL)].reshape(LOCAL // 128, 128).astype(F32)

    barrier = pltpu.get_barrier_semaphore()
    for d in [near(*i) for i in plane] + [near(0, 0, 0, d) for d in z_order]:
        pl.semaphore_signal(barrier, inc=1, device_id=d, device_id_type=MESH)

    ri = lax.broadcasted_iota(jnp.int32, (LO, LO), 0)
    ci = lax.broadcasted_iota(jnp.int32, (LO, LO), 1)
    h = ((1 - 2 * parity(ri & ci)).astype(F32) * (1.0 / 1024.0)).astype(BF16)
    h = jnp.concatenate([h, h, h], axis=1)

    def butterfly(i):
        fetch(i).wait()
        rows = pl.ds(pl.multiple_of(i * 8, 8), 8)
        for bt in range(LO // 128):
            v = []
            for u in range(NU):
                at = u * LO + bt * 128
                v.append(xv[rows, at : at + 128] * sgv[at // 128 : at // 128 + 1, :])
            step = 1
            while step < NU:
                for u in range(NU):
                    if not u & step:
                        v[u], v[u + step] = v[u] + v[u + step], v[u] - v[u + step]
                step *= 2
            for u in range(NU):
                at = u * LO + bt * 128
                xv[rows, at : at + 128] = v[u]

    loop(0, 8, butterfly)

    def lower(g):
        parts = []
        for i in range(2):
            for top in (0, NU // 2):
                at = (2 * g + i + top) * LO
                v = xv[:, at : at + LO]
                hi = v.astype(BF16)
                rest = v - hi.astype(F32)
                mid = rest.astype(BF16)
                low = (rest - mid.astype(F32)).astype(BF16)
                parts.append(jnp.concatenate([hi, mid, low], axis=1))
        w = jnp.concatenate(parts, axis=0)
        o = lax.dot_general(h, w, (((1,), (1,)), ((), ())), preferred_element_type=F32)
        for i in range(2):
            part = o[:, 128 * i : 128 * i + 128]
            at = (2 * g + i) * LO
            t[at : at + LO, :] = part
            t[at + LOCAL : at + LOCAL + LO, :] = part
            t[at + HALF : at + HALF + LO, :] = pltpu.roll(part, 64, 1)

    for g in range(NU // 4):
        lower(g)

    place_rows.wait()
    pl.semaphore_wait(barrier, 38)

    left = lax.broadcasted_iota(jnp.int32, (8, 128), 1) < 64
    sub = lax.broadcasted_iota(jnp.int32, (8, 128), 0)
    shifted = t.at[pl.ds(HALF, LOCAL)]

    def pick(out, k, cq):
        zq = (z + away(k)) & 7

        def body(i, carry):
            q = zq * 16 + i * 2 + cq
            sign = (1 - 2 * parity(row & q)).astype(F32)
            for top in (0, 8):
                v = None
                for j in range(8):
                    a = jnp.broadcast_to(t[pl.ds(idx[q * 32 + top + j], 1), :], (8, 128))
                    b = jnp.broadcast_to(shifted[pl.ds(idx[q * 32 + 16 + top + j], 1), :], (8, 128))
                    r = jnp.where(left, a, b)
                    v = r if v is None else jnp.where(sub == j, r, v)
                out[k, pl.ds(pl.multiple_of(i * 16, 16) + top, 8), :] = v * sign
            return carry

        lax.fori_loop(0, 8, body, 0, unroll=8)

    def remote(src, dst, ss, rs, device):
        return pltpu.make_async_remote_copy(
            src_ref=src, dst_ref=dst, send_sem=ss, recv_sem=rs,
            device_id=device, device_id_type=MESH,
        )

    def all_of(ref, ss, rs):
        return remote(ref, ref, ss, rs, near(0, 0, 1))

    def block(i):
        return pl.ds(pl.multiple_of(i * 32, 32), 32)

    def to_core(k):
        return remote(zo.at[k], rc.at[k], cs, cr.at[k], near(0, 0, 1))

    def to_y(k, d):
        return remote(acc.at[k, block((y + d) & 3)], ry.at[k - 2, d - 1], ys, yr.at[k - 2], near(d, 0, 0))

    def to_z(k):
        return remote(acc.at[k, block(y)], rz.at[k - 2], zs, zr, along_z(away(k)))

    def to_first(k):
        return remote(acc.at[k], rf.at[k], fs, fr, along_z(away(k)))

    def pick_other(k):
        pick(zo, k, 1 - c)
        to_core(k).start()

    def send_y(k):
        for d in (2, 1, 3):
            to_y(k, d).start()

    def pick_own(k):
        pick(acc, k, c)
        to_core(k).wait_recv()
        acc[k] = acc[k] + rc[k]
        pl.when(k < 2)(lambda: to_first(k).start())
        pl.when((k >= 2) & (k < 7))(lambda: send_y(k))

    def add_y(k):
        all_of(ry.at[k - 2], ys, yr.at[k - 2]).wait_recv()
        mine = block(y)
        acc[k, mine] = (acc[k, mine] + ry[k - 2, 0]) + (ry[k - 2, 1] + ry[k - 2, 2])

    def pass_z(k):
        add_y(k)
        to_z(k).start()

    loop(0, 8, pick_other)
    loop(0, 8, pick_own)
    all_of(rf, fs, fr).wait_recv()
    acc[7] = acc[7] + (rf[0] + rf[1])
    send_y(7)
    loop(2, 7, pass_z)
    add_y(7)
    all_of(rz, zs, zr).wait_recv()
    rx[x] = (acc[7, block(y)] + rz[0]) + ((rz[1] + rz[2]) + (rz[3] + rz[4]))

    def to_x(d):
        return remote(rx.at[x], rx.at[x], xs, xr, near(0, d, 0))

    for d in (2, 1, 3):
        to_x(d).start()

    all_of(zo, cs, cr.at[0]).wait_send()
    all_of(rf, fs, fr).wait_send()
    all_of(ry, ys, yr.at[0]).wait_send()
    all_of(rx.at[pl.ds(0, 3)], xs, xr).wait_recv()
    a0 = rx[0] + rx[1]
    a1 = rx[2] + rx[3]
    first = jnp.concatenate([a0[:, :64], a1[:, :64]], axis=1)
    second = jnp.concatenate([a0[:, 64:], a1[:, 64:]], axis=1)
    m = jnp.concatenate([first, second], axis=0)
    mt[...] = m.T
    g = jnp.dot(
        mt[pl.ds(pl.multiple_of(x * 32, 32), 32), :], m,
        preferred_element_type=F32, precision=lax.Precision.HIGHEST,
    )
    for e in range(8):
        gs[e] = g[4 * e : 4 * e + 4]

    own = y * 2 + c

    def to_gs(i):
        dy, _, dc = part[i]
        return remote(gs.at[((y + dy) & 3) * 2 + c_at[dc]], gr.at[i], gss, gsr, near(dy, 0, dc))

    def to_gz(d):
        return remote(gz.at[z], gz.at[z], gzs, gzr, near(0, 0, 0, d))

    place = x * 8 + own

    def to_gf(i):
        return remote(gf.at[place], gf.at[place], gfs, gfr, near(*plane[i]))

    for i in range(7):
        to_gs(i).start()
    ms[0, 0], ms[0, 1] = first[:16], first[16:]
    ms[1, 0], ms[1, 1] = second[:16], second[16:]
    both_out[128:144, :] = ms[0, xl]
    both_out[144:160, :] = ms[1, xl]
    all_of(rz, zs, zr).wait_send()
    all_of(rx.at[pl.ds(0, 3)], xs, xr).wait_send()
    all_of(gr, gss, gsr).wait_recv()
    gz[z] = ((gs[own] + gr[0]) + (gr[1] + gr[2])) + ((gr[3] + gr[4]) + (gr[5] + gr[6]))
    for d in z_order:
        to_gz(d).start()
    all_of(gr, gss, gsr).wait_send()
    all_of(gz.at[pl.ds(0, 7)], gzs, gzr).wait_recv()
    gf[place] = (((gz[0] + gz[1]) + (gz[2] + gz[3])) + ((gz[4] + gz[5]) + (gz[6] + gz[7]))) * (1.0 / 4096.0)
    for i in range(31):
        to_gf(i).start()
    all_of(gz.at[pl.ds(0, 7)], gzs, gzr).wait_send()
    all_of(gf.at[pl.ds(0, 31)], gfs, gfr).wait_recv()
    for e in range(32):
        both_out[e * 4 : (e + 1) * 4, :] = gf[e]
    all_of(gf.at[pl.ds(0, 31)], gfs, gfr).wait_send()


def mix(panel, signs, rows):
    vm = pl.BlockSpec(memory_space=pltpu.VMEM)
    hbm = pl.BlockSpec(memory_space=pltpu.HBM)
    V = pltpu.VMEM
    D = pltpu.SemaphoreType.DMA
    return pl.pallas_call(
        mix_kernel,
        out_shape=jax.ShapeDtypeStruct((160, 128), F32),
        in_specs=[hbm, vm],
        out_specs=vm,
        scratch_shapes=[
            V((64, LOCAL), F32),
            V((LOCAL // 128, 128), F32),
            V((4096,), jnp.int32),
            pltpu.SMEM((4096,), jnp.int32),
            V((LOCAL + HALF, 128), F32),
            V((8, 128, 128), F32),
            V((8, 128, 128), F32),
            V((8, 128, 128), F32),
            V((2, 128, 128), F32),
            V((6, 3, 32, 128), F32),
            V((5, 32, 128), F32),
            V((4, 32, 128), F32),
            V((2, 2, 16, 128), F32),
            V((128, 64), F32),
            V((8, 4, 128), F32),
            V((7, 4, 128), F32),
            V((8, 4, 128), F32),
            V((32, 4, 128), F32),
            D((9,)),
            D, D((8,)), D, D, D, D((6,)), D, D, D, D, D, D, D, D, D, D,
        ],
        compiler_params=pltpu.CompilerParams(
            collective_id=0, has_side_effects=True, vmem_limit_bytes=52 << 20
        ),
        name="mix",
    )(panel, jnp.concatenate([signs, rows]))


def rows_const(v, j):
    return jnp.broadcast_to(v[:, j : j + 1], (8, 128))


def factor_kernel(both_ref, basis_ref, tri_ref, a_ref, u_ref):
    n, width = 128, 32
    col = lax.axis_index("col")
    a_ref[:, :128] = both_ref[:128, :]
    samples = jnp.concatenate([both_ref[128:, :], jnp.zeros((96, 128), F32)], axis=0)
    a_ref[:, 128:] = samples.T
    lane = lax.broadcasted_iota(jnp.int32, (8, 128), 1)
    for panel in range(n // width):
        top = panel * width
        nb = width // 8
        blocks = [
            [a_ref[top + 8 * i : top + 8 * i + 8, 128 * t : 128 * t + 128] for t in range(2)]
            for i in range(nb)
        ]
        for j in range(nb):
            at = top + 8 * j
            rows = [
                [jnp.broadcast_to(blocks[j][t][k : k + 1, :], (8, 128)) for t in range(2)]
                for k in range(8)
            ]
            d = {(i, k): rows_const(rows[i][0], at + k) for i in range(8) for k in range(i + 1)}
            below = [[rows_const(blocks[i][0], at + k) for k in range(8)] for i in range(j + 1, nb)]
            for k in range(8):
                r = lax.rsqrt(d[k, k])
                for i in range(k + 1, 8):
                    d[i, k] = d[i, k] * r
                for i in range(k + 1, 8):
                    for q in range(k + 1, i + 1):
                        d[i, q] = d[i, q] - d[i, k] * d[q, k]
                for t in range(2):
                    rows[k][t] = rows[k][t] * r
                    for q in range(k + 1, 8):
                        rows[q][t] = rows[q][t] - d[q, k] * rows[k][t]
                for b in below:
                    b[k] = b[k] * r
                    for q in range(k + 1, 8):
                        b[q] = b[q] - d[q, k] * b[k]
            for k in range(8):
                keep = lane >= at + k
                u_ref[at + k : at + k + 1, :128] = jnp.where(keep, rows[k][0], 0.0)[:1]
                u_ref[at + k : at + k + 1, 128:] = rows[k][1][:1]
            for i in range(j + 1, nb):
                b = below[i - j - 1]
                for t in range(2):
                    v = blocks[i][t]
                    for k in range(8):
                        v = v - b[k] * rows[k][t]
                    blocks[i][t] = v
        if top + width < n:
            rest = top + width
            u = u_ref[top:rest, :]
            left = u[:, :128].T[rest:, :]
            upd = jnp.dot(left, u, preferred_element_type=F32, precision=lax.Precision.HIGHEST)
            a_ref[rest:, :] = a_ref[rest:, :] - upd
    half = pl.ds(pl.multiple_of(col * 64, 64), 64)
    tri_ref[...] = u_ref[half, :128]
    basis_ref[...] = u_ref[half, 128:].T[:32]


def factor(both):
    vm = pl.BlockSpec(memory_space=pltpu.VMEM)
    return pl.pallas_call(
        factor_kernel,
        out_shape=(jax.ShapeDtypeStruct((32, 64), F32), jax.ShapeDtypeStruct((64, 128), F32)),
        in_specs=[vm],
        out_specs=(vm, vm),
        scratch_shapes=[pltpu.VMEM((128, 256), F32), pltpu.VMEM((128, 256), F32)],
        compiler_params=pltpu.CompilerParams(vmem_limit_bytes=16 << 20),
        name="factor",
    )(both)


def shards(tall_panel_array, row_signs, sample_rows):
    basis, upper = factor(mix(tall_panel_array, row_signs, sample_rows))
    return basis.T, upper


def solution(mesh):
    return jax.shard_map(
        shards,
        mesh=mesh,
        in_specs=(P("col", "row"), P("row"), P()),
        out_specs=(P("col", "row"), P("col", None)),
        check_vma=False,
    )
```

```python
import jax
import jax.numpy as jnp
from jax import lax
from jax.experimental import pallas as pl
from jax.experimental.pallas import tpu as pltpu
from jax.sharding import PartitionSpec as P

F32 = jnp.float32
BF16 = jnp.bfloat16
MESH = pl.DeviceIdType.MESH
LO = 256
NU = 32
LOCAL = LO * NU
HALF = LOCAL // 2


def parity(bits):
    bits = bits ^ (bits >> 4)
    bits = bits ^ (bits >> 2)
    bits = bits ^ (bits >> 1)
    return bits & 1


def away(k):
    b = (k + 6) & 7
    return 4 + (b >> 1) * (1 - 2 * (b & 1)) - (b & 1) + ((b + 1) >> 3) - ((k + 1) >> 3)


def mix_kernel(
    x_hbm, ints, both_out,
    xv, sgv, idxv, idx, t, zo, acc, rc, rf, ry, rz, mx, gs, gr, gz, gf,
    in_sem, cs, cr, fs, fr, ys, yr, zs, zr, xs, xr, gss, gsr, gzs, gzr, gfs, gfr,
):
    row, col = lax.axis_index("row"), lax.axis_index("col")
    c = row & 1
    y = (row >> 2) & 3
    z = row >> 4
    x = col * 2 + ((row >> 1) & 1)

    y_at = [((y + d) & 3) * 4 for d in range(4)]
    x_at = [(((x + d) & 1) * 2, ((x + d) & 3) >> 1) for d in range(4)]
    c_at = [c, 1 - c]
    z_at = [((z + d) & 7) * 16 for d in range(8)]

    def near(dy, dx, dc, dz=0):
        return {"row": z_at[dz] + y_at[dy] + x_at[dx][0] + c_at[dc], "col": x_at[dx][1]}

    def along_z(d):
        return {"row": ((z + d) & 7) * 16 + (row & 15), "col": col}

    plane = [(dy, dx, dc) for dy in (2, 1, 3, 0) for dx in (2, 1, 3, 0) for dc in (1, 0) if dy or dx or dc]
    z_order = (4, 3, 5, 2, 6, 1, 7)

    def loop(first, last, body):
        def step(i, carry):
            body(i)
            return carry

        lax.fori_loop(first, last, step, 0)

    place_rows = pltpu.make_async_copy(idxv, idx, in_sem.at[8])

    def fetch(i):
        at = pl.ds(pl.multiple_of(i * 8, 8), 8)
        return pltpu.make_async_copy(x_hbm.at[at], xv.at[at], in_sem.at[i])

    loop(0, 8, lambda i: fetch(i).start())
    idxv[...] = ints[pl.ds(LOCAL, 4096)] & (LOCAL - 1)
    place_rows.start()
    sgv[...] = ints[pl.ds(0, LOCAL)].reshape(LOCAL // 128, 128).astype(F32)

    barrier = pltpu.get_barrier_semaphore()
    for d in [near(*i) for i in plane] + [near(0, i, 0, d) for d in z_order for i in range(4 if 1 < d < 7 else 1)]:
        pl.semaphore_signal(barrier, inc=1, device_id=d, device_id_type=MESH)

    ri = lax.broadcasted_iota(jnp.int32, (LO, LO), 0)
    ci = lax.broadcasted_iota(jnp.int32, (LO, LO), 1)
    h = ((1 - 2 * parity(ri & ci)).astype(F32) * (1.0 / 1024.0)).astype(BF16)
    h = jnp.concatenate([h, h, h], axis=1)

    def butterfly(i):
        fetch(i).wait()
        rows = pl.ds(pl.multiple_of(i * 8, 8), 8)
        for bt in range(LO // 128):
            v = []
            for u in range(NU):
                at = u * LO + bt * 128
                v.append(xv[rows, at : at + 128] * sgv[at // 128 : at // 128 + 1, :])
            step = 1
            while step < NU:
                for u in range(NU):
                    if not u & step:
                        v[u], v[u + step] = v[u] + v[u + step], v[u] - v[u + step]
                step *= 2
            for u in range(NU):
                at = u * LO + bt * 128
                xv[rows, at : at + 128] = v[u]

    loop(0, 8, butterfly)

    def lower(g):
        parts = []
        for i in range(2):
            for top in (0, NU // 2):
                at = (2 * g + i + top) * LO
                v = xv[:, at : at + LO]
                hi = v.astype(BF16)
                rest = v - hi.astype(F32)
                mid = rest.astype(BF16)
                low = (rest - mid.astype(F32)).astype(BF16)
                parts.append(jnp.concatenate([hi, mid, low], axis=1))
        w = jnp.concatenate(parts, axis=0)
        o = lax.dot_general(h, w, (((1,), (1,)), ((), ())), preferred_element_type=F32)
        for i in range(2):
            part = o[:, 128 * i : 128 * i + 128]
            at = (2 * g + i) * LO
            t[at : at + LO, :] = part
            t[at + LOCAL : at + LOCAL + LO, :] = part
            t[at + HALF : at + HALF + LO, :] = pltpu.roll(part, 64, 1)

    for g in range(NU // 4):
        lower(g)

    place_rows.wait()
    pl.semaphore_wait(barrier, 53)

    left = lax.broadcasted_iota(jnp.int32, (8, 128), 1) < 64
    sub = lax.broadcasted_iota(jnp.int32, (8, 128), 0)
    shifted = t.at[pl.ds(HALF, LOCAL)]

    def pick(out, k, cq):
        zq = (z + away(k)) & 7

        def body(i, carry):
            q = zq * 16 + i * 2 + cq
            sign = (1 - 2 * parity(row & q)).astype(F32)
            for top in (0, 8):
                v = None
                for j in range(8):
                    a = jnp.broadcast_to(t[pl.ds(idx[q * 32 + top + j], 1), :], (8, 128))
                    b = jnp.broadcast_to(shifted[pl.ds(idx[q * 32 + 16 + top + j], 1), :], (8, 128))
                    r = jnp.where(left, a, b)
                    v = r if v is None else jnp.where(sub == j, r, v)
                out[k, pl.ds(pl.multiple_of(i * 16, 16) + top, 8), :] = v * sign
            return carry

        lax.fori_loop(0, 8, body, 0, unroll=8)

    def remote(src, dst, ss, rs, device):
        return pltpu.make_async_remote_copy(
            src_ref=src, dst_ref=dst, send_sem=ss, recv_sem=rs,
            device_id=device, device_id_type=MESH,
        )

    def all_of(ref, ss, rs):
        return remote(ref, ref, ss, rs, near(0, 0, 1))

    def block(i):
        return pl.ds(pl.multiple_of(i * 32, 32), 32)

    def to_core(k):
        return remote(zo.at[k], rc.at[k], cs, cr.at[k], near(0, 0, 1))

    def to_y(k, d):
        return remote(acc.at[k, block((y + d) & 3)], ry.at[k - 2, d - 1], ys, yr.at[k - 2], near(d, 0, 0))

    def quarter(k, i):
        return acc.at[k, pl.ds(pl.multiple_of(y * 32 + (i & 1) * 16 + (i >> 1) * 8, 8), 8)]

    def to_z(k, zq, d):
        device = {"row": zq * 16 + y_at[0] + x_at[d][0] + c, "col": x_at[d][1]}
        return remote(quarter(k, (x + d) & 3), rz.at[(k - 2) * 4 + x], zs, zr, device)

    def to_first(k):
        return remote(acc.at[k], rf.at[k], fs, fr, along_z(away(k)))

    def pick_other(k):
        pick(zo, k, 1 - c)
        to_core(k).start()

    def send_y(k):
        for d in (2, 1, 3):
            to_y(k, d).start()

    def pick_own(k):
        pick(acc, k, c)
        to_core(k).wait_recv()
        acc[k] = acc[k] + rc[k]
        pl.when(k < 2)(lambda: to_first(k).start())
        pl.when((k >= 2) & (k < 7))(lambda: send_y(k))

    def add_y(k):
        all_of(ry.at[k - 2], ys, yr.at[k - 2]).wait_recv()
        mine = block(y)
        acc[k, mine] = (acc[k, mine] + ry[k - 2, 0]) + (ry[k - 2, 1] + ry[k - 2, 2])

    def pass_z(k):
        add_y(k)
        zq = (z + away(k)) & 7
        for d in (2, 1, 3, 0):
            to_z(k, zq, d).start()

    loop(0, 8, pick_other)
    loop(0, 8, pick_own)
    all_of(rf, fs, fr).wait_recv()
    acc[7] = acc[7] + (rf[0] + rf[1])
    send_y(7)
    loop(2, 7, pass_z)
    add_y(7)
    for d in (2, 1, 3):
        to_z(7, z, d).start()
    rz[20 + x] = quarter(7, x)[...]
    all_of(zo, cs, cr.at[0]).wait_send()
    all_of(rf, fs, fr).wait_send()
    all_of(ry, ys, yr.at[0]).wait_send()
    others = all_of(rz.at[pl.ds(0, 23)], zs, zr)
    others.wait_recv()

    def total(i):
        v = [rz[4 * k + i] for k in range(6)] + [rz[4 * k + i + 1] for k in range(6)]
        while len(v) > 1:
            v = [v[j] + v[j + 1] if j + 1 < len(v) else v[j] for j in range(0, len(v), 2)]
        return v[0]

    a0, a1 = total(0), total(2)
    first = jnp.concatenate([a0[:, :64], a1[:, :64]], axis=1)
    second = jnp.concatenate([a0[:, 64:], a1[:, 64:]], axis=1)
    m = jnp.concatenate([first, second], axis=0)
    g = jnp.dot(m.T, m, preferred_element_type=F32, precision=lax.Precision.HIGHEST)
    for e in range(32):
        gs[e] = g[4 * e : 4 * e + 4]

    place = x * 8 + y * 2 + c

    def to_gs(i):
        dy, dx, dc = plane[i]
        e = ((x + dx) & 3) * 8 + ((y + dy) & 3) * 2 + c_at[dc]
        return remote(gs.at[e], gr.at[i], gss, gsr, near(dy, dx, dc))

    to_mate = remote(mx.at[x >> 1], mx.at[x >> 1], xs, xr, near(0, 2, 0))

    def to_gz(d):
        return remote(gz.at[z], gz.at[z], gzs, gzr, near(0, 0, 0, d))

    def to_gf(i):
        return remote(gf.at[place], gf.at[place], gfs, gfr, near(*plane[i]))

    for i in range(31):
        to_gs(i).start()
    mx[x >> 1] = m
    to_mate.start()
    others.wait_send()
    all_of(gr, gss, gsr).wait_recv()
    v = [gr[i] for i in range(31)] + [gs[place]]
    while len(v) > 1:
        v = [v[j] + v[j + 1] for j in range(0, len(v), 2)]
    gz[z] = v[0]
    for d in z_order:
        to_gz(d).start()
    all_of(gr, gss, gsr).wait_send()
    to_mate.wait()
    for i in range(2):
        for j in range(2):
            both_out[128 + 16 * j + 8 * i : 136 + 16 * j + 8 * i, :] = mx[i, 8 * j : 8 * j + 8]
    all_of(gz.at[pl.ds(0, 7)], gzs, gzr).wait_recv()
    gf[place] = (((gz[0] + gz[1]) + (gz[2] + gz[3])) + ((gz[4] + gz[5]) + (gz[6] + gz[7]))) * (1.0 / 4096.0)
    for i in range(31):
        to_gf(i).start()
    all_of(gz.at[pl.ds(0, 7)], gzs, gzr).wait_send()
    all_of(gf.at[pl.ds(0, 31)], gfs, gfr).wait_recv()
    for e in range(32):
        both_out[e * 4 : (e + 1) * 4, :] = gf[e]
    all_of(gf.at[pl.ds(0, 31)], gfs, gfr).wait_send()


def mix(panel, signs, rows):
    vm = pl.BlockSpec(memory_space=pltpu.VMEM)
    hbm = pl.BlockSpec(memory_space=pltpu.HBM)
    V = pltpu.VMEM
    D = pltpu.SemaphoreType.DMA
    return pl.pallas_call(
        mix_kernel,
        out_shape=jax.ShapeDtypeStruct((160, 128), F32),
        in_specs=[hbm, vm],
        out_specs=vm,
        scratch_shapes=[
            V((64, LOCAL), F32),
            V((LOCAL // 128, 128), F32),
            V((4096,), jnp.int32),
            pltpu.SMEM((4096,), jnp.int32),
            V((LOCAL + HALF, 128), F32),
            V((8, 128, 128), F32),
            V((8, 128, 128), F32),
            V((8, 128, 128), F32),
            V((2, 128, 128), F32),
            V((6, 3, 32, 128), F32),
            V((24, 8, 128), F32),
            V((2, 16, 128), F32),
            V((32, 4, 128), F32),
            V((31, 4, 128), F32),
            V((8, 4, 128), F32),
            V((32, 4, 128), F32),
            D((9,)),
            D, D((8,)), D, D, D, D((6,)), D, D, D, D, D, D, D, D, D, D,
        ],
        compiler_params=pltpu.CompilerParams(
            collective_id=0, has_side_effects=True, vmem_limit_bytes=52 << 20
        ),
        name="mix",
    )(panel, jnp.concatenate([signs, rows]))


def rows_const(v, j):
    return jnp.broadcast_to(v[:, j : j + 1], (8, 128))


def factor_kernel(both_ref, basis_ref, tri_ref, a_ref, u_ref):
    n, width = 128, 64
    col = lax.axis_index("col")
    a_ref[:, :128] = both_ref[:128, :]
    samples = jnp.concatenate([both_ref[128:, :], jnp.zeros((96, 128), F32)], axis=0)
    a_ref[:, 128:] = samples.T
    lane = lax.broadcasted_iota(jnp.int32, (8, 128), 1)
    for panel in range(n // width):
        top = panel * width
        nb = width // 8
        blocks = [
            [a_ref[top + 8 * i : top + 8 * i + 8, 128 * t : 128 * t + 128] for t in range(2)]
            for i in range(nb)
        ]
        for j in range(nb):
            at = top + 8 * j
            rows = [
                [jnp.broadcast_to(blocks[j][t][k : k + 1, :], (8, 128)) for t in range(2)]
                for k in range(8)
            ]
            d = {(i, k): rows_const(rows[i][0], at + k) for i in range(8) for k in range(i + 1)}
            below = [[rows_const(blocks[i][0], at + k) for k in range(8)] for i in range(j + 1, nb)]
            for k in range(8):
                r = lax.rsqrt(d[k, k])
                for i in range(k + 1, 8):
                    d[i, k] = d[i, k] * r
                for i in range(k + 1, 8):
                    for q in range(k + 1, i + 1):
                        d[i, q] = d[i, q] - d[i, k] * d[q, k]
                for t in range(2):
                    rows[k][t] = rows[k][t] * r
                    for q in range(k + 1, 8):
                        rows[q][t] = rows[q][t] - d[q, k] * rows[k][t]
                for b in below:
                    b[k] = b[k] * r
                    for q in range(k + 1, 8):
                        b[q] = b[q] - d[q, k] * b[k]
            for k in range(8):
                keep = lane >= at + k
                u_ref[at + k : at + k + 1, :128] = jnp.where(keep, rows[k][0], 0.0)[:1]
                u_ref[at + k : at + k + 1, 128:] = rows[k][1][:1]
            for i in range(j + 1, nb):
                b = below[i - j - 1]
                for t in range(2):
                    v = blocks[i][t]
                    for k in range(8):
                        v = v - b[k] * rows[k][t]
                    blocks[i][t] = v
        if top + width < n:
            rest = top + width
            u = u_ref[top:rest, :]
            left = u[:, :128].T[rest:, :]
            upd = jnp.dot(left, u, preferred_element_type=F32, precision=lax.Precision.HIGHEST)
            a_ref[rest:, :] = a_ref[rest:, :] - upd
    half = pl.ds(pl.multiple_of(col * 64, 64), 64)
    tri_ref[...] = u_ref[half, :128]
    basis_ref[...] = u_ref[half, 128:].T[:32]


def factor(both):
    vm = pl.BlockSpec(memory_space=pltpu.VMEM)
    return pl.pallas_call(
        factor_kernel,
        out_shape=(jax.ShapeDtypeStruct((32, 64), F32), jax.ShapeDtypeStruct((64, 128), F32)),
        in_specs=[vm],
        out_specs=(vm, vm),
        scratch_shapes=[pltpu.VMEM((128, 256), F32), pltpu.VMEM((128, 256), F32)],
        compiler_params=pltpu.CompilerParams(vmem_limit_bytes=16 << 20),
        name="factor",
    )(both)


def shards(tall_panel_array, row_signs, sample_rows):
    basis, upper = factor(mix(tall_panel_array, row_signs, sample_rows))
    return basis.T, upper


def solution(mesh):
    return jax.shard_map(
        shards,
        mesh=mesh,
        in_specs=(P("col", "row"), P("row"), P()),
        out_specs=(P("col", "row"), P("col", None)),
        check_vma=False,
    )
```

```python
import jax
import jax.numpy as jnp
from jax import lax
from jax.experimental import pallas as pl
from jax.experimental.pallas import tpu as pltpu
from jax.sharding import PartitionSpec as P

F32 = jnp.float32
BF16 = jnp.bfloat16
MESH = pl.DeviceIdType.MESH
LO = 256
NU = 32
LOCAL = LO * NU
HALF = LOCAL // 2


def parity(bits):
    bits = bits ^ (bits >> 4)
    bits = bits ^ (bits >> 2)
    bits = bits ^ (bits >> 1)
    return bits & 1


def away(k):
    b = (k + 6) & 7
    return 4 + (b >> 1) * (1 - 2 * (b & 1)) - (b & 1) + ((b + 1) >> 3) - ((k + 1) >> 3)


def mix_kernel(
    x_hbm, ints, both_out,
    xv, sgv, idxv, idx, t, zo, acc, rc, rf, ry, rz, mx, gs, gr, gz, gf,
    in_sem, cs, cr, fs, fr, ys, yr, zs, zr, xs, xr, gss, gsr, gzs, gzr, gfs, gfr,
):
    row, col = lax.axis_index("row"), lax.axis_index("col")
    c = row & 1
    y = (row >> 2) & 3
    z = row >> 4
    x = col * 2 + ((row >> 1) & 1)

    y_at = [((y + d) & 3) * 4 for d in range(4)]
    x_at = [(((x + d) & 1) * 2, ((x + d) & 3) >> 1) for d in range(4)]
    c_at = [c, 1 - c]
    z_at = [((z + d) & 7) * 16 for d in range(8)]

    def near(dy, dx, dc, dz=0):
        return {"row": z_at[dz] + y_at[dy] + x_at[dx][0] + c_at[dc], "col": x_at[dx][1]}

    def along_z(d):
        return {"row": ((z + d) & 7) * 16 + (row & 15), "col": col}

    plane = [(dy, dx, dc) for dy in (2, 1, 3, 0) for dx in (2, 1, 3, 0) for dc in (1, 0) if dy or dx or dc]
    z_order = (4, 3, 5, 2, 6, 1, 7)

    def loop(first, last, body):
        def step(i, carry):
            body(i)
            return carry

        lax.fori_loop(first, last, step, 0)

    place_rows = pltpu.make_async_copy(idxv, idx, in_sem.at[8])

    def fetch(i):
        at = pl.ds(pl.multiple_of(i * 8, 8), 8)
        return pltpu.make_async_copy(x_hbm.at[at], xv.at[at], in_sem.at[i])

    loop(0, 8, lambda i: fetch(i).start())
    idxv[...] = ints[pl.ds(LOCAL, 4096)] & (LOCAL - 1)
    place_rows.start()
    sgv[...] = ints[pl.ds(0, LOCAL)].reshape(LOCAL // 128, 128).astype(F32)

    barrier = pltpu.get_barrier_semaphore()
    for d in [near(*i) for i in plane] + [near(0, i, 0, d) for d in z_order for i in range(4 if 1 < d < 7 else 1)]:
        pl.semaphore_signal(barrier, inc=1, device_id=d, device_id_type=MESH)

    ri = lax.broadcasted_iota(jnp.int32, (LO, LO), 0)
    ci = lax.broadcasted_iota(jnp.int32, (LO, LO), 1)
    h = ((1 - 2 * parity(ri & ci)).astype(F32) * (1.0 / 1024.0)).astype(BF16)
    h = jnp.concatenate([h, h, h], axis=1)

    def butterfly(i):
        fetch(i).wait()
        rows = pl.ds(pl.multiple_of(i * 8, 8), 8)
        for bt in range(LO // 128):
            v = []
            for u in range(NU):
                at = u * LO + bt * 128
                v.append(xv[rows, at : at + 128] * sgv[at // 128 : at // 128 + 1, :])
            step = 1
            while step < NU:
                for u in range(NU):
                    if not u & step:
                        v[u], v[u + step] = v[u] + v[u + step], v[u] - v[u + step]
                step *= 2
            for u in range(NU):
                at = u * LO + bt * 128
                xv[rows, at : at + 128] = v[u]

    loop(0, 8, butterfly)

    def lower(g):
        parts = []
        for i in range(2):
            for top in (0, NU // 2):
                at = (2 * g + i + top) * LO
                v = xv[:, at : at + LO]
                hi = v.astype(BF16)
                rest = v - hi.astype(F32)
                mid = rest.astype(BF16)
                low = (rest - mid.astype(F32)).astype(BF16)
                parts.append(jnp.concatenate([hi, mid, low], axis=1))
        w = jnp.concatenate(parts, axis=0)
        o = lax.dot_general(h, w, (((1,), (1,)), ((), ())), preferred_element_type=F32)
        for i in range(2):
            part = o[:, 128 * i : 128 * i + 128]
            at = (2 * g + i) * LO
            t[at : at + LO, :] = part
            t[at + LOCAL : at + LOCAL + LO, :] = part
            t[at + HALF : at + HALF + LO, :] = pltpu.roll(part, 64, 1)

    for g in range(NU // 4):
        lower(g)

    place_rows.wait()
    pl.semaphore_wait(barrier, 53)

    left = lax.broadcasted_iota(jnp.int32, (8, 128), 1) < 64
    sub = lax.broadcasted_iota(jnp.int32, (8, 128), 0)
    shifted = t.at[pl.ds(HALF, LOCAL)]

    def pick(out, k, cq):
        zq = (z + away(k)) & 7

        def body(i, carry):
            q = zq * 16 + i * 2 + cq
            sign = (1 - 2 * parity(row & q)).astype(F32)
            for top in (0, 8):
                v = None
                for j in range(8):
                    a = jnp.broadcast_to(t[pl.ds(idx[q * 32 + top + j], 1), :], (8, 128))
                    b = jnp.broadcast_to(shifted[pl.ds(idx[q * 32 + 16 + top + j], 1), :], (8, 128))
                    r = jnp.where(left, a, b)
                    v = r if v is None else jnp.where(sub == j, r, v)
                out[k, pl.ds(pl.multiple_of(i * 16, 16) + top, 8), :] = v * sign
            return carry

        lax.fori_loop(0, 8, body, 0, unroll=8)

    def remote(src, dst, ss, rs, device):
        return pltpu.make_async_remote_copy(
            src_ref=src, dst_ref=dst, send_sem=ss, recv_sem=rs,
            device_id=device, device_id_type=MESH,
        )

    def all_of(ref, ss, rs):
        return remote(ref, ref, ss, rs, near(0, 0, 1))

    def block(i):
        return pl.ds(pl.multiple_of(i * 32, 32), 32)

    def to_core(k):
        return remote(zo.at[k], rc.at[k], cs, cr.at[k], near(0, 0, 1))

    def to_y(k, d):
        return remote(acc.at[k, block((y + d) & 3)], ry.at[k - 2, d - 1], ys, yr.at[k - 2], near(d, 0, 0))

    def quarter(k, i):
        return acc.at[k, pl.ds(pl.multiple_of(y * 32 + (i & 1) * 16 + (i >> 1) * 8, 8), 8)]

    def to_z(k, zq, d):
        device = {"row": zq * 16 + y_at[0] + x_at[d][0] + c, "col": x_at[d][1]}
        return remote(quarter(k, (x + d) & 3), rz.at[(k - 2) * 4 + x], zs, zr, device)

    def to_first(k):
        return remote(acc.at[k], rf.at[k], fs, fr, along_z(away(k)))

    def pick_other(k):
        pick(zo, k, 1 - c)
        to_core(k).start()

    def send_y(k):
        for d in (2, 1, 3):
            to_y(k, d).start()

    def share(k):
        to_core(k).wait_recv()
        acc[k] = acc[k] + rc[k]
        pl.when(k < 2)(lambda: to_first(k).start())
        pl.when((k >= 2) & (k < 7))(lambda: send_y(k))

    def pick_own(k):
        pl.when(k < 8)(lambda: pick(acc, k, c))
        pl.when(k >= 5)(lambda: share(k - 5))

    def add_y(k):
        all_of(ry.at[k - 2], ys, yr.at[k - 2]).wait_recv()
        mine = block(y)
        acc[k, mine] = (acc[k, mine] + ry[k - 2, 0]) + (ry[k - 2, 1] + ry[k - 2, 2])

    def pass_z(k):
        add_y(k)
        zq = (z + away(k)) & 7
        for d in (2, 1, 3, 0):
            to_z(k, zq, d).start()

    loop(0, 8, pick_other)
    loop(0, 13, pick_own)
    all_of(rf, fs, fr).wait_recv()
    acc[7] = acc[7] + (rf[0] + rf[1])
    send_y(7)
    loop(2, 7, pass_z)
    add_y(7)
    for d in (2, 1, 3):
        to_z(7, z, d).start()
    rz[20 + x] = quarter(7, x)[...]
    all_of(zo, cs, cr.at[0]).wait_send()
    all_of(rf, fs, fr).wait_send()
    all_of(ry, ys, yr.at[0]).wait_send()
    others = all_of(rz.at[pl.ds(0, 23)], zs, zr)
    others.wait_recv()

    def total(i):
        v = [rz[4 * k + i] for k in range(6)] + [rz[4 * k + i + 1] for k in range(6)]
        while len(v) > 1:
            v = [v[j] + v[j + 1] if j + 1 < len(v) else v[j] for j in range(0, len(v), 2)]
        return v[0]

    a0, a1 = total(0), total(2)
    first = jnp.concatenate([a0[:, :64], a1[:, :64]], axis=1)
    second = jnp.concatenate([a0[:, 64:], a1[:, 64:]], axis=1)
    m = jnp.concatenate([first, second], axis=0)
    g = jnp.dot(m.T, m, preferred_element_type=F32, precision=lax.Precision.HIGHEST)
    for e in range(32):
        gs[e] = g[4 * e : 4 * e + 4]

    place = x * 8 + y * 2 + c

    def to_gs(i):
        dy, dx, dc = plane[i]
        e = ((x + dx) & 3) * 8 + ((y + dy) & 3) * 2 + c_at[dc]
        return remote(gs.at[e], gr.at[i], gss, gsr, near(dy, dx, dc))

    to_mate = remote(mx.at[x >> 1], mx.at[x >> 1], xs, xr, near(0, 2, 0))

    def to_gz(d):
        return remote(gz.at[z], gz.at[z], gzs, gzr, near(0, 0, 0, d))

    def to_gf(i):
        return remote(gf.at[place], gf.at[place], gfs, gfr, near(*plane[i]))

    for i in range(31):
        to_gs(i).start()
    mx[x >> 1] = m
    to_mate.start()
    others.wait_send()
    all_of(gr, gss, gsr).wait_recv()
    v = [gr[i] for i in range(31)] + [gs[place]]
    while len(v) > 1:
        v = [v[j] + v[j + 1] for j in range(0, len(v), 2)]
    gz[z] = v[0]
    for d in z_order:
        to_gz(d).start()
    all_of(gr, gss, gsr).wait_send()
    to_mate.wait()
    for i in range(2):
        for j in range(2):
            both_out[128 + 16 * j + 8 * i : 136 + 16 * j + 8 * i, :] = mx[i, 8 * j : 8 * j + 8]
    all_of(gz.at[pl.ds(0, 7)], gzs, gzr).wait_recv()
    gf[place] = (((gz[0] + gz[1]) + (gz[2] + gz[3])) + ((gz[4] + gz[5]) + (gz[6] + gz[7]))) * (1.0 / 4096.0)
    for i in range(31):
        to_gf(i).start()
    all_of(gz.at[pl.ds(0, 7)], gzs, gzr).wait_send()
    all_of(gf.at[pl.ds(0, 31)], gfs, gfr).wait_recv()
    for e in range(32):
        both_out[e * 4 : (e + 1) * 4, :] = gf[e]
    all_of(gf.at[pl.ds(0, 31)], gfs, gfr).wait_send()


def mix(panel, signs, rows):
    vm = pl.BlockSpec(memory_space=pltpu.VMEM)
    hbm = pl.BlockSpec(memory_space=pltpu.HBM)
    V = pltpu.VMEM
    D = pltpu.SemaphoreType.DMA
    return pl.pallas_call(
        mix_kernel,
        out_shape=jax.ShapeDtypeStruct((160, 128), F32),
        in_specs=[hbm, vm],
        out_specs=vm,
        scratch_shapes=[
            V((64, LOCAL), F32),
            V((LOCAL // 128, 128), F32),
            V((4096,), jnp.int32),
            pltpu.SMEM((4096,), jnp.int32),
            V((LOCAL + HALF, 128), F32),
            V((8, 128, 128), F32),
            V((8, 128, 128), F32),
            V((8, 128, 128), F32),
            V((2, 128, 128), F32),
            V((6, 3, 32, 128), F32),
            V((24, 8, 128), F32),
            V((2, 16, 128), F32),
            V((32, 4, 128), F32),
            V((31, 4, 128), F32),
            V((8, 4, 128), F32),
            V((32, 4, 128), F32),
            D((9,)),
            D, D((8,)), D, D, D, D((6,)), D, D, D, D, D, D, D, D, D, D,
        ],
        compiler_params=pltpu.CompilerParams(
            collective_id=0, has_side_effects=True, vmem_limit_bytes=52 << 20
        ),
        name="mix",
    )(panel, jnp.concatenate([signs, rows]))


def rows_const(v, j):
    return jnp.broadcast_to(v[:, j : j + 1], (8, 128))


def factor_kernel(both_ref, basis_ref, tri_ref, a_ref, u_ref):
    n, width = 128, 32
    col = lax.axis_index("col")
    gram = both_ref[:128, :]
    eye = lax.broadcasted_iota(jnp.int32, (n, n), 0) == lax.broadcasted_iota(jnp.int32, (n, n), 1)
    diagonal = jnp.where(eye, gram, 0.0)
    across = jnp.sum(diagonal, axis=0, keepdims=True)
    scale = lax.rsqrt(across)
    down = lax.rsqrt(jnp.sum(diagonal, axis=1, keepdims=True))
    a_ref[:, :128] = gram * scale * down
    samples = jnp.concatenate([both_ref[128:, :], jnp.zeros((96, 128), F32)], axis=0)
    a_ref[:, 128:] = samples.T * down
    back = across * scale
    lane = lax.broadcasted_iota(jnp.int32, (8, 128), 1)
    for panel in range(n // width):
        top = panel * width
        nb = width // 8
        blocks = [
            [a_ref[top + 8 * i : top + 8 * i + 8, 128 * t : 128 * t + 128] for t in range(2)]
            for i in range(nb)
        ]
        for j in range(nb):
            at = top + 8 * j
            rows = [
                [jnp.broadcast_to(blocks[j][t][k : k + 1, :], (8, 128)) for t in range(2)]
                for k in range(8)
            ]
            d = {(i, k): rows_const(rows[i][0], at + k) for i in range(8) for k in range(i + 1)}
            below = [[rows_const(blocks[i][0], at + k) for k in range(8)] for i in range(j + 1, nb)]
            for k in range(0, 8, 2):
                first = lax.rsqrt(d[k, k])
                det = d[k, k] * d[k + 1, k + 1] - d[k + 1, k] * d[k + 1, k]
                second = lax.rsqrt(det) * (d[k, k] * first)
                low = d[k + 1, k] * first

                def pair(v, w):
                    v = v * first
                    return v, (w - low * v) * second

                for i in range(k + 2, 8):
                    d[i, k], d[i, k + 1] = pair(d[i, k], d[i, k + 1])
                for i in range(k + 2, 8):
                    for q in range(k + 2, i + 1):
                        d[i, q] = d[i, q] - d[i, k] * d[q, k] - d[i, k + 1] * d[q, k + 1]
                for t in range(2):
                    rows[k][t], rows[k + 1][t] = pair(rows[k][t], rows[k + 1][t])
                    for q in range(k + 2, 8):
                        rows[q][t] = rows[q][t] - d[q, k] * rows[k][t] - d[q, k + 1] * rows[k + 1][t]
                for b in below:
                    b[k], b[k + 1] = pair(b[k], b[k + 1])
                    for q in range(k + 2, 8):
                        b[q] = b[q] - d[q, k] * b[k] - d[q, k + 1] * b[k + 1]
            for k in range(8):
                keep = lane >= at + k
                u_ref[at + k : at + k + 1, :128] = jnp.where(keep, rows[k][0], 0.0)[:1]
                u_ref[at + k : at + k + 1, 128:] = rows[k][1][:1]
            for i in range(j + 1, nb):
                b = below[i - j - 1]
                for t in range(2):
                    v = blocks[i][t]
                    for k in range(8):
                        v = v - b[k] * rows[k][t]
                    blocks[i][t] = v
        if top + width < n:
            rest = top + width
            u = u_ref[top:rest, :]
            left = u[:, :128].T[rest:, :]
            upd = jnp.dot(left, u, preferred_element_type=F32, precision=lax.Precision.HIGHEST)
            a_ref[rest:, :] = a_ref[rest:, :] - upd
    half = pl.ds(pl.multiple_of(col * 64, 64), 64)
    tri_ref[...] = u_ref[half, :128] * back
    basis_ref[...] = u_ref[half, 128:].T[:32]


def factor(both):
    vm = pl.BlockSpec(memory_space=pltpu.VMEM)
    return pl.pallas_call(
        factor_kernel,
        out_shape=(jax.ShapeDtypeStruct((32, 64), F32), jax.ShapeDtypeStruct((64, 128), F32)),
        in_specs=[vm],
        out_specs=(vm, vm),
        scratch_shapes=[pltpu.VMEM((128, 256), F32), pltpu.VMEM((128, 256), F32)],
        compiler_params=pltpu.CompilerParams(vmem_limit_bytes=16 << 20),
        name="factor",
    )(both)


def shards(tall_panel_array, row_signs, sample_rows):
    basis, upper = factor(mix(tall_panel_array, row_signs, sample_rows))
    return basis.T, upper


def solution(mesh):
    return jax.shard_map(
        shards,
        mesh=mesh,
        in_specs=(P("col", "row"), P("row"), P()),
        out_specs=(P("col", "row"), P("col", None)),
        check_vma=False,
    )
```

```python
import jax
import jax.numpy as jnp
from jax import lax
from jax.experimental import pallas as pl
from jax.experimental.pallas import tpu as pltpu
from jax.sharding import PartitionSpec as P

F32 = jnp.float32
BF16 = jnp.bfloat16
MESH = pl.DeviceIdType.MESH
LO = 256
NU = 32
LOCAL = LO * NU
HALF = LOCAL // 2


def parity(bits):
    bits = bits ^ (bits >> 4)
    bits = bits ^ (bits >> 2)
    bits = bits ^ (bits >> 1)
    return bits & 1


def away(k):
    b = (k + 6) & 7
    return 4 + (b >> 1) * (1 - 2 * (b & 1)) - (b & 1) + ((b + 1) >> 3) - ((k + 1) >> 3)


def mix_kernel(
    x_hbm, ints, both_out,
    xv, sgv, idxv, idx, t, zo, acc, rc, rf, ry, rz, mx, gs, gr, gz, gf,
    in_sem, cs, cr, fs, fr, ys, yr, zs, zr, xs, xr, gss, gsr, gzs, gzr, gfs, gfr,
):
    row, col = lax.axis_index("row"), lax.axis_index("col")
    c = row & 1
    y = (row >> 2) & 3
    z = row >> 4
    x = col * 2 + ((row >> 1) & 1)

    y_at = [((y + d) & 3) * 4 for d in range(4)]
    x_at = [(((x + d) & 1) * 2, ((x + d) & 3) >> 1) for d in range(4)]
    c_at = [c, 1 - c]
    z_at = [((z + d) & 7) * 16 for d in range(8)]

    def near(dy, dx, dc, dz=0):
        return {"row": z_at[dz] + y_at[dy] + x_at[dx][0] + c_at[dc], "col": x_at[dx][1]}

    def along_z(d):
        return {"row": ((z + d) & 7) * 16 + (row & 15), "col": col}

    plane = [(dy, dx, dc) for dy in (2, 1, 3, 0) for dx in (2, 1, 3, 0) for dc in (1, 0) if dy or dx or dc]
    z_order = (4, 3, 5, 2, 6, 1, 7)

    def loop(first, last, body):
        def step(i, carry):
            body(i)
            return carry

        lax.fori_loop(first, last, step, 0)

    place_rows = pltpu.make_async_copy(idxv, idx, in_sem.at[8])

    def fetch(i):
        at = pl.ds(pl.multiple_of(i * 8, 8), 8)
        return pltpu.make_async_copy(x_hbm.at[at], xv.at[at], in_sem.at[i])

    loop(0, 8, lambda i: fetch(i).start())
    idxv[...] = ints[pl.ds(LOCAL, 4096)] & (LOCAL - 1)
    place_rows.start()
    sgv[...] = ints[pl.ds(0, LOCAL)].reshape(LOCAL // 128, 128).astype(F32)

    barrier = pltpu.get_barrier_semaphore()
    for d in [near(*i) for i in plane] + [near(0, i, 0, d) for d in z_order for i in range(4 if 1 < d < 7 else 1)]:
        pl.semaphore_signal(barrier, inc=1, device_id=d, device_id_type=MESH)

    ri = lax.broadcasted_iota(jnp.int32, (LO, LO), 0)
    ci = lax.broadcasted_iota(jnp.int32, (LO, LO), 1)
    h = ((1 - 2 * parity(ri & ci)).astype(F32) * (1.0 / 1024.0)).astype(BF16)
    h = jnp.concatenate([h, h, h], axis=1)

    def butterfly(i):
        fetch(i).wait()
        rows = pl.ds(pl.multiple_of(i * 8, 8), 8)
        for bt in range(LO // 128):
            v = []
            for u in range(NU):
                at = u * LO + bt * 128
                v.append(xv[rows, at : at + 128] * sgv[at // 128 : at // 128 + 1, :])
            step = 1
            while step < NU:
                for u in range(NU):
                    if not u & step:
                        v[u], v[u + step] = v[u] + v[u + step], v[u] - v[u + step]
                step *= 2
            for u in range(NU):
                at = u * LO + bt * 128
                xv[rows, at : at + 128] = v[u]

    loop(0, 8, butterfly)

    def lower(g):
        parts = []
        for i in range(2):
            for top in (0, NU // 2):
                at = (2 * g + i + top) * LO
                v = xv[:, at : at + LO]
                hi = v.astype(BF16)
                rest = v - hi.astype(F32)
                mid = rest.astype(BF16)
                low = (rest - mid.astype(F32)).astype(BF16)
                parts.append(jnp.concatenate([hi, mid, low], axis=1))
        w = jnp.concatenate(parts, axis=0)
        o = lax.dot_general(h, w, (((1,), (1,)), ((), ())), preferred_element_type=F32)
        for i in range(2):
            part = o[:, 128 * i : 128 * i + 128]
            at = (2 * g + i) * LO
            t[at : at + LO, :] = part
            t[at + LOCAL : at + LOCAL + LO, :] = part
            t[at + HALF : at + HALF + LO, :] = pltpu.roll(part, 64, 1)

    for g in range(NU // 4):
        lower(g)

    place_rows.wait()
    pl.semaphore_wait(barrier, 53)

    left = lax.broadcasted_iota(jnp.int32, (8, 128), 1) < 64
    sub = lax.broadcasted_iota(jnp.int32, (8, 128), 0)
    table = t.reshape(LOCAL + HALF, 1, 128)

    def pick(out, k, cq):
        zq = (z + away(k)) & 7

        def body(i, carry):
            q = zq * 16 + i * 2 + cq
            sign = (1 - 2 * parity(row & q)).astype(F32)
            for top in (0, 8):
                v = None
                for j in range(8):
                    a = jnp.broadcast_to(table[idx[q * 32 + top + j]], (8, 128))
                    b = jnp.broadcast_to(table[idx[q * 32 + 16 + top + j] + HALF], (8, 128))
                    r = jnp.where(left, a, b)
                    v = r if v is None else jnp.where(sub == j, r, v)
                out[k, pl.ds(pl.multiple_of(i * 16, 16) + top, 8), :] = v * sign
            return carry

        lax.fori_loop(0, 8, body, 0, unroll=8)

    def remote(src, dst, ss, rs, device):
        return pltpu.make_async_remote_copy(
            src_ref=src, dst_ref=dst, send_sem=ss, recv_sem=rs,
            device_id=device, device_id_type=MESH,
        )

    def all_of(ref, ss, rs):
        return remote(ref, ref, ss, rs, near(0, 0, 1))

    def block(i):
        return pl.ds(pl.multiple_of(i * 32, 32), 32)

    def to_core(k):
        return remote(zo.at[k], rc.at[k], cs, cr.at[k], near(0, 0, 1))

    def to_y(k, d):
        return remote(acc.at[k, block((y + d) & 3)], ry.at[k - 2, d - 1], ys, yr.at[k - 2], near(d, 0, 0))

    def quarter(k, i):
        return acc.at[k, pl.ds(pl.multiple_of(y * 32 + (i & 1) * 16 + (i >> 1) * 8, 8), 8)]

    def to_z(k, zq, d):
        device = {"row": zq * 16 + y_at[0] + x_at[d][0] + c, "col": x_at[d][1]}
        return remote(quarter(k, (x + d) & 3), rz.at[(k - 2) * 4 + x], zs, zr, device)

    def to_first(k):
        return remote(acc.at[k], rf.at[k], fs, fr, along_z(away(k)))

    def pick_other(k):
        pick(zo, k, 1 - c)
        to_core(k).start()

    def send_y(k):
        for d in (2, 1, 3):
            to_y(k, d).start()

    def pick_own(k):
        pick(acc, k, c)
        to_core(k).wait_recv()
        acc[k] = acc[k] + rc[k]
        pl.when(k < 2)(lambda: to_first(k).start())
        pl.when((k >= 2) & (k < 7))(lambda: send_y(k))

    def add_y(k):
        all_of(ry.at[k - 2], ys, yr.at[k - 2]).wait_recv()
        mine = block(y)
        acc[k, mine] = (acc[k, mine] + ry[k - 2, 0]) + (ry[k - 2, 1] + ry[k - 2, 2])

    def pass_z(k):
        add_y(k)
        zq = (z + away(k)) & 7
        for d in (2, 1, 3, 0):
            to_z(k, zq, d).start()

    loop(0, 8, pick_other)
    loop(0, 8, pick_own)
    all_of(rf, fs, fr).wait_recv()
    acc[7] = acc[7] + (rf[0] + rf[1])
    send_y(7)
    loop(2, 7, pass_z)
    add_y(7)
    for d in (2, 1, 3):
        to_z(7, z, d).start()
    rz[20 + x] = quarter(7, x)[...]
    all_of(zo, cs, cr.at[0]).wait_send()
    all_of(rf, fs, fr).wait_send()
    all_of(ry, ys, yr.at[0]).wait_send()
    others = all_of(rz.at[pl.ds(0, 23)], zs, zr)
    others.wait_recv()

    def total(i):
        v = [rz[4 * k + i] for k in range(6)] + [rz[4 * k + i + 1] for k in range(6)]
        while len(v) > 1:
            v = [v[j] + v[j + 1] if j + 1 < len(v) else v[j] for j in range(0, len(v), 2)]
        return v[0]

    a0, a1 = total(0), total(2)
    first = jnp.concatenate([a0[:, :64], a1[:, :64]], axis=1)
    second = jnp.concatenate([a0[:, 64:], a1[:, 64:]], axis=1)
    m = jnp.concatenate([first, second], axis=0)
    g = jnp.dot(m.T, m, preferred_element_type=F32, precision=lax.Precision.HIGHEST)
    for e in range(32):
        gs[e] = g[4 * e : 4 * e + 4]

    place = x * 8 + y * 2 + c

    def to_gs(i):
        dy, dx, dc = plane[i]
        e = ((x + dx) & 3) * 8 + ((y + dy) & 3) * 2 + c_at[dc]
        return remote(gs.at[e], gr.at[i], gss, gsr, near(dy, dx, dc))

    to_mate = remote(mx.at[x >> 1], mx.at[x >> 1], xs, xr, near(0, 2, 0))

    def to_gz(d):
        return remote(gz.at[z], gz.at[z], gzs, gzr, near(0, 0, 0, d))

    def to_gf(i):
        return remote(gf.at[place], gf.at[place], gfs, gfr, near(*plane[i]))

    for i in range(31):
        to_gs(i).start()
    mx[x >> 1] = m
    to_mate.start()
    others.wait_send()
    all_of(gr, gss, gsr).wait_recv()
    v = [gr[i] for i in range(31)] + [gs[place]]
    while len(v) > 1:
        v = [v[j] + v[j + 1] for j in range(0, len(v), 2)]
    gz[z] = v[0]
    for d in z_order:
        to_gz(d).start()
    all_of(gr, gss, gsr).wait_send()
    to_mate.wait()
    for i in range(2):
        for j in range(2):
            both_out[128 + 16 * j + 8 * i : 136 + 16 * j + 8 * i, :] = mx[i, 8 * j : 8 * j + 8]
    all_of(gz.at[pl.ds(0, 7)], gzs, gzr).wait_recv()
    gf[place] = (((gz[0] + gz[1]) + (gz[2] + gz[3])) + ((gz[4] + gz[5]) + (gz[6] + gz[7]))) * (1.0 / 4096.0)
    for i in range(31):
        to_gf(i).start()
    all_of(gz.at[pl.ds(0, 7)], gzs, gzr).wait_send()
    all_of(gf.at[pl.ds(0, 31)], gfs, gfr).wait_recv()
    for e in range(32):
        both_out[e * 4 : (e + 1) * 4, :] = gf[e]
    all_of(gf.at[pl.ds(0, 31)], gfs, gfr).wait_send()


def mix(panel, signs, rows):
    vm = pl.BlockSpec(memory_space=pltpu.VMEM)
    hbm = pl.BlockSpec(memory_space=pltpu.HBM)
    V = pltpu.VMEM
    D = pltpu.SemaphoreType.DMA
    return pl.pallas_call(
        mix_kernel,
        out_shape=jax.ShapeDtypeStruct((160, 128), F32),
        in_specs=[hbm, vm],
        out_specs=vm,
        scratch_shapes=[
            V((64, LOCAL), F32),
            V((LOCAL // 128, 128), F32),
            V((4096,), jnp.int32),
            pltpu.SMEM((4096,), jnp.int32),
            V((LOCAL + HALF, 128), F32),
            V((8, 128, 128), F32),
            V((8, 128, 128), F32),
            V((8, 128, 128), F32),
            V((2, 128, 128), F32),
            V((6, 3, 32, 128), F32),
            V((24, 8, 128), F32),
            V((2, 16, 128), F32),
            V((32, 4, 128), F32),
            V((31, 4, 128), F32),
            V((8, 4, 128), F32),
            V((32, 4, 128), F32),
            D((9,)),
            D, D((8,)), D, D, D, D((6,)), D, D, D, D, D, D, D, D, D, D,
        ],
        compiler_params=pltpu.CompilerParams(
            collective_id=0, has_side_effects=True, vmem_limit_bytes=52 << 20
        ),
        name="mix",
    )(panel, jnp.concatenate([signs, rows]))


def rows_const(v, j):
    return jnp.broadcast_to(v[:, j : j + 1], (8, 128))


def factor_kernel(both_ref, basis_ref, tri_ref, a_ref, u_ref):
    n, width = 128, 32
    col = lax.axis_index("col")
    a_ref[:, :128] = both_ref[:128, :]
    samples = jnp.concatenate([both_ref[128:, :], jnp.zeros((96, 128), F32)], axis=0)
    a_ref[:, 128:] = samples.T
    lane = lax.broadcasted_iota(jnp.int32, (8, 128), 1)
    for panel in range(n // width):
        top = panel * width
        nb = width // 8
        blocks = [
            [a_ref[top + 8 * i : top + 8 * i + 8, 128 * t : 128 * t + 128] for t in range(2)]
            for i in range(nb)
        ]
        for j in range(nb):
            at = top + 8 * j
            rows = [
                [jnp.broadcast_to(blocks[j][t][k : k + 1, :], (8, 128)) for t in range(2)]
                for k in range(8)
            ]
            d = {(i, k): rows_const(rows[i][0], at + k) for i in range(8) for k in range(i + 1)}
            below = [[rows_const(blocks[i][0], at + k) for k in range(8)] for i in range(j + 1, nb)]
            for k in range(8):
                r = lax.rsqrt(d[k, k])
                for i in range(k + 1, 8):
                    d[i, k] = d[i, k] * r
                for i in range(k + 1, 8):
                    for q in range(k + 1, i + 1):
                        d[i, q] = d[i, q] - d[i, k] * d[q, k]
                for t in range(2):
                    rows[k][t] = rows[k][t] * r
                    for q in range(k + 1, 8):
                        rows[q][t] = rows[q][t] - d[q, k] * rows[k][t]
                for b in below:
                    b[k] = b[k] * r
                    for q in range(k + 1, 8):
                        b[q] = b[q] - d[q, k] * b[k]
            for k in range(8):
                keep = lane >= at + k
                u_ref[at + k : at + k + 1, :128] = jnp.where(keep, rows[k][0], 0.0)[:1]
                u_ref[at + k : at + k + 1, 128:] = rows[k][1][:1]
            for i in range(j + 1, nb):
                b = below[i - j - 1]
                for t in range(2):
                    v = blocks[i][t]
                    for k in range(8):
                        v = v - b[k] * rows[k][t]
                    blocks[i][t] = v
        if top + width < n:
            rest = top + width
            u = u_ref[top:rest, :]
            hi = u.astype(BF16)
            low = u - hi.astype(F32)
            mid = low.astype(BF16)
            low = (low - mid.astype(F32)).astype(BF16)
            left = jnp.concatenate([v[:, :128] for v in (hi, hi, mid, hi, low, mid)], axis=0)
            right = jnp.concatenate([hi, mid, hi, low, hi, mid], axis=0)
            upd = jnp.dot(left.T[rest:, :], right, preferred_element_type=F32)
            a_ref[rest:, :] = a_ref[rest:, :] - upd
    half = pl.ds(pl.multiple_of(col * 64, 64), 64)
    tri_ref[...] = u_ref[half, :128]
    basis_ref[...] = u_ref[half, 128:].T[:32]


def factor(both):
    vm = pl.BlockSpec(memory_space=pltpu.VMEM)
    return pl.pallas_call(
        factor_kernel,
        out_shape=(jax.ShapeDtypeStruct((32, 64), F32), jax.ShapeDtypeStruct((64, 128), F32)),
        in_specs=[vm],
        out_specs=(vm, vm),
        scratch_shapes=[pltpu.VMEM((128, 256), F32), pltpu.VMEM((128, 256), F32)],
        compiler_params=pltpu.CompilerParams(vmem_limit_bytes=16 << 20),
        name="factor",
    )(both)


def shards(tall_panel_array, row_signs, sample_rows):
    basis, upper = factor(mix(tall_panel_array, row_signs, sample_rows))
    return basis.T, upper


def solution(mesh):
    return jax.shard_map(
        shards,
        mesh=mesh,
        in_specs=(P("col", "row"), P("row"), P()),
        out_specs=(P("col", "row"), P("col", None)),
        check_vma=False,
    )
```

```python
import jax
import jax.numpy as jnp
from jax import lax
from jax.experimental import pallas as pl
from jax.experimental.pallas import tpu as pltpu
from jax.sharding import PartitionSpec as P

F32 = jnp.float32
BF16 = jnp.bfloat16
MESH = pl.DeviceIdType.MESH
LO = 256
NU = 32
LOCAL = LO * NU
HALF = LOCAL // 2


def parity(bits):
    bits = bits ^ (bits >> 4)
    bits = bits ^ (bits >> 2)
    bits = bits ^ (bits >> 1)
    return bits & 1


def away(k):
    b = (k + 6) & 7
    return 4 + (b >> 1) * (1 - 2 * (b & 1)) - (b & 1) + ((b + 1) >> 3) - ((k + 1) >> 3)


def mix_kernel(
    x_hbm, ints, both_out,
    xv, sgv, idxv, idx, t, zo, acc, rc, rf, ry, rz, mx, gs, gr, gz, gf,
    in_sem, cs, cr, fs, fr, ys, yr, zs, zr, xs, xr, gss, gsr, gzs, gzr, gfs, gfr,
):
    row, col = lax.axis_index("row"), lax.axis_index("col")
    c = row & 1
    y = (row >> 2) & 3
    z = row >> 4
    x = col * 2 + ((row >> 1) & 1)

    y_at = [((y + d) & 3) * 4 for d in range(4)]
    x_at = [(((x + d) & 1) * 2, ((x + d) & 3) >> 1) for d in range(4)]
    c_at = [c, 1 - c]
    z_at = [((z + d) & 7) * 16 for d in range(8)]

    def near(dy, dx, dc, dz=0):
        return {"row": z_at[dz] + y_at[dy] + x_at[dx][0] + c_at[dc], "col": x_at[dx][1]}

    def along_z(d):
        return {"row": ((z + d) & 7) * 16 + (row & 15), "col": col}

    plane = [(dy, dx, dc) for dy in (2, 1, 3, 0) for dx in (2, 1, 3, 0) for dc in (1, 0) if dy or dx or dc]
    z_order = (4, 3, 5, 2, 6, 1, 7)

    def loop(first, last, body):
        def step(i, carry):
            body(i)
            return carry

        lax.fori_loop(first, last, step, 0)

    place_rows = pltpu.make_async_copy(idxv, idx, in_sem.at[8])

    def fetch(i):
        at = pl.ds(pl.multiple_of(i * 8, 8), 8)
        return pltpu.make_async_copy(x_hbm.at[at], xv.at[at], in_sem.at[i])

    loop(0, 8, lambda i: fetch(i).start())
    idxv[...] = ints[pl.ds(LOCAL, 4096)] & (LOCAL - 1)
    place_rows.start()
    sgv[...] = ints[pl.ds(0, LOCAL)].reshape(LOCAL // 128, 128).astype(F32)

    barrier = pltpu.get_barrier_semaphore()
    for d in [near(*i) for i in plane] + [near(0, i, 0, d) for d in z_order for i in range(4 if 1 < d < 7 else 1)]:
        pl.semaphore_signal(barrier, inc=1, device_id=d, device_id_type=MESH)

    ri = lax.broadcasted_iota(jnp.int32, (LO, LO), 0)
    ci = lax.broadcasted_iota(jnp.int32, (LO, LO), 1)
    h = ((1 - 2 * parity(ri & ci)).astype(F32) * (1.0 / 1024.0)).astype(BF16)
    h = jnp.concatenate([h, h, h], axis=1)

    def butterfly(i):
        fetch(i).wait()
        rows = pl.ds(pl.multiple_of(i * 8, 8), 8)
        for bt in range(LO // 128):
            v = []
            for u in range(NU):
                at = u * LO + bt * 128
                v.append(xv[rows, at : at + 128] * sgv[at // 128 : at // 128 + 1, :])
            step = 1
            while step < NU:
                for u in range(NU):
                    if not u & step:
                        v[u], v[u + step] = v[u] + v[u + step], v[u] - v[u + step]
                step *= 2
            for u in range(NU):
                at = u * LO + bt * 128
                xv[rows, at : at + 128] = v[u]

    loop(0, 8, butterfly)

    def lower(g):
        parts = []
        for i in range(2):
            for top in (0, NU // 2):
                at = (2 * g + i + top) * LO
                v = xv[:, at : at + LO]
                hi = v.astype(BF16)
                rest = v - hi.astype(F32)
                mid = rest.astype(BF16)
                low = (rest - mid.astype(F32)).astype(BF16)
                parts.append(jnp.concatenate([hi, mid, low], axis=1))
        w = jnp.concatenate(parts, axis=0)
        o = lax.dot_general(h, w, (((1,), (1,)), ((), ())), preferred_element_type=F32)
        for i in range(2):
            part = o[:, 128 * i : 128 * i + 128]
            at = (2 * g + i) * LO
            t[at : at + LO, :] = part
            t[at + LOCAL : at + LOCAL + LO, :] = part
            t[at + HALF : at + HALF + LO, :] = pltpu.roll(part, 64, 1)

    for g in range(NU // 4):
        lower(g)

    place_rows.wait()
    pl.semaphore_wait(barrier, 53)

    left = lax.broadcasted_iota(jnp.int32, (1, 128), 1) < 64
    table = t.reshape(LOCAL + HALF, 1, 128)

    def pick(out, k, cq):
        zq = (z + away(k)) & 7

        def body(i, carry):
            q = zq * 16 + i * 2 + cq
            sign = (1 - 2 * parity(row & q)).astype(F32)
            for j in range(16):
                a = table[idx[q * 32 + j]]
                b = table[idx[q * 32 + 16 + j] + HALF]
                out[k, pl.ds(pl.multiple_of(i * 16, 16) + j, 1), :] = jnp.where(left, a, b) * sign
            return carry

        lax.fori_loop(0, 8, body, 0, unroll=8)

    def remote(src, dst, ss, rs, device):
        return pltpu.make_async_remote_copy(
            src_ref=src, dst_ref=dst, send_sem=ss, recv_sem=rs,
            device_id=device, device_id_type=MESH,
        )

    def all_of(ref, ss, rs):
        return remote(ref, ref, ss, rs, near(0, 0, 1))

    def block(i):
        return pl.ds(pl.multiple_of(i * 32, 32), 32)

    def to_core(k):
        return remote(zo.at[k], rc.at[k], cs, cr.at[k], near(0, 0, 1))

    def to_y(k, d):
        return remote(acc.at[k, block((y + d) & 3)], ry.at[k - 2, d - 1], ys, yr.at[k - 2], near(d, 0, 0))

    def quarter(k, i):
        return acc.at[k, pl.ds(pl.multiple_of(y * 32 + (i & 1) * 16 + (i >> 1) * 8, 8), 8)]

    def to_z(k, zq, d):
        device = {"row": zq * 16 + y_at[0] + x_at[d][0] + c, "col": x_at[d][1]}
        return remote(quarter(k, (x + d) & 3), rz.at[(k - 2) * 4 + x], zs, zr, device)

    def to_first(k):
        return remote(acc.at[k], rf.at[k], fs, fr, along_z(away(k)))

    def pick_other(k):
        pick(zo, k, 1 - c)
        to_core(k).start()

    def send_y(k):
        for d in (2, 1, 3):
            to_y(k, d).start()

    def pick_own(k):
        pick(acc, k, c)
        to_core(k).wait_recv()
        acc[k] = acc[k] + rc[k]
        pl.when(k < 2)(lambda: to_first(k).start())
        pl.when((k >= 2) & (k < 7))(lambda: send_y(k))

    def add_y(k):
        all_of(ry.at[k - 2], ys, yr.at[k - 2]).wait_recv()
        mine = block(y)
        acc[k, mine] = (acc[k, mine] + ry[k - 2, 0]) + (ry[k - 2, 1] + ry[k - 2, 2])

    def pass_z(k):
        add_y(k)
        zq = (z + away(k)) & 7
        for d in (2, 1, 3, 0):
            to_z(k, zq, d).start()

    loop(0, 8, pick_other)
    loop(0, 8, pick_own)
    all_of(rf, fs, fr).wait_recv()
    acc[7] = acc[7] + (rf[0] + rf[1])
    send_y(7)
    loop(2, 7, pass_z)
    add_y(7)
    for d in (2, 1, 3):
        to_z(7, z, d).start()
    rz[20 + x] = quarter(7, x)[...]
    all_of(zo, cs, cr.at[0]).wait_send()
    all_of(rf, fs, fr).wait_send()
    all_of(ry, ys, yr.at[0]).wait_send()
    others = all_of(rz.at[pl.ds(0, 23)], zs, zr)
    others.wait_recv()

    def total(i):
        v = [rz[4 * k + i] for k in range(6)] + [rz[4 * k + i + 1] for k in range(6)]
        while len(v) > 1:
            v = [v[j] + v[j + 1] if j + 1 < len(v) else v[j] for j in range(0, len(v), 2)]
        return v[0]

    a0, a1 = total(0), total(2)
    first = jnp.concatenate([a0[:, :64], a1[:, :64]], axis=1)
    second = jnp.concatenate([a0[:, 64:], a1[:, 64:]], axis=1)
    m = jnp.concatenate([first, second], axis=0)
    g = jnp.dot(m.T, m, preferred_element_type=F32, precision=lax.Precision.HIGHEST)
    for e in range(32):
        gs[e] = g[4 * e : 4 * e + 4]

    place = x * 8 + y * 2 + c

    def to_gs(i):
        dy, dx, dc = plane[i]
        e = ((x + dx) & 3) * 8 + ((y + dy) & 3) * 2 + c_at[dc]
        return remote(gs.at[e], gr.at[i], gss, gsr, near(dy, dx, dc))

    to_mate = remote(mx.at[x >> 1], mx.at[x >> 1], xs, xr, near(0, 2, 0))

    def to_gz(d):
        return remote(gz.at[z], gz.at[z], gzs, gzr, near(0, 0, 0, d))

    def to_gf(i):
        return remote(gf.at[place], gf.at[place], gfs, gfr, near(*plane[i]))

    for i in range(31):
        to_gs(i).start()
    mx[x >> 1] = m
    to_mate.start()
    others.wait_send()
    all_of(gr, gss, gsr).wait_recv()
    v = [gr[i] for i in range(31)] + [gs[place]]
    while len(v) > 1:
        v = [v[j] + v[j + 1] for j in range(0, len(v), 2)]
    gz[z] = v[0]
    for d in z_order:
        to_gz(d).start()
    all_of(gr, gss, gsr).wait_send()
    to_mate.wait()
    for i in range(2):
        for j in range(2):
            both_out[128 + 16 * j + 8 * i : 136 + 16 * j + 8 * i, :] = mx[i, 8 * j : 8 * j + 8]
    all_of(gz.at[pl.ds(0, 7)], gzs, gzr).wait_recv()
    gf[place] = (((gz[0] + gz[1]) + (gz[2] + gz[3])) + ((gz[4] + gz[5]) + (gz[6] + gz[7]))) * (1.0 / 4096.0)
    for i in range(31):
        to_gf(i).start()
    all_of(gz.at[pl.ds(0, 7)], gzs, gzr).wait_send()
    all_of(gf.at[pl.ds(0, 31)], gfs, gfr).wait_recv()
    for e in range(32):
        both_out[e * 4 : (e + 1) * 4, :] = gf[e]
    all_of(gf.at[pl.ds(0, 31)], gfs, gfr).wait_send()


def mix(panel, signs, rows):
    vm = pl.BlockSpec(memory_space=pltpu.VMEM)
    hbm = pl.BlockSpec(memory_space=pltpu.HBM)
    V = pltpu.VMEM
    D = pltpu.SemaphoreType.DMA
    return pl.pallas_call(
        mix_kernel,
        out_shape=jax.ShapeDtypeStruct((160, 128), F32),
        in_specs=[hbm, vm],
        out_specs=vm,
        scratch_shapes=[
            V((64, LOCAL), F32),
            V((LOCAL // 128, 128), F32),
            V((4096,), jnp.int32),
            pltpu.SMEM((4096,), jnp.int32),
            V((LOCAL + HALF, 128), F32),
            V((8, 128, 128), F32),
            V((8, 128, 128), F32),
            V((8, 128, 128), F32),
            V((2, 128, 128), F32),
            V((6, 3, 32, 128), F32),
            V((24, 8, 128), F32),
            V((2, 16, 128), F32),
            V((32, 4, 128), F32),
            V((31, 4, 128), F32),
            V((8, 4, 128), F32),
            V((32, 4, 128), F32),
            D((9,)),
            D, D((8,)), D, D, D, D((6,)), D, D, D, D, D, D, D, D, D, D,
        ],
        compiler_params=pltpu.CompilerParams(
            collective_id=0, has_side_effects=True, vmem_limit_bytes=52 << 20
        ),
        name="mix",
    )(panel, jnp.concatenate([signs, rows]))


def rows_const(v, j):
    return jnp.broadcast_to(v[:, j : j + 1], (8, 128))


def factor_kernel(both_ref, basis_ref, tri_ref, a_ref, u_ref):
    n, width = 128, 32
    col = lax.axis_index("col")
    a_ref[:, :128] = both_ref[:128, :]
    samples = jnp.concatenate([both_ref[128:, :], jnp.zeros((96, 128), F32)], axis=0)
    a_ref[:, 128:] = samples.T
    lane = lax.broadcasted_iota(jnp.int32, (8, 128), 1)
    for panel in range(n // width):
        top = panel * width
        nb = width // 8
        blocks = [
            [a_ref[top + 8 * i : top + 8 * i + 8, 128 * t : 128 * t + 128] for t in range(2)]
            for i in range(nb)
        ]
        for j in range(nb):
            at = top + 8 * j
            rows = [
                [jnp.broadcast_to(blocks[j][t][k : k + 1, :], (8, 128)) for t in range(2)]
                for k in range(8)
            ]
            d = {(i, k): rows_const(rows[i][0], at + k) for i in range(8) for k in range(i + 1)}
            below = [[rows_const(blocks[i][0], at + k) for k in range(8)] for i in range(j + 1, nb)]
            for k in range(8):
                r = lax.rsqrt(d[k, k])
                for i in range(k + 1, 8):
                    d[i, k] = d[i, k] * r
                for i in range(k + 1, 8):
                    for q in range(k + 1, i + 1):
                        d[i, q] = d[i, q] - d[i, k] * d[q, k]
                for t in range(2):
                    rows[k][t] = rows[k][t] * r
                    for q in range(k + 1, 8):
                        rows[q][t] = rows[q][t] - d[q, k] * rows[k][t]
                for b in below:
                    b[k] = b[k] * r
                    for q in range(k + 1, 8):
                        b[q] = b[q] - d[q, k] * b[k]
            for k in range(8):
                keep = lane >= at + k
                u_ref[at + k : at + k + 1, :128] = jnp.where(keep, rows[k][0], 0.0)[:1]
                u_ref[at + k : at + k + 1, 128:] = rows[k][1][:1]
            for i in range(j + 1, nb):
                b = below[i - j - 1]
                for t in range(2):
                    v = blocks[i][t]
                    for k in range(8):
                        v = v - b[k] * rows[k][t]
                    blocks[i][t] = v
        if top + width < n:
            rest = top + width
            u = u_ref[top:rest, :]
            hi = u.astype(BF16)
            low = u - hi.astype(F32)
            mid = low.astype(BF16)
            low = (low - mid.astype(F32)).astype(BF16)
            left = jnp.concatenate([v[:, :128] for v in (hi, hi, mid, hi, low, mid)], axis=0)
            right = jnp.concatenate([hi, mid, hi, low, hi, mid], axis=0)
            upd = jnp.dot(left.T[rest:, :], right, preferred_element_type=F32)
            a_ref[rest:, :] = a_ref[rest:, :] - upd
    half = pl.ds(pl.multiple_of(col * 64, 64), 64)
    tri_ref[...] = u_ref[half, :128]
    basis_ref[...] = u_ref[half, 128:].T[:32]


def factor(both):
    vm = pl.BlockSpec(memory_space=pltpu.VMEM)
    return pl.pallas_call(
        factor_kernel,
        out_shape=(jax.ShapeDtypeStruct((32, 64), F32), jax.ShapeDtypeStruct((64, 128), F32)),
        in_specs=[vm],
        out_specs=(vm, vm),
        scratch_shapes=[pltpu.VMEM((128, 256), F32), pltpu.VMEM((128, 256), F32)],
        compiler_params=pltpu.CompilerParams(vmem_limit_bytes=16 << 20),
        name="factor",
    )(both)


def shards(tall_panel_array, row_signs, sample_rows):
    basis, upper = factor(mix(tall_panel_array, row_signs, sample_rows))
    return basis.T, upper


def solution(mesh):
    return jax.shard_map(
        shards,
        mesh=mesh,
        in_specs=(P("col", "row"), P("row"), P()),
        out_specs=(P("col", "row"), P("col", None)),
        check_vma=False,
    )
```

```python
import jax
import jax.numpy as jnp
from jax import lax
from jax.experimental import pallas as pl
from jax.experimental.pallas import tpu as pltpu
from jax.sharding import PartitionSpec as P

F32 = jnp.float32
BF16 = jnp.bfloat16
MESH = pl.DeviceIdType.MESH
LO = 256
NU = 32
LOCAL = LO * NU
HALF = LOCAL // 2


def parity(bits):
    bits = bits ^ (bits >> 4)
    bits = bits ^ (bits >> 2)
    bits = bits ^ (bits >> 1)
    return bits & 1


def away(k):
    b = (k + 6) & 7
    return 4 + (b >> 1) * (1 - 2 * (b & 1)) - (b & 1) + ((b + 1) >> 3) - ((k + 1) >> 3)


def mix_kernel(
    x_hbm, ints, both_out,
    xv, sgv, idxv, idx, t, zo, acc, rc, rf, ry, rz, mx, gs, gr, gz, gf,
    in_sem, cs, cr, fs, fr, ys, yr, zs, zr, xs, xr, gss, gsr, gzs, gzr, gfs, gfr,
):
    row, col = lax.axis_index("row"), lax.axis_index("col")
    c = row & 1
    y = (row >> 2) & 3
    z = row >> 4
    x = col * 2 + ((row >> 1) & 1)

    y_at = [((y + d) & 3) * 4 for d in range(4)]
    x_at = [(((x + d) & 1) * 2, ((x + d) & 3) >> 1) for d in range(4)]
    c_at = [c, 1 - c]
    z_at = [((z + d) & 7) * 16 for d in range(8)]

    def near(dy, dx, dc, dz=0):
        return {"row": z_at[dz] + y_at[dy] + x_at[dx][0] + c_at[dc], "col": x_at[dx][1]}

    def along_z(d):
        return {"row": ((z + d) & 7) * 16 + (row & 15), "col": col}

    plane = [(dy, dx, dc) for dy in (2, 1, 3, 0) for dx in (2, 1, 3, 0) for dc in (1, 0) if dy or dx or dc]
    z_order = (4, 3, 5, 2, 6, 1, 7)

    def loop(first, last, body):
        def step(i, carry):
            body(i)
            return carry

        lax.fori_loop(first, last, step, 0)

    place_rows = pltpu.make_async_copy(idxv, idx, in_sem.at[8])

    def fetch(i):
        at = pl.ds(pl.multiple_of(i * 8, 8), 8)
        return pltpu.make_async_copy(x_hbm.at[at], xv.at[at], in_sem.at[i])

    loop(0, 8, lambda i: fetch(i).start())
    idxv[...] = ints[pl.ds(LOCAL, 4096)] & (LOCAL - 1)
    place_rows.start()
    sgv[...] = ints[pl.ds(0, LOCAL)].reshape(LOCAL // 128, 128).astype(F32)

    barrier = pltpu.get_barrier_semaphore()

    def greet(i):
        plane_row = z_at[0] + ((y + (i >> 1)) & 3) * 4 + ((c + i) & 1)
        line_row = ((z + i) & 7) * 16 + y_at[0] + c
        for first in (plane_row, line_row):
            for d in range(4):
                device = {"row": first + x_at[d][0], "col": x_at[d][1]}
                pl.semaphore_signal(barrier, inc=1, device_id=device, device_id_type=MESH)

    ri = lax.broadcasted_iota(jnp.int32, (LO, LO), 0)
    ci = lax.broadcasted_iota(jnp.int32, (LO, LO), 1)
    h = ((1 - 2 * parity(ri & ci)).astype(F32) * (1.0 / 1024.0)).astype(BF16)
    h = jnp.concatenate([h, h, h], axis=1)

    def butterfly(i):
        fetch(i).wait()
        greet(i)
        rows = pl.ds(pl.multiple_of(i * 8, 8), 8)
        for bt in range(LO // 128):
            v = []
            for u in range(NU):
                at = u * LO + bt * 128
                v.append(xv[rows, at : at + 128] * sgv[at // 128 : at // 128 + 1, :])
            step = 1
            while step < NU:
                for u in range(NU):
                    if not u & step:
                        v[u], v[u + step] = v[u] + v[u + step], v[u] - v[u + step]
                step *= 2
            for u in range(NU):
                at = u * LO + bt * 128
                xv[rows, at : at + 128] = v[u]

    loop(0, 8, butterfly)

    def lower(g):
        parts = []
        for i in range(2):
            for top in (0, NU // 2):
                at = (2 * g + i + top) * LO
                v = xv[:, at : at + LO]
                hi = v.astype(BF16)
                rest = v - hi.astype(F32)
                mid = rest.astype(BF16)
                low = (rest - mid.astype(F32)).astype(BF16)
                parts.append(jnp.concatenate([hi, mid, low], axis=1))
        w = jnp.concatenate(parts, axis=0)
        o = lax.dot_general(h, w, (((1,), (1,)), ((), ())), preferred_element_type=F32)
        for i in range(2):
            part = o[:, 128 * i : 128 * i + 128]
            at = (2 * g + i) * LO
            t[at : at + LO, :] = part
            t[at + LOCAL : at + LOCAL + LO, :] = part
            t[at + HALF : at + HALF + LO, :] = pltpu.roll(part, 64, 1)

    for g in range(NU // 4):
        lower(g)

    place_rows.wait()
    pl.semaphore_wait(barrier, 64)

    left = lax.broadcasted_iota(jnp.int32, (8, 128), 1) < 64
    sub = lax.broadcasted_iota(jnp.int32, (8, 128), 0)
    table = t.reshape(LOCAL + HALF, 1, 128)

    def pick(out, k, cq):
        zq = (z + away(k)) & 7

        def body(i, carry):
            q = zq * 16 + i * 2 + cq
            sign = (1 - 2 * parity(row & q)).astype(F32)
            for top in (0, 8):
                v = None
                for j in range(8):
                    a = jnp.broadcast_to(table[idx[q * 32 + top + j]], (8, 128))
                    b = jnp.broadcast_to(table[idx[q * 32 + 16 + top + j] + HALF], (8, 128))
                    r = jnp.where(left, a, b)
                    v = r if v is None else jnp.where(sub == j, r, v)
                out[k, pl.ds(pl.multiple_of(i * 16, 16) + top, 8), :] = v * sign
            return carry

        lax.fori_loop(0, 8, body, 0, unroll=8)

    def remote(src, dst, ss, rs, device):
        return pltpu.make_async_remote_copy(
            src_ref=src, dst_ref=dst, send_sem=ss, recv_sem=rs,
            device_id=device, device_id_type=MESH,
        )

    def all_of(ref, ss, rs):
        return remote(ref, ref, ss, rs, near(0, 0, 1))

    def block(i):
        return pl.ds(pl.multiple_of(i * 32, 32), 32)

    def to_core(k):
        return remote(zo.at[k], rc.at[k], cs, cr.at[k], near(0, 0, 1))

    def to_y(k, d):
        return remote(acc.at[k, block((y + d) & 3)], ry.at[k - 2, d - 1], ys, yr.at[k - 2], near(d, 0, 0))

    def quarter(k, i):
        return acc.at[k, pl.ds(pl.multiple_of(y * 32 + (i & 1) * 16 + (i >> 1) * 8, 8), 8)]

    def to_z(k, zq, d):
        device = {"row": zq * 16 + y_at[0] + x_at[d][0] + c, "col": x_at[d][1]}
        return remote(quarter(k, (x + d) & 3), rz.at[(k - 2) * 4 + x], zs, zr, device)

    def to_first(k):
        return remote(acc.at[k], rf.at[k], fs, fr, along_z(away(k)))

    def pick_other(k):
        pick(zo, k, 1 - c)
        to_core(k).start()

    def send_y(k):
        for d in (2, 1, 3):
            to_y(k, d).start()

    def pick_own(k):
        pick(acc, k, c)
        to_core(k).wait_recv()
        acc[k] = acc[k] + rc[k]
        pl.when(k < 2)(lambda: to_first(k).start())
        pl.when((k >= 2) & (k < 7))(lambda: send_y(k))

    def add_y(k):
        all_of(ry.at[k - 2], ys, yr.at[k - 2]).wait_recv()
        mine = block(y)
        acc[k, mine] = (acc[k, mine] + ry[k - 2, 0]) + (ry[k - 2, 1] + ry[k - 2, 2])

    def pass_z(k):
        add_y(k)
        zq = (z + away(k)) & 7
        for d in (2, 1, 3, 0):
            to_z(k, zq, d).start()

    loop(0, 8, pick_other)
    loop(0, 8, pick_own)
    all_of(rf, fs, fr).wait_recv()
    acc[7] = acc[7] + (rf[0] + rf[1])
    send_y(7)
    loop(2, 7, pass_z)
    add_y(7)
    for d in (2, 1, 3):
        to_z(7, z, d).start()
    rz[20 + x] = quarter(7, x)[...]
    all_of(zo, cs, cr.at[0]).wait_send()
    all_of(rf, fs, fr).wait_send()
    all_of(ry, ys, yr.at[0]).wait_send()
    others = all_of(rz.at[pl.ds(0, 23)], zs, zr)
    others.wait_recv()

    def total(i):
        v = [rz[4 * k + i] for k in range(6)] + [rz[4 * k + i + 1] for k in range(6)]
        while len(v) > 1:
            v = [v[j] + v[j + 1] if j + 1 < len(v) else v[j] for j in range(0, len(v), 2)]
        return v[0]

    a0, a1 = total(0), total(2)
    first = jnp.concatenate([a0[:, :64], a1[:, :64]], axis=1)
    second = jnp.concatenate([a0[:, 64:], a1[:, 64:]], axis=1)
    m = jnp.concatenate([first, second], axis=0)
    g = jnp.dot(m.T, m, preferred_element_type=F32, precision=lax.Precision.HIGHEST)
    for e in range(32):
        gs[e] = g[4 * e : 4 * e + 4]

    place = x * 8 + y * 2 + c

    def to_gs(i):
        dy, dx, dc = plane[i]
        e = ((x + dx) & 3) * 8 + ((y + dy) & 3) * 2 + c_at[dc]
        return remote(gs.at[e], gr.at[i], gss, gsr, near(dy, dx, dc))

    to_mate = remote(mx.at[x >> 1], mx.at[x >> 1], xs, xr, near(0, 2, 0))

    def to_gz(d):
        return remote(gz.at[z], gz.at[z], gzs, gzr, near(0, 0, 0, d))

    def to_gf(i):
        return remote(gf.at[place], gf.at[place], gfs, gfr, near(*plane[i]))

    for i in range(31):
        to_gs(i).start()
    mx[x >> 1] = m
    to_mate.start()
    others.wait_send()
    all_of(gr, gss, gsr).wait_recv()
    v = [gr[i] for i in range(31)] + [gs[place]]
    while len(v) > 1:
        v = [v[j] + v[j + 1] for j in range(0, len(v), 2)]
    gz[z] = v[0]
    for d in z_order:
        to_gz(d).start()
    all_of(gr, gss, gsr).wait_send()
    to_mate.wait()
    for i in range(2):
        for j in range(2):
            both_out[128 + 16 * j + 8 * i : 136 + 16 * j + 8 * i, :] = mx[i, 8 * j : 8 * j + 8]
    all_of(gz.at[pl.ds(0, 7)], gzs, gzr).wait_recv()
    gf[place] = (((gz[0] + gz[1]) + (gz[2] + gz[3])) + ((gz[4] + gz[5]) + (gz[6] + gz[7]))) * (1.0 / 4096.0)
    for i in range(31):
        to_gf(i).start()
    all_of(gz.at[pl.ds(0, 7)], gzs, gzr).wait_send()
    all_of(gf.at[pl.ds(0, 31)], gfs, gfr).wait_recv()
    for e in range(32):
        both_out[e * 4 : (e + 1) * 4, :] = gf[e]
    all_of(gf.at[pl.ds(0, 31)], gfs, gfr).wait_send()


def mix(panel, signs, rows):
    vm = pl.BlockSpec(memory_space=pltpu.VMEM)
    hbm = pl.BlockSpec(memory_space=pltpu.HBM)
    V = pltpu.VMEM
    D = pltpu.SemaphoreType.DMA
    return pl.pallas_call(
        mix_kernel,
        out_shape=jax.ShapeDtypeStruct((160, 128), F32),
        in_specs=[hbm, vm],
        out_specs=vm,
        scratch_shapes=[
            V((64, LOCAL), F32),
            V((LOCAL // 128, 128), F32),
            V((4096,), jnp.int32),
            pltpu.SMEM((4096,), jnp.int32),
            V((LOCAL + HALF, 128), F32),
            V((8, 128, 128), F32),
            V((8, 128, 128), F32),
            V((8, 128, 128), F32),
            V((2, 128, 128), F32),
            V((6, 3, 32, 128), F32),
            V((24, 8, 128), F32),
            V((2, 16, 128), F32),
            V((32, 4, 128), F32),
            V((31, 4, 128), F32),
            V((8, 4, 128), F32),
            V((32, 4, 128), F32),
            D((9,)),
            D, D((8,)), D, D, D, D((6,)), D, D, D, D, D, D, D, D, D, D,
        ],
        compiler_params=pltpu.CompilerParams(
            collective_id=0, has_side_effects=True, vmem_limit_bytes=52 << 20
        ),
        name="mix",
    )(panel, jnp.concatenate([signs, rows]))


def rows_const(v, j):
    return jnp.broadcast_to(v[:, j : j + 1], (8, 128))


def factor_kernel(both_ref, basis_ref, tri_ref, a_ref, u_ref):
    n, width = 128, 32
    col = lax.axis_index("col")
    a_ref[:, :128] = both_ref[:128, :]
    samples = jnp.concatenate([both_ref[128:, :], jnp.zeros((96, 128), F32)], axis=0)
    a_ref[:, 128:] = samples.T
    lane = lax.broadcasted_iota(jnp.int32, (8, 128), 1)
    for panel in range(n // width):
        top = panel * width
        nb = width // 8
        blocks = [
            [a_ref[top + 8 * i : top + 8 * i + 8, 128 * t : 128 * t + 128] for t in range(2)]
            for i in range(nb)
        ]
        for j in range(nb):
            at = top + 8 * j
            rows = [
                [jnp.broadcast_to(blocks[j][t][k : k + 1, :], (8, 128)) for t in range(2)]
                for k in range(8)
            ]
            d = {(i, k): rows_const(rows[i][0], at + k) for i in range(8) for k in range(i + 1)}
            below = [[rows_const(blocks[i][0], at + k) for k in range(8)] for i in range(j + 1, nb)]
            for k in range(8):
                r = lax.rsqrt(d[k, k])
                for i in range(k + 1, 8):
                    d[i, k] = d[i, k] * r
                for i in range(k + 1, 8):
                    for q in range(k + 1, i + 1):
                        d[i, q] = d[i, q] - d[i, k] * d[q, k]
                for t in range(2):
                    rows[k][t] = rows[k][t] * r
                    for q in range(k + 1, 8):
                        rows[q][t] = rows[q][t] - d[q, k] * rows[k][t]
                for b in below:
                    b[k] = b[k] * r
                    for q in range(k + 1, 8):
                        b[q] = b[q] - d[q, k] * b[k]
            for k in range(8):
                keep = lane >= at + k
                u_ref[at + k : at + k + 1, :128] = jnp.where(keep, rows[k][0], 0.0)[:1]
                u_ref[at + k : at + k + 1, 128:] = rows[k][1][:1]
            for i in range(j + 1, nb):
                b = below[i - j - 1]
                for t in range(2):
                    v = blocks[i][t]
                    for k in range(8):
                        v = v - b[k] * rows[k][t]
                    blocks[i][t] = v
        if top + width < n:
            rest = top + width
            u = u_ref[top:rest, :]
            hi = u.astype(BF16)
            low = u - hi.astype(F32)
            mid = low.astype(BF16)
            low = (low - mid.astype(F32)).astype(BF16)
            left = jnp.concatenate([v[:, :128] for v in (hi, hi, mid, hi, low, mid)], axis=0)
            right = jnp.concatenate([hi, mid, hi, low, hi, mid], axis=0)
            upd = jnp.dot(left.T[rest:, :], right, preferred_element_type=F32)
            a_ref[rest:, :] = a_ref[rest:, :] - upd
    half = pl.ds(pl.multiple_of(col * 64, 64), 64)
    tri_ref[...] = u_ref[half, :128]
    basis_ref[...] = u_ref[half, 128:].T[:32]


def factor(both):
    vm = pl.BlockSpec(memory_space=pltpu.VMEM)
    return pl.pallas_call(
        factor_kernel,
        out_shape=(jax.ShapeDtypeStruct((32, 64), F32), jax.ShapeDtypeStruct((64, 128), F32)),
        in_specs=[vm],
        out_specs=(vm, vm),
        scratch_shapes=[pltpu.VMEM((128, 256), F32), pltpu.VMEM((128, 256), F32)],
        compiler_params=pltpu.CompilerParams(vmem_limit_bytes=16 << 20),
        name="factor",
    )(both)


def shards(tall_panel_array, row_signs, sample_rows):
    basis, upper = factor(mix(tall_panel_array, row_signs, sample_rows))
    return basis.T, upper


def solution(mesh):
    return jax.shard_map(
        shards,
        mesh=mesh,
        in_specs=(P("col", "row"), P("row"), P()),
        out_specs=(P("col", "row"), P("col", None)),
        check_vma=False,
    )
```

```python
import jax
import jax.numpy as jnp
from jax import lax
from jax.experimental import pallas as pl
from jax.experimental.pallas import tpu as pltpu
from jax.sharding import PartitionSpec as P

F32 = jnp.float32
BF16 = jnp.bfloat16
MESH = pl.DeviceIdType.MESH
LO = 256
NU = 32
LOCAL = LO * NU
HALF = LOCAL // 2


def parity(bits):
    bits = bits ^ (bits >> 4)
    bits = bits ^ (bits >> 2)
    bits = bits ^ (bits >> 1)
    return bits & 1


def split(v):
    hi = v.astype(BF16)
    rest = v - hi.astype(F32)
    mid = rest.astype(BF16)
    return hi, mid, (rest - mid.astype(F32)).astype(BF16)


def away(k):
    b = (k + 6) & 7
    return 4 + (b >> 1) * (1 - 2 * (b & 1)) - (b & 1) + ((b + 1) >> 3) - ((k + 1) >> 3)


def mix_kernel(
    x_hbm, ints, both_out,
    xv, sgv, idxv, idx, t, zo, acc, rc, rf, ry, rz, mx, gs, gr, gz, gf,
    in_sem, cs, cr, fs, fr, ys, yr, zs, zr, xs, xr, gss, gsr, gzs, gzr, gfs, gfr,
):
    row, col = lax.axis_index("row"), lax.axis_index("col")
    c = row & 1
    y = (row >> 2) & 3
    z = row >> 4
    x = col * 2 + ((row >> 1) & 1)

    y_at = [((y + d) & 3) * 4 for d in range(4)]
    x_at = [(((x + d) & 1) * 2, ((x + d) & 3) >> 1) for d in range(4)]
    c_at = [c, 1 - c]
    z_at = [((z + d) & 7) * 16 for d in range(8)]

    def near(dy, dx, dc, dz=0):
        return {"row": z_at[dz] + y_at[dy] + x_at[dx][0] + c_at[dc], "col": x_at[dx][1]}

    def along_z(d):
        return {"row": ((z + d) & 7) * 16 + (row & 15), "col": col}

    plane = [(dy, dx, dc) for dy in (2, 1, 3, 0) for dx in (2, 1, 3, 0) for dc in (1, 0) if dy or dx or dc]
    z_order = (4, 3, 5, 2, 6, 1, 7)

    def loop(first, last, body):
        def step(i, carry):
            body(i)
            return carry

        lax.fori_loop(first, last, step, 0)

    place_rows = pltpu.make_async_copy(idxv, idx, in_sem.at[8])

    def fetch(i):
        at = pl.ds(pl.multiple_of(i * 8, 8), 8)
        return pltpu.make_async_copy(x_hbm.at[at], xv.at[at], in_sem.at[i])

    loop(0, 8, lambda i: fetch(i).start())
    idxv[...] = ints[pl.ds(LOCAL, 4096)] & (LOCAL - 1)
    place_rows.start()
    sgv[...] = ints[pl.ds(0, LOCAL)].reshape(LOCAL // 128, 128).astype(F32)

    barrier = pltpu.get_barrier_semaphore()
    for d in [near(*i) for i in plane] + [near(0, i, 0, d) for d in z_order for i in range(4 if 1 < d < 7 else 1)]:
        pl.semaphore_signal(barrier, inc=1, device_id=d, device_id_type=MESH)

    ri = lax.broadcasted_iota(jnp.int32, (LO, LO), 0)
    ci = lax.broadcasted_iota(jnp.int32, (LO, LO), 1)
    h = ((1 - 2 * parity(ri & ci)).astype(F32) * (1.0 / 1024.0)).astype(BF16)
    h = jnp.concatenate([h, h, h], axis=1)

    def butterfly(i):
        fetch(i).wait()
        rows = pl.ds(pl.multiple_of(i * 8, 8), 8)
        for bt in range(LO // 128):
            v = []
            for u in range(NU):
                at = u * LO + bt * 128
                v.append(xv[rows, at : at + 128] * sgv[at // 128 : at // 128 + 1, :])
            step = 1
            while step < NU:
                for u in range(NU):
                    if not u & step:
                        v[u], v[u + step] = v[u] + v[u + step], v[u] - v[u + step]
                step *= 2
            for u in range(NU):
                at = u * LO + bt * 128
                xv[rows, at : at + 128] = v[u]

    loop(0, 8, butterfly)

    def lower(g):
        parts = []
        for i in range(2):
            for top in (0, NU // 2):
                at = (2 * g + i + top) * LO
                v = xv[:, at : at + LO]
                parts.append(jnp.concatenate(split(v), axis=1))
        w = jnp.concatenate(parts, axis=0)
        o = lax.dot_general(h, w, (((1,), (1,)), ((), ())), preferred_element_type=F32)
        for i in range(2):
            part = o[:, 128 * i : 128 * i + 128]
            at = (2 * g + i) * LO
            t[at : at + LO, :] = part
            t[at + LOCAL : at + LOCAL + LO, :] = part
            t[at + HALF : at + HALF + LO, :] = pltpu.roll(part, 64, 1)

    for g in range(NU // 4):
        lower(g)

    place_rows.wait()
    pl.semaphore_wait(barrier, 53)

    left = lax.broadcasted_iota(jnp.int32, (8, 128), 1) < 64
    sub = lax.broadcasted_iota(jnp.int32, (8, 128), 0)
    table = t.reshape(LOCAL + HALF, 1, 128)

    def pick(out, k, cq):
        zq = (z + away(k)) & 7

        def body(i, carry):
            q = zq * 16 + i * 2 + cq
            sign = (1 - 2 * parity(row & q)).astype(F32)
            for top in (0, 8):
                v = None
                for j in range(8):
                    a = jnp.broadcast_to(table[idx[q * 32 + top + j]], (8, 128))
                    b = jnp.broadcast_to(table[idx[q * 32 + 16 + top + j] + HALF], (8, 128))
                    r = jnp.where(left, a, b)
                    v = r if v is None else jnp.where(sub == j, r, v)
                out[k, pl.ds(pl.multiple_of(i * 16, 16) + top, 8), :] = v * sign
            return carry

        lax.fori_loop(0, 8, body, 0, unroll=8)

    def remote(src, dst, ss, rs, device):
        return pltpu.make_async_remote_copy(
            src_ref=src, dst_ref=dst, send_sem=ss, recv_sem=rs,
            device_id=device, device_id_type=MESH,
        )

    def all_of(ref, ss, rs):
        return remote(ref, ref, ss, rs, near(0, 0, 1))

    def block(i):
        return pl.ds(pl.multiple_of(i * 32, 32), 32)

    def to_core(k):
        return remote(zo.at[k], rc.at[k], cs, cr.at[k], near(0, 0, 1))

    def to_y(k, d):
        return remote(acc.at[k, block((y + d) & 3)], ry.at[k - 2, d - 1], ys, yr.at[k - 2], near(d, 0, 0))

    def quarter(k, i):
        return acc.at[k, pl.ds(pl.multiple_of(y * 32 + (i & 1) * 16 + (i >> 1) * 8, 8), 8)]

    def to_z(k, zq, d):
        device = {"row": zq * 16 + y_at[0] + x_at[d][0] + c, "col": x_at[d][1]}
        return remote(quarter(k, (x + d) & 3), rz.at[(k - 2) * 4 + x], zs, zr, device)

    def to_first(k):
        return remote(acc.at[k], rf.at[k], fs, fr, along_z(away(k)))

    def pick_other(k):
        pick(zo, k, 1 - c)
        to_core(k).start()

    def send_y(k):
        for d in (2, 1, 3):
            to_y(k, d).start()

    def pick_own(k):
        pick(acc, k, c)
        to_core(k).wait_recv()
        acc[k] = acc[k] + rc[k]
        pl.when(k < 2)(lambda: to_first(k).start())
        pl.when((k >= 2) & (k < 7))(lambda: send_y(k))

    def add_y(k):
        all_of(ry.at[k - 2], ys, yr.at[k - 2]).wait_recv()
        mine = block(y)
        acc[k, mine] = (acc[k, mine] + ry[k - 2, 0]) + (ry[k - 2, 1] + ry[k - 2, 2])

    def pass_z(k):
        add_y(k)
        zq = (z + away(k)) & 7
        for d in (2, 1, 3, 0):
            to_z(k, zq, d).start()

    loop(0, 8, pick_other)
    loop(0, 8, pick_own)
    all_of(rf, fs, fr).wait_recv()
    acc[7] = acc[7] + (rf[0] + rf[1])
    send_y(7)
    loop(2, 7, pass_z)
    add_y(7)
    for d in (2, 1, 3):
        to_z(7, z, d).start()
    rz[20 + x] = quarter(7, x)[...]
    all_of(zo, cs, cr.at[0]).wait_send()
    all_of(rf, fs, fr).wait_send()
    all_of(ry, ys, yr.at[0]).wait_send()
    others = all_of(rz.at[pl.ds(0, 23)], zs, zr)
    others.wait_recv()

    def total(i):
        v = [rz[4 * k + i] for k in range(6)] + [rz[4 * k + i + 1] for k in range(6)]
        while len(v) > 1:
            v = [v[j] + v[j + 1] if j + 1 < len(v) else v[j] for j in range(0, len(v), 2)]
        return v[0]

    a0, a1 = total(0), total(2)
    first = jnp.concatenate([a0[:, :64], a1[:, :64]], axis=1)
    second = jnp.concatenate([a0[:, 64:], a1[:, 64:]], axis=1)
    m = jnp.concatenate([first, second], axis=0)
    hi, mid, low = split(m)
    deep = jnp.concatenate([hi, hi, mid, hi, low, mid], axis=0)
    g = jnp.dot(deep.T, jnp.concatenate([hi, mid, hi, low, hi, mid], axis=0), preferred_element_type=F32)
    for e in range(32):
        gs[e] = g[4 * e : 4 * e + 4]

    place = x * 8 + y * 2 + c

    def to_gs(i):
        dy, dx, dc = plane[i]
        e = ((x + dx) & 3) * 8 + ((y + dy) & 3) * 2 + c_at[dc]
        return remote(gs.at[e], gr.at[i], gss, gsr, near(dy, dx, dc))

    to_mate = remote(mx.at[x >> 1], mx.at[x >> 1], xs, xr, near(0, 2, 0))

    def to_gz(d):
        return remote(gz.at[z], gz.at[z], gzs, gzr, near(0, 0, 0, d))

    def to_gf(i):
        return remote(gf.at[place], gf.at[place], gfs, gfr, near(*plane[i]))

    for i in range(31):
        to_gs(i).start()
    mx[x >> 1] = m
    to_mate.start()
    others.wait_send()
    all_of(gr, gss, gsr).wait_recv()
    v = [gr[i] for i in range(31)] + [gs[place]]
    while len(v) > 1:
        v = [v[j] + v[j + 1] for j in range(0, len(v), 2)]
    gz[z] = v[0]
    for d in z_order:
        to_gz(d).start()
    all_of(gr, gss, gsr).wait_send()
    to_mate.wait()
    for i in range(2):
        for j in range(2):
            both_out[128 + 16 * j + 8 * i : 136 + 16 * j + 8 * i, :] = mx[i, 8 * j : 8 * j + 8]
    all_of(gz.at[pl.ds(0, 7)], gzs, gzr).wait_recv()
    gf[place] = (((gz[0] + gz[1]) + (gz[2] + gz[3])) + ((gz[4] + gz[5]) + (gz[6] + gz[7]))) * (1.0 / 4096.0)
    for i in range(31):
        to_gf(i).start()
    all_of(gz.at[pl.ds(0, 7)], gzs, gzr).wait_send()
    all_of(gf.at[pl.ds(0, 31)], gfs, gfr).wait_recv()
    for e in range(32):
        both_out[e * 4 : (e + 1) * 4, :] = gf[e]
    all_of(gf.at[pl.ds(0, 31)], gfs, gfr).wait_send()


def mix(panel, signs, rows):
    vm = pl.BlockSpec(memory_space=pltpu.VMEM)
    hbm = pl.BlockSpec(memory_space=pltpu.HBM)
    V = pltpu.VMEM
    D = pltpu.SemaphoreType.DMA
    return pl.pallas_call(
        mix_kernel,
        out_shape=jax.ShapeDtypeStruct((160, 128), F32),
        in_specs=[hbm, vm],
        out_specs=vm,
        scratch_shapes=[
            V((64, LOCAL), F32),
            V((LOCAL // 128, 128), F32),
            V((4096,), jnp.int32),
            pltpu.SMEM((4096,), jnp.int32),
            V((LOCAL + HALF, 128), F32),
            V((8, 128, 128), F32),
            V((8, 128, 128), F32),
            V((8, 128, 128), F32),
            V((2, 128, 128), F32),
            V((6, 3, 32, 128), F32),
            V((24, 8, 128), F32),
            V((2, 16, 128), F32),
            V((32, 4, 128), F32),
            V((31, 4, 128), F32),
            V((8, 4, 128), F32),
            V((32, 4, 128), F32),
            D((9,)),
            D, D((8,)), D, D, D, D((6,)), D, D, D, D, D, D, D, D, D, D,
        ],
        compiler_params=pltpu.CompilerParams(
            collective_id=0, has_side_effects=True, vmem_limit_bytes=52 << 20
        ),
        name="mix",
    )(panel, jnp.concatenate([signs, rows]))


def rows_const(v, j):
    return jnp.broadcast_to(v[:, j : j + 1], (8, 128))


def factor_kernel(both_ref, basis_ref, tri_ref, a_ref, u_ref, p_ref):
    n, width = 128, 32
    col = lax.axis_index("col")
    a_ref[:, :128] = both_ref[:128, :]
    samples = jnp.concatenate([both_ref[128:, :], jnp.zeros((96, 128), F32)], axis=0)
    a_ref[:, 128:] = samples.T
    lane = lax.broadcasted_iota(jnp.int32, (8, 128), 1)
    for panel in range(n // width):
        top = panel * width
        nb = width // 8
        blocks = [
            [a_ref[top + 8 * i : top + 8 * i + 8, 128 * t : 128 * t + 128] for t in range(2)]
            for i in range(nb)
        ]
        for j in range(nb):
            at = top + 8 * j
            for i in range(2):
                p_ref[2 * at + 8 * i : 2 * at + 8 * i + 8, :] = blocks[j][i]
            rows = [[p_ref[pl.ds(2 * at + 8 * i + k, 8, stride=0), :] for i in range(2)] for k in range(8)]
            d = {(i, k): rows_const(rows[i][0], at + k) for i in range(8) for k in range(i + 1)}
            below = [[rows_const(blocks[i][0], at + k) for k in range(8)] for i in range(j + 1, nb)]
            for k in range(8):
                r = lax.rsqrt(d[k, k])
                for i in range(k + 1, 8):
                    d[i, k] = d[i, k] * r
                for i in range(k + 1, 8):
                    for q in range(k + 1, i + 1):
                        d[i, q] = d[i, q] - d[i, k] * d[q, k]
                for t in range(2):
                    rows[k][t] = rows[k][t] * r
                    for q in range(k + 1, 8):
                        rows[q][t] = rows[q][t] - d[q, k] * rows[k][t]
                for b in below:
                    b[k] = b[k] * r
                    for q in range(k + 1, 8):
                        b[q] = b[q] - d[q, k] * b[k]
            for k in range(8):
                keep = lane >= at + k
                u_ref[at + k : at + k + 1, :128] = jnp.where(keep, rows[k][0], 0.0)[:1]
                u_ref[at + k : at + k + 1, 128:] = rows[k][1][:1]
            for i in range(j + 1, nb):
                b = below[i - j - 1]
                for t in range(2):
                    v = blocks[i][t]
                    for k in range(8):
                        v = v - b[k] * rows[k][t]
                    blocks[i][t] = v
        if top + width < n:
            rest = top + width
            u = u_ref[top:rest, :]
            hi, mid, low = split(u)
            left = jnp.concatenate([v[:, :128] for v in (hi, hi, mid, hi, low, mid)], axis=0)
            right = jnp.concatenate([hi, mid, hi, low, hi, mid], axis=0)
            upd = jnp.dot(left.T[rest:, :], right, preferred_element_type=F32)
            a_ref[rest:, :] = a_ref[rest:, :] - upd
    half = pl.ds(pl.multiple_of(col * 64, 64), 64)
    tri_ref[...] = u_ref[half, :128]
    basis_ref[...] = u_ref[half, 128:].T[:32]


def factor(both):
    vm = pl.BlockSpec(memory_space=pltpu.VMEM)
    return pl.pallas_call(
        factor_kernel,
        out_shape=(jax.ShapeDtypeStruct((32, 64), F32), jax.ShapeDtypeStruct((64, 128), F32)),
        in_specs=[vm],
        out_specs=(vm, vm),
        scratch_shapes=[pltpu.VMEM((128, 256), F32), pltpu.VMEM((128, 256), F32), pltpu.VMEM((256, 128), F32)],
        compiler_params=pltpu.CompilerParams(vmem_limit_bytes=16 << 20),
        name="factor",
    )(both)


def shards(tall_panel_array, row_signs, sample_rows):
    basis, upper = factor(mix(tall_panel_array, row_signs, sample_rows))
    return basis.T, upper


def solution(mesh):
    return jax.shard_map(
        shards,
        mesh=mesh,
        in_specs=(P("col", "row"), P("row"), P()),
        out_specs=(P("col", "row"), P("col", None)),
        check_vma=False,
    )
```

```python
import jax
import jax.numpy as jnp
from jax import lax
from jax.experimental import pallas as pl
from jax.experimental.pallas import tpu as pltpu
from jax.sharding import PartitionSpec as P

F32 = jnp.float32
BF16 = jnp.bfloat16
MESH = pl.DeviceIdType.MESH
LO = 256
NU = 32
LOCAL = LO * NU
HALF = LOCAL // 2


def parity(bits):
    bits = bits ^ (bits >> 4)
    bits = bits ^ (bits >> 2)
    bits = bits ^ (bits >> 1)
    return bits & 1


def split(v):
    hi = v.astype(BF16)
    rest = v - hi.astype(F32)
    mid = rest.astype(BF16)
    return hi, mid, (rest - mid.astype(F32)).astype(BF16)


def away(k):
    b = (k + 6) & 7
    return 4 + (b >> 1) * (1 - 2 * (b & 1)) - (b & 1) + ((b + 1) >> 3) - ((k + 1) >> 3)


def mix_kernel(
    x_hbm, ints, both_out,
    xv, sgv, idxv, idx, t, zo, acc, rc, rf, ry, rz, mx, gs, gr, gz, gf,
    in_sem, cs, cr, fs, fr, ys, yr, zs, zr, xs, xr, gss, gsr, gzs, gzr, gfs, gfr,
):
    row, col = lax.axis_index("row"), lax.axis_index("col")
    c = row & 1
    y = (row >> 2) & 3
    z = row >> 4
    x = col * 2 + ((row >> 1) & 1)

    y_at = [((y + d) & 3) * 4 for d in range(4)]
    x_at = [(((x + d) & 1) * 2, ((x + d) & 3) >> 1) for d in range(4)]
    c_at = [c, 1 - c]
    z_at = [((z + d) & 7) * 16 for d in range(8)]

    def near(dy, dx, dc, dz=0):
        return {"row": z_at[dz] + y_at[dy] + x_at[dx][0] + c_at[dc], "col": x_at[dx][1]}

    def along_z(d):
        return {"row": ((z + d) & 7) * 16 + (row & 15), "col": col}

    plane = [(dy, dx, dc) for dy in (2, 1, 3, 0) for dx in (2, 1, 3, 0) for dc in (1, 0) if dy or dx or dc]
    z_order = (4, 3, 5, 2, 6, 1, 7)

    def loop(first, last, body):
        def step(i, carry):
            body(i)
            return carry

        lax.fori_loop(first, last, step, 0)

    place_rows = pltpu.make_async_copy(idxv, idx, in_sem.at[8])

    def fetch(i):
        at = pl.ds(pl.multiple_of(i * 8, 8), 8)
        return pltpu.make_async_copy(x_hbm.at[at], xv.at[at], in_sem.at[i])

    loop(0, 8, lambda i: fetch(i).start())
    idxv[...] = ints[pl.ds(LOCAL, 4096)] & (LOCAL - 1)
    place_rows.start()
    signs = ints[pl.ds(0, LOCAL)].reshape(LOCAL // 128, 128).astype(F32)
    for i in range(LOCAL // 128):
        sgv[8 * i : 8 * i + 8, :] = jnp.broadcast_to(signs[i : i + 1, :], (8, 128))

    barrier = pltpu.get_barrier_semaphore()
    for d in [near(*i) for i in plane] + [near(0, i, 0, d) for d in z_order for i in range(4 if 1 < d < 7 else 1)]:
        pl.semaphore_signal(barrier, inc=1, device_id=d, device_id_type=MESH)

    ri = lax.broadcasted_iota(jnp.int32, (LO, LO), 0)
    ci = lax.broadcasted_iota(jnp.int32, (LO, LO), 1)
    h = ((1 - 2 * parity(ri & ci)).astype(F32) * (1.0 / 1024.0)).astype(BF16)
    h = jnp.concatenate([h, h, h], axis=1)

    def butterfly(i):
        fetch(i).wait()
        rows = pl.ds(pl.multiple_of(i * 8, 8), 8)
        for bt in range(LO // 128):
            v = []
            for u in range(NU):
                at = u * LO + bt * 128
                v.append(xv[rows, at : at + 128] * sgv[at // 16 : at // 16 + 8, :])
            step = 1
            while step < NU:
                for u in range(NU):
                    if not u & step:
                        v[u], v[u + step] = v[u] + v[u + step], v[u] - v[u + step]
                step *= 2
            for u in range(NU):
                at = u * LO + bt * 128
                xv[rows, at : at + 128] = v[u]

    loop(0, 8, butterfly)

    def lower(g):
        parts = []
        for i in range(2):
            for top in (0, NU // 2):
                at = (2 * g + i + top) * LO
                v = xv[:, at : at + LO]
                parts.append(jnp.concatenate(split(v), axis=1))
        w = jnp.concatenate(parts, axis=0)
        o = lax.dot_general(h, w, (((1,), (1,)), ((), ())), preferred_element_type=F32)
        for i in range(2):
            part = o[:, 128 * i : 128 * i + 128]
            at = (2 * g + i) * LO
            t[at : at + LO, :] = part
            t[at + LOCAL : at + LOCAL + LO, :] = part
            t[at + HALF : at + HALF + LO, :] = pltpu.roll(part, 64, 1)

    for g in range(NU // 4):
        lower(g)

    place_rows.wait()
    pl.semaphore_wait(barrier, 53)

    left = lax.broadcasted_iota(jnp.int32, (8, 128), 1) < 64
    sub = lax.broadcasted_iota(jnp.int32, (8, 128), 0)
    table = t.reshape(LOCAL + HALF, 1, 128)

    def pick(out, k, cq):
        zq = (z + away(k)) & 7

        def body(i, carry):
            q = zq * 16 + i * 2 + cq
            sign = (1 - 2 * parity(row & q)).astype(F32)
            for top in (0, 8):
                v = None
                for j in range(8):
                    a = jnp.broadcast_to(table[idx[q * 32 + top + j]], (8, 128))
                    b = jnp.broadcast_to(table[idx[q * 32 + 16 + top + j] + HALF], (8, 128))
                    r = jnp.where(left, a, b)
                    v = r if v is None else jnp.where(sub == j, r, v)
                out[k, pl.ds(pl.multiple_of(i * 16, 16) + top, 8), :] = v * sign
            return carry

        lax.fori_loop(0, 8, body, 0, unroll=8)

    def remote(src, dst, ss, rs, device):
        return pltpu.make_async_remote_copy(
            src_ref=src, dst_ref=dst, send_sem=ss, recv_sem=rs,
            device_id=device, device_id_type=MESH,
        )

    def all_of(ref, ss, rs):
        return remote(ref, ref, ss, rs, near(0, 0, 1))

    def block(i):
        return pl.ds(pl.multiple_of(i * 32, 32), 32)

    def to_core(k):
        return remote(zo.at[k], rc.at[k], cs, cr.at[k], near(0, 0, 1))

    def to_y(k, d):
        return remote(acc.at[k, block((y + d) & 3)], ry.at[k - 2, d - 1], ys, yr.at[k - 2], near(d, 0, 0))

    def quarter(k, i):
        return acc.at[k, pl.ds(pl.multiple_of(y * 32 + (i & 1) * 16 + (i >> 1) * 8, 8), 8)]

    def to_z(k, zq, d):
        device = {"row": zq * 16 + y_at[0] + x_at[d][0] + c, "col": x_at[d][1]}
        return remote(quarter(k, (x + d) & 3), rz.at[(k - 2) * 4 + x], zs, zr, device)

    def to_first(k):
        return remote(acc.at[k], rf.at[k], fs, fr, along_z(away(k)))

    def pick_other(k):
        pick(zo, k, 1 - c)
        to_core(k).start()

    def send_y(k):
        for d in (2, 1, 3):
            to_y(k, d).start()

    def pick_own(k):
        pick(acc, k, c)
        to_core(k).wait_recv()
        acc[k] = acc[k] + rc[k]
        pl.when(k < 2)(lambda: to_first(k).start())
        pl.when((k >= 2) & (k < 7))(lambda: send_y(k))

    def add_y(k):
        all_of(ry.at[k - 2], ys, yr.at[k - 2]).wait_recv()
        mine = block(y)
        acc[k, mine] = (acc[k, mine] + ry[k - 2, 0]) + (ry[k - 2, 1] + ry[k - 2, 2])

    def pass_z(k):
        add_y(k)
        zq = (z + away(k)) & 7
        for d in (2, 1, 3, 0):
            to_z(k, zq, d).start()

    loop(0, 8, pick_other)
    loop(0, 8, pick_own)
    all_of(rf, fs, fr).wait_recv()
    acc[7] = acc[7] + (rf[0] + rf[1])
    send_y(7)
    loop(2, 7, pass_z)
    add_y(7)
    for d in (2, 1, 3):
        to_z(7, z, d).start()
    rz[20 + x] = quarter(7, x)[...]
    all_of(zo, cs, cr.at[0]).wait_send()
    all_of(rf, fs, fr).wait_send()
    all_of(ry, ys, yr.at[0]).wait_send()
    others = all_of(rz.at[pl.ds(0, 23)], zs, zr)
    others.wait_recv()

    def total(i):
        v = [rz[4 * k + i] for k in range(6)] + [rz[4 * k + i + 1] for k in range(6)]
        while len(v) > 1:
            v = [v[j] + v[j + 1] if j + 1 < len(v) else v[j] for j in range(0, len(v), 2)]
        return v[0]

    a0, a1 = total(0), total(2)
    first = jnp.concatenate([a0[:, :64], a1[:, :64]], axis=1)
    second = jnp.concatenate([a0[:, 64:], a1[:, 64:]], axis=1)
    m = jnp.concatenate([first, second], axis=0)
    hi, mid, low = split(m)
    deep = jnp.concatenate([hi, hi, mid, hi, low, mid], axis=0)
    g = jnp.dot(deep.T, jnp.concatenate([hi, mid, hi, low, hi, mid], axis=0), preferred_element_type=F32)
    for e in range(32):
        gs[e] = g[4 * e : 4 * e + 4]

    place = x * 8 + y * 2 + c

    def to_gs(i):
        dy, dx, dc = plane[i]
        e = ((x + dx) & 3) * 8 + ((y + dy) & 3) * 2 + c_at[dc]
        return remote(gs.at[e], gr.at[i], gss, gsr, near(dy, dx, dc))

    to_mate = remote(mx.at[x >> 1], mx.at[x >> 1], xs, xr, near(0, 2, 0))

    def to_gz(d):
        return remote(gz.at[z], gz.at[z], gzs, gzr, near(0, 0, 0, d))

    def to_gf(i):
        return remote(gf.at[place], gf.at[place], gfs, gfr, near(*plane[i]))

    for i in range(31):
        to_gs(i).start()
    mx[x >> 1] = m
    to_mate.start()
    others.wait_send()
    all_of(gr, gss, gsr).wait_recv()
    v = [gr[i] for i in range(31)] + [gs[place]]
    while len(v) > 1:
        v = [v[j] + v[j + 1] for j in range(0, len(v), 2)]
    gz[z] = v[0]
    for d in z_order:
        to_gz(d).start()
    all_of(gr, gss, gsr).wait_send()
    to_mate.wait()
    quarters = [mx[i, 8 * j : 8 * j + 8] for j in range(2) for i in range(2)]
    both_out[:, 128:] = jnp.concatenate(quarters + [jnp.zeros((96, 128), F32)], axis=0).T
    all_of(gz.at[pl.ds(0, 7)], gzs, gzr).wait_recv()
    gf[place] = (((gz[0] + gz[1]) + (gz[2] + gz[3])) + ((gz[4] + gz[5]) + (gz[6] + gz[7]))) * (1.0 / 4096.0)
    for i in range(31):
        to_gf(i).start()
    all_of(gz.at[pl.ds(0, 7)], gzs, gzr).wait_send()
    all_of(gf.at[pl.ds(0, 31)], gfs, gfr).wait_recv()
    for e in range(32):
        both_out[e * 4 : (e + 1) * 4, :128] = gf[e]
    all_of(gf.at[pl.ds(0, 31)], gfs, gfr).wait_send()


def mix(panel, signs, rows):
    vm = pl.BlockSpec(memory_space=pltpu.VMEM)
    hbm = pl.BlockSpec(memory_space=pltpu.HBM)
    V = pltpu.VMEM
    D = pltpu.SemaphoreType.DMA
    return pl.pallas_call(
        mix_kernel,
        out_shape=jax.ShapeDtypeStruct((128, 256), F32),
        in_specs=[hbm, vm],
        out_specs=vm,
        scratch_shapes=[
            V((64, LOCAL), F32),
            V((LOCAL // 16, 128), F32),
            V((4096,), jnp.int32),
            pltpu.SMEM((4096,), jnp.int32),
            V((LOCAL + HALF, 128), F32),
            V((8, 128, 128), F32),
            V((8, 128, 128), F32),
            V((8, 128, 128), F32),
            V((2, 128, 128), F32),
            V((6, 3, 32, 128), F32),
            V((24, 8, 128), F32),
            V((2, 16, 128), F32),
            V((32, 4, 128), F32),
            V((31, 4, 128), F32),
            V((8, 4, 128), F32),
            V((32, 4, 128), F32),
            D((9,)),
            D, D((8,)), D, D, D, D((6,)), D, D, D, D, D, D, D, D, D, D,
        ],
        compiler_params=pltpu.CompilerParams(
            collective_id=0, has_side_effects=True, vmem_limit_bytes=52 << 20
        ),
        name="mix",
    )(panel, jnp.concatenate([signs, rows]))


def rows_const(v, j):
    return jnp.broadcast_to(v[:, j : j + 1], (8, 128))


def factor_kernel(both_ref, basis_ref, tri_ref, a_ref, u_ref, p_ref):
    n, width = 128, 32
    col = lax.axis_index("col")
    lane = lax.broadcasted_iota(jnp.int32, (8, 128), 1)
    for panel in range(n // width):
        top = panel * width
        nb = width // 8
        source = a_ref if panel else both_ref
        blocks = [
            [source[top + 8 * i : top + 8 * i + 8, 128 * t : 128 * t + 128] for t in range(2)]
            for i in range(nb)
        ]
        for j in range(nb):
            at = top + 8 * j
            for i in range(2):
                p_ref[2 * at + 8 * i : 2 * at + 8 * i + 8, :] = blocks[j][i]
            rows = [[p_ref[pl.ds(2 * at + 8 * i + k, 8, stride=0), :] for i in range(2)] for k in range(8)]
            d = {(i, k): rows_const(rows[i][0], at + k) for i in range(8) for k in range(i + 1)}
            below = [[rows_const(blocks[i][0], at + k) for k in range(8)] for i in range(j + 1, nb)]
            for k in range(8):
                r = lax.rsqrt(d[k, k])
                for i in range(k + 1, 8):
                    d[i, k] = d[i, k] * r
                for i in range(k + 1, 8):
                    for q in range(k + 1, i + 1):
                        d[i, q] = d[i, q] - d[i, k] * d[q, k]
                for t in range(2):
                    rows[k][t] = rows[k][t] * r
                    for q in range(k + 1, 8):
                        rows[q][t] = rows[q][t] - d[q, k] * rows[k][t]
                for b in below:
                    b[k] = b[k] * r
                    for q in range(k + 1, 8):
                        b[q] = b[q] - d[q, k] * b[k]
            for k in range(8):
                keep = lane >= at + k
                u_ref[at + k : at + k + 1, :128] = jnp.where(keep, rows[k][0], 0.0)[:1]
                u_ref[at + k : at + k + 1, 128:] = rows[k][1][:1]
            for i in range(j + 1, nb):
                b = below[i - j - 1]
                for t in range(2):
                    v = blocks[i][t]
                    for k in range(8):
                        v = v - b[k] * rows[k][t]
                    blocks[i][t] = v
        if top + width < n:
            rest = top + width
            u = u_ref[top:rest, :]
            hi, mid, low = split(u)
            left = jnp.concatenate([v[:, :128] for v in (hi, hi, mid, hi, low, mid)], axis=0)
            right = jnp.concatenate([hi, mid, hi, low, hi, mid], axis=0)
            upd = jnp.dot(left.T[rest:, :], right, preferred_element_type=F32)
            a_ref[rest:, :] = source[rest:, :] - upd
    half = pl.ds(pl.multiple_of(col * 64, 64), 64)
    tri_ref[...] = u_ref[half, :128]
    basis_ref[...] = u_ref[half, 128:].T[:32]


def factor(both):
    vm = pl.BlockSpec(memory_space=pltpu.VMEM)
    return pl.pallas_call(
        factor_kernel,
        out_shape=(jax.ShapeDtypeStruct((32, 64), F32), jax.ShapeDtypeStruct((64, 128), F32)),
        in_specs=[vm],
        out_specs=(vm, vm),
        scratch_shapes=[pltpu.VMEM((128, 256), F32), pltpu.VMEM((128, 256), F32), pltpu.VMEM((256, 128), F32)],
        compiler_params=pltpu.CompilerParams(vmem_limit_bytes=16 << 20),
        name="factor",
    )(both)


def shards(tall_panel_array, row_signs, sample_rows):
    basis, upper = factor(mix(tall_panel_array, row_signs, sample_rows))
    return basis.T, upper


def solution(mesh):
    return jax.shard_map(
        shards,
        mesh=mesh,
        in_specs=(P("col", "row"), P("row"), P()),
        out_specs=(P("col", "row"), P("col", None)),
        check_vma=False,
    )
```

```python
import jax
import jax.numpy as jnp
from jax import lax
from jax.experimental import pallas as pl
from jax.experimental.pallas import tpu as pltpu
from jax.sharding import PartitionSpec as P

F32 = jnp.float32
BF16 = jnp.bfloat16
MESH = pl.DeviceIdType.MESH
LO = 256
NU = 32
LOCAL = LO * NU
HALF = LOCAL // 2


def parity(bits):
    bits = bits ^ (bits >> 4)
    bits = bits ^ (bits >> 2)
    bits = bits ^ (bits >> 1)
    return bits & 1


def split(v):
    hi = v.astype(BF16)
    rest = v - hi.astype(F32)
    mid = rest.astype(BF16)
    return hi, mid, (rest - mid.astype(F32)).astype(BF16)


def away(k):
    b = (k + 6) & 7
    return 4 + (b >> 1) * (1 - 2 * (b & 1)) - (b & 1) + ((b + 1) >> 3) - ((k + 1) >> 3)


def mix_kernel(
    x_hbm, ints, both_out,
    xv, sgv, idxv, idx, t, zo, acc, rc, rf, ry, rz, mx, gs, gr, gz, gf,
    in_sem, cs, cr, fs, fr, ys, yr, zs, zr, xs, xr, gss, gsr, gzs, gzr, gfs, gfr,
):
    row, col = lax.axis_index("row"), lax.axis_index("col")
    c = row & 1
    y = (row >> 2) & 3
    z = row >> 4
    x = col * 2 + ((row >> 1) & 1)

    y_at = [((y + d) & 3) * 4 for d in range(4)]
    x_at = [(((x + d) & 1) * 2, ((x + d) & 3) >> 1) for d in range(4)]
    c_at = [c, 1 - c]
    z_at = [((z + d) & 7) * 16 for d in range(8)]

    def near(dy, dx, dc, dz=0):
        return {"row": z_at[dz] + y_at[dy] + x_at[dx][0] + c_at[dc], "col": x_at[dx][1]}

    def along_z(d):
        return {"row": ((z + d) & 7) * 16 + (row & 15), "col": col}

    plane = [(dy, dx, dc) for dy in (2, 1, 3, 0) for dx in (2, 1, 3, 0) for dc in (1, 0) if dy or dx or dc]
    z_order = (4, 3, 5, 2, 6, 1, 7)

    def loop(first, last, body):
        def step(i, carry):
            body(i)
            return carry

        lax.fori_loop(first, last, step, 0)

    place_rows = pltpu.make_async_copy(idxv, idx, in_sem.at[8])

    def fetch(i):
        at = pl.ds(pl.multiple_of(i * 8, 8), 8)
        return pltpu.make_async_copy(x_hbm.at[at], xv.at[at], in_sem.at[i])

    loop(0, 8, lambda i: fetch(i).start())
    idxv[...] = ints[pl.ds(LOCAL, 4096)] & (LOCAL - 1)
    place_rows.start()
    sgv[...] = ints[pl.ds(0, LOCAL)].reshape(LOCAL // 128, 128).astype(F32)

    barrier = pltpu.get_barrier_semaphore()
    early = [(0, 0, 1, 0), (0, 0, 0, 1), (0, 0, 0, 7)] + [(d, 0, 0, 0) for d in (2, 1, 3)]
    early += [(0, i, 0, d) for d in (4, 3, 5, 2, 6, 0) for i in range(4) if d or i]
    for at in early:
        pl.semaphore_signal(barrier, inc=1, device_id=near(*at), device_id_type=MESH)
    ri = lax.broadcasted_iota(jnp.int32, (LO, LO), 0)
    ci = lax.broadcasted_iota(jnp.int32, (LO, LO), 1)
    h = ((1 - 2 * parity(ri & ci)).astype(F32) * (1.0 / 1024.0)).astype(BF16)
    h = jnp.concatenate([h, h, h], axis=1)

    def butterfly(i):
        fetch(i).wait()
        rows = pl.ds(pl.multiple_of(i * 8, 8), 8)
        for bt in range(LO // 128):
            v = []
            for u in range(NU):
                at = u * LO + bt * 128
                v.append(xv[rows, at : at + 128] * sgv[at // 128 : at // 128 + 1, :])
            step = 1
            while step < NU:
                for u in range(NU):
                    if not u & step:
                        v[u], v[u + step] = v[u] + v[u + step], v[u] - v[u + step]
                step *= 2
            for u in range(NU):
                at = u * LO + bt * 128
                xv[rows, at : at + 128] = v[u]

    loop(0, 8, butterfly)

    def lower(g):
        parts = []
        for i in range(2):
            for top in (0, NU // 2):
                at = (2 * g + i + top) * LO
                v = xv[:, at : at + LO]
                parts.append(jnp.concatenate(split(v), axis=1))
        w = jnp.concatenate(parts, axis=0)
        o = lax.dot_general(h, w, (((1,), (1,)), ((), ())), preferred_element_type=F32)
        for i in range(2):
            part = o[:, 128 * i : 128 * i + 128]
            at = (2 * g + i) * LO
            t[at : at + LO, :] = part
            t[at + LOCAL : at + LOCAL + LO, :] = part
            t[at + HALF : at + HALF + LO, :] = pltpu.roll(part, 64, 1)

    for g in range(NU // 4):
        lower(g)

    place_rows.wait()
    pl.semaphore_wait(barrier, len(early))

    left = lax.broadcasted_iota(jnp.int32, (8, 128), 1) < 64
    sub = lax.broadcasted_iota(jnp.int32, (8, 128), 0)
    table = t.reshape(LOCAL + HALF, 1, 128)

    def pick(out, k, cq):
        zq = (z + away(k)) & 7

        def body(i, carry):
            q = zq * 16 + i * 2 + cq
            sign = (1 - 2 * parity(row & q)).astype(F32)
            for top in (0, 8):
                v = None
                for j in range(8):
                    a = jnp.broadcast_to(table[idx[q * 32 + top + j]], (8, 128))
                    b = jnp.broadcast_to(table[idx[q * 32 + 16 + top + j] + HALF], (8, 128))
                    r = jnp.where(left, a, b)
                    v = r if v is None else jnp.where(sub == j, r, v)
                out[k, pl.ds(pl.multiple_of(i * 16, 16) + top, 8), :] = v * sign
            return carry

        lax.fori_loop(0, 8, body, 0, unroll=8)

    def remote(src, dst, ss, rs, device):
        return pltpu.make_async_remote_copy(
            src_ref=src, dst_ref=dst, send_sem=ss, recv_sem=rs,
            device_id=device, device_id_type=MESH,
        )

    def all_of(ref, ss, rs):
        return remote(ref, ref, ss, rs, near(0, 0, 1))

    def block(i):
        return pl.ds(pl.multiple_of(i * 32, 32), 32)

    def to_core(k):
        return remote(zo.at[k], rc.at[k], cs, cr.at[k], near(0, 0, 1))

    def to_y(k, d):
        return remote(acc.at[k, block((y + d) & 3)], ry.at[k - 2, d - 1], ys, yr.at[k - 2], near(d, 0, 0))

    def quarter(k, i):
        return acc.at[k, pl.ds(pl.multiple_of(y * 32 + (i & 1) * 16 + (i >> 1) * 8, 8), 8)]

    def to_z(k, zq, d):
        device = {"row": zq * 16 + y_at[0] + x_at[d][0] + c, "col": x_at[d][1]}
        return remote(quarter(k, (x + d) & 3), rz.at[(k - 2) * 4 + x], zs, zr, device)

    def to_first(k):
        return remote(acc.at[k], rf.at[k], fs, fr, along_z(away(k)))

    def pick_other(k):
        pick(zo, k, 1 - c)
        to_core(k).start()

    def send_y(k):
        for d in (2, 1, 3):
            to_y(k, d).start()

    def pick_own(k):
        pick(acc, k, c)
        to_core(k).wait_recv()
        acc[k] = acc[k] + rc[k]
        pl.when(k < 2)(lambda: to_first(k).start())
        pl.when((k >= 2) & (k < 7))(lambda: send_y(k))

    def add_y(k):
        all_of(ry.at[k - 2], ys, yr.at[k - 2]).wait_recv()
        mine = block(y)
        acc[k, mine] = (acc[k, mine] + ry[k - 2, 0]) + (ry[k - 2, 1] + ry[k - 2, 2])

    def pass_z(k):
        add_y(k)
        zq = (z + away(k)) & 7
        for d in (2, 1, 3, 0):
            to_z(k, zq, d).start()

    loop(0, 8, pick_other)
    loop(0, 8, pick_own)
    all_of(rf, fs, fr).wait_recv()
    acc[7] = acc[7] + (rf[0] + rf[1])
    send_y(7)
    loop(2, 7, pass_z)
    add_y(7)
    for d in (2, 1, 3):
        to_z(7, z, d).start()
    rz[20 + x] = quarter(7, x)[...]
    all_of(zo, cs, cr.at[0]).wait_send()
    all_of(rf, fs, fr).wait_send()
    all_of(ry, ys, yr.at[0]).wait_send()
    others = all_of(rz.at[pl.ds(0, 23)], zs, zr)
    others.wait_recv()

    def total(i):
        v = [rz[4 * k + i] for k in range(6)] + [rz[4 * k + i + 1] for k in range(6)]
        while len(v) > 1:
            v = [v[j] + v[j + 1] if j + 1 < len(v) else v[j] for j in range(0, len(v), 2)]
        return v[0]

    a0, a1 = total(0), total(2)
    first = jnp.concatenate([a0[:, :64], a1[:, :64]], axis=1)
    second = jnp.concatenate([a0[:, 64:], a1[:, 64:]], axis=1)
    m = jnp.concatenate([first, second], axis=0)
    hi, mid, low = split(m)
    deep = jnp.concatenate([hi, hi, mid, hi, low, mid], axis=0)
    g = jnp.dot(deep.T, jnp.concatenate([hi, mid, hi, low, hi, mid], axis=0), preferred_element_type=F32)
    for e in range(32):
        gs[e] = g[4 * e : 4 * e + 4]

    place = x * 8 + y * 2 + c

    def to_gs(i):
        dy, dx, dc = plane[i]
        e = ((x + dx) & 3) * 8 + ((y + dy) & 3) * 2 + c_at[dc]
        return remote(gs.at[e], gr.at[i], gss, gsr, near(dy, dx, dc))

    to_mate = remote(mx.at[x >> 1], mx.at[x >> 1], xs, xr, near(0, 2, 0))

    def to_gz(d):
        return remote(gz.at[z], gz.at[z], gzs, gzr, near(0, 0, 0, d))

    def to_gf(i):
        return remote(gf.at[place], gf.at[place], gfs, gfr, near(*plane[i]))

    for i in range(31):
        to_gs(i).start()
    mx[x >> 1] = m
    to_mate.start()
    others.wait_send()
    all_of(gr, gss, gsr).wait_recv()
    v = [gr[i] for i in range(31)] + [gs[place]]
    while len(v) > 1:
        v = [v[j] + v[j + 1] for j in range(0, len(v), 2)]
    gz[z] = v[0]
    for d in z_order:
        to_gz(d).start()
    all_of(gr, gss, gsr).wait_send()
    to_mate.wait()
    for i in range(2):
        for j in range(2):
            both_out[128 + 16 * j + 8 * i : 136 + 16 * j + 8 * i, :] = mx[i, 8 * j : 8 * j + 8]
    all_of(gz.at[pl.ds(0, 7)], gzs, gzr).wait_recv()
    gf[place] = (((gz[0] + gz[1]) + (gz[2] + gz[3])) + ((gz[4] + gz[5]) + (gz[6] + gz[7]))) * (1.0 / 4096.0)
    for i in range(31):
        to_gf(i).start()
    all_of(gz.at[pl.ds(0, 7)], gzs, gzr).wait_send()
    all_of(gf.at[pl.ds(0, 31)], gfs, gfr).wait_recv()
    for e in range(32):
        both_out[e * 4 : (e + 1) * 4, :] = gf[e]
    all_of(gf.at[pl.ds(0, 31)], gfs, gfr).wait_send()


def mix(panel, signs, rows):
    vm = pl.BlockSpec(memory_space=pltpu.VMEM)
    hbm = pl.BlockSpec(memory_space=pltpu.HBM)
    V = pltpu.VMEM
    D = pltpu.SemaphoreType.DMA
    return pl.pallas_call(
        mix_kernel,
        out_shape=jax.ShapeDtypeStruct((160, 128), F32),
        in_specs=[hbm, vm],
        out_specs=vm,
        scratch_shapes=[
            V((64, LOCAL), F32),
            V((LOCAL // 128, 128), F32),
            V((4096,), jnp.int32),
            pltpu.SMEM((4096,), jnp.int32),
            V((LOCAL + HALF, 128), F32),
            V((8, 128, 128), F32),
            V((8, 128, 128), F32),
            V((8, 128, 128), F32),
            V((2, 128, 128), F32),
            V((6, 3, 32, 128), F32),
            V((24, 8, 128), F32),
            V((2, 16, 128), F32),
            V((32, 4, 128), F32),
            V((31, 4, 128), F32),
            V((8, 4, 128), F32),
            V((32, 4, 128), F32),
            D((9,)),
            D, D((8,)), D, D, D, D((6,)), D, D, D, D, D, D, D, D, D, D,
        ],
        compiler_params=pltpu.CompilerParams(
            collective_id=0, has_side_effects=True, vmem_limit_bytes=52 << 20
        ),
        name="mix",
    )(panel, jnp.concatenate([signs, rows]))


def rows_const(v, j):
    return jnp.broadcast_to(v[:, j : j + 1], (8, 128))


def factor_kernel(both_ref, basis_ref, tri_ref, a_ref, u_ref, p_ref):
    n, width = 128, 32
    col = lax.axis_index("col")
    a_ref[:, :128] = both_ref[:128, :]
    samples = jnp.concatenate([both_ref[128:, :], jnp.zeros((96, 128), F32)], axis=0)
    a_ref[:, 128:] = samples.T
    lane = lax.broadcasted_iota(jnp.int32, (8, 128), 1)
    for panel in range(n // width):
        top = panel * width
        nb = width // 8
        blocks = [
            [a_ref[top + 8 * i : top + 8 * i + 8, 128 * t : 128 * t + 128] for t in range(2)]
            for i in range(nb)
        ]
        for j in range(nb):
            at = top + 8 * j
            for i in range(2):
                p_ref[2 * at + 8 * i : 2 * at + 8 * i + 8, :] = blocks[j][i]
            rows = [[p_ref[pl.ds(2 * at + 8 * i + k, 8, stride=0), :] for i in range(2)] for k in range(8)]
            d = {(i, k): rows_const(rows[i][0], at + k) for i in range(8) for k in range(i + 1)}
            below = [[rows_const(blocks[i][0], at + k) for k in range(8)] for i in range(j + 1, nb)]
            for k in range(8):
                r = lax.rsqrt(d[k, k])
                for i in range(k + 1, 8):
                    d[i, k] = d[i, k] * r
                for i in range(k + 1, 8):
                    for q in range(k + 1, i + 1):
                        d[i, q] = d[i, q] - d[i, k] * d[q, k]
                for t in range(2):
                    rows[k][t] = rows[k][t] * r
                    for q in range(k + 1, 8):
                        rows[q][t] = rows[q][t] - d[q, k] * rows[k][t]
                for b in below:
                    b[k] = b[k] * r
                    for q in range(k + 1, 8):
                        b[q] = b[q] - d[q, k] * b[k]
            for k in range(8):
                keep = lane >= at + k
                u_ref[at + k : at + k + 1, :128] = jnp.where(keep, rows[k][0], 0.0)[:1]
                u_ref[at + k : at + k + 1, 128:] = rows[k][1][:1]
            for i in range(j + 1, nb):
                b = below[i - j - 1]
                for t in range(2):
                    v = blocks[i][t]
                    for k in range(8):
                        v = v - b[k] * rows[k][t]
                    blocks[i][t] = v
        if top + width < n:
            rest = top + width
            u = u_ref[top:rest, :]
            hi, mid, low = split(u)
            left = jnp.concatenate([v[:, :128] for v in (hi, hi, mid, hi, low, mid)], axis=0)
            right = jnp.concatenate([hi, mid, hi, low, hi, mid], axis=0)
            upd = jnp.dot(left.T[rest:, :], right, preferred_element_type=F32)
            a_ref[rest:, :] = a_ref[rest:, :] - upd
    half = pl.ds(pl.multiple_of(col * 64, 64), 64)
    tri_ref[...] = u_ref[half, :128]
    basis_ref[...] = u_ref[half, 128:].T[:32]


def factor(both):
    vm = pl.BlockSpec(memory_space=pltpu.VMEM)
    return pl.pallas_call(
        factor_kernel,
        out_shape=(jax.ShapeDtypeStruct((32, 64), F32), jax.ShapeDtypeStruct((64, 128), F32)),
        in_specs=[vm],
        out_specs=(vm, vm),
        scratch_shapes=[pltpu.VMEM((128, 256), F32), pltpu.VMEM((128, 256), F32), pltpu.VMEM((256, 128), F32)],
        compiler_params=pltpu.CompilerParams(vmem_limit_bytes=16 << 20),
        name="factor",
    )(both)


def shards(tall_panel_array, row_signs, sample_rows):
    basis, upper = factor(mix(tall_panel_array, row_signs, sample_rows))
    return basis.T, upper


def solution(mesh):
    return jax.shard_map(
        shards,
        mesh=mesh,
        in_specs=(P("col", "row"), P("row"), P()),
        out_specs=(P("col", "row"), P("col", None)),
        check_vma=False,
    )
```

```python
import jax
import jax.numpy as jnp
from jax import lax
from jax.experimental import pallas as pl
from jax.experimental.pallas import tpu as pltpu
from jax.sharding import PartitionSpec as P

F32 = jnp.float32
BF16 = jnp.bfloat16
MESH = pl.DeviceIdType.MESH
LO = 256
NU = 32
LOCAL = LO * NU
HALF = LOCAL // 2


def parity(bits):
    bits = bits ^ (bits >> 4)
    bits = bits ^ (bits >> 2)
    bits = bits ^ (bits >> 1)
    return bits & 1


def split(v):
    hi = v.astype(BF16)
    rest = v - hi.astype(F32)
    mid = rest.astype(BF16)
    return hi, mid, (rest - mid.astype(F32)).astype(BF16)


def away(k):
    b = (k + 6) & 7
    return 4 + (b >> 1) * (1 - 2 * (b & 1)) - (b & 1) + ((b + 1) >> 3) - ((k + 1) >> 3)


def mix_kernel(
    x_hbm, ints, both_out,
    xv, sgv, idxv, idx, t, zo, acc, rc, rf, ry, rz, mx, gs, gr, gz, gf,
    in_sem, cs, cr, fs, fr, ys, yr, zs, zr, xs, xr, gss, gsr, gzs, gzr, gfs, gfr,
):
    row, col = lax.axis_index("row"), lax.axis_index("col")
    c = row & 1
    y = (row >> 2) & 3
    z = row >> 4
    x = col * 2 + ((row >> 1) & 1)

    y_at = [((y + d) & 3) * 4 for d in range(4)]
    x_at = [(((x + d) & 1) * 2, ((x + d) & 3) >> 1) for d in range(4)]
    c_at = [c, 1 - c]
    z_at = [((z + d) & 7) * 16 for d in range(8)]

    def near(dy, dx, dc, dz=0):
        return {"row": z_at[dz] + y_at[dy] + x_at[dx][0] + c_at[dc], "col": x_at[dx][1]}

    def along_z(d):
        return {"row": ((z + d) & 7) * 16 + (row & 15), "col": col}

    plane = [(dy, dx, dc) for dy in (2, 1, 3, 0) for dx in (2, 1, 3, 0) for dc in (1, 0) if dy or dx or dc]
    z_order = (4, 3, 5, 2, 6, 1, 7)

    def loop(first, last, body):
        def step(i, carry):
            body(i)
            return carry

        lax.fori_loop(first, last, step, 0)

    place_rows = pltpu.make_async_copy(idxv, idx, in_sem.at[8])

    def fetch(i):
        at = pl.ds(pl.multiple_of(i * 8, 8), 8)
        return pltpu.make_async_copy(x_hbm.at[at], xv.at[at], in_sem.at[i])

    loop(0, 8, lambda i: fetch(i).start())
    idxv[...] = ints[pl.ds(LOCAL, 4096)] & (LOCAL - 1)
    place_rows.start()
    sgv[...] = ints[pl.ds(0, LOCAL)].reshape(LOCAL // 128, 128).astype(F32)

    barrier = pltpu.get_barrier_semaphore()
    early = [(0, 0, 1, 0), (0, 0, 0, 1), (0, 0, 0, 7)] + [(d, 0, 0, 0) for d in (2, 1, 3)]
    early += [(0, i, 0, d) for d in (4, 3, 5, 2, 6, 0) for i in range(4) if d or i]
    for at in early:
        pl.semaphore_signal(barrier, inc=1, device_id=near(*at), device_id_type=MESH)
    ri = lax.broadcasted_iota(jnp.int32, (LO, LO), 0)
    ci = lax.broadcasted_iota(jnp.int32, (LO, LO), 1)
    h = ((1 - 2 * parity(ri & ci)).astype(F32) * (1.0 / 1024.0)).astype(BF16)
    h = jnp.concatenate([h, h, h], axis=1)

    def butterfly(i):
        fetch(i).wait()
        rows = pl.ds(pl.multiple_of(i * 8, 8), 8)
        for bt in range(LO // 128):
            v = []
            for u in range(NU):
                at = u * LO + bt * 128
                v.append(xv[rows, at : at + 128] * sgv[at // 128 : at // 128 + 1, :])
            step = 1
            while step < NU:
                for u in range(NU):
                    if not u & step:
                        v[u], v[u + step] = v[u] + v[u + step], v[u] - v[u + step]
                step *= 2
            for u in range(NU):
                at = u * LO + bt * 128
                xv[rows, at : at + 128] = v[u]

    loop(0, 8, butterfly)

    def lower(g):
        parts = []
        for i in range(2):
            for top in (0, NU // 2):
                at = (2 * g + i + top) * LO
                v = xv[:, at : at + LO]
                parts.append(jnp.concatenate(split(v), axis=1))
        w = jnp.concatenate(parts, axis=0)
        o = lax.dot_general(h, w, (((1,), (1,)), ((), ())), preferred_element_type=F32)
        for i in range(2):
            part = o[:, 128 * i : 128 * i + 128]
            at = (2 * g + i) * LO
            t[at : at + LO, :] = part
            t[at + LOCAL : at + LOCAL + LO, :] = part
            t[at + HALF : at + HALF + LO, :] = pltpu.roll(part, 64, 1)

    for g in range(NU // 4):
        lower(g)

    place_rows.wait()
    pl.semaphore_wait(barrier, len(early))

    left = lax.broadcasted_iota(jnp.int32, (8, 128), 1) < 64
    sub = lax.broadcasted_iota(jnp.int32, (8, 128), 0)
    table = t.reshape(LOCAL + HALF, 1, 128)

    def pick(out, k, cq):
        zq = (z + away(k)) & 7

        def body(i, carry):
            q = zq * 16 + i * 2 + cq
            sign = (1 - 2 * parity(row & q)).astype(F32)
            for top in (0, 8):
                v = None
                for j in range(8):
                    a = jnp.broadcast_to(table[idx[q * 32 + top + j]], (8, 128))
                    b = jnp.broadcast_to(table[idx[q * 32 + 16 + top + j] + HALF], (8, 128))
                    r = jnp.where(left, a, b)
                    v = r if v is None else jnp.where(sub == j, r, v)
                out[k, pl.ds(pl.multiple_of(i * 16, 16) + top, 8), :] = v * sign
            return carry

        lax.fori_loop(0, 8, body, 0, unroll=8)

    def remote(src, dst, ss, rs, device):
        return pltpu.make_async_remote_copy(
            src_ref=src, dst_ref=dst, send_sem=ss, recv_sem=rs,
            device_id=device, device_id_type=MESH,
        )

    def all_of(ref, ss, rs):
        return remote(ref, ref, ss, rs, near(0, 0, 1))

    def block(i):
        return pl.ds(pl.multiple_of(i * 32, 32), 32)

    def to_core(k):
        return remote(zo.at[k], rc.at[k], cs, cr.at[k], near(0, 0, 1))

    def to_y(k, d):
        return remote(acc.at[k, block((y + d) & 3)], ry.at[k - 2, d - 1], ys, yr.at[k - 2], near(d, 0, 0))

    def quarter(k, i):
        return acc.at[k, pl.ds(pl.multiple_of(y * 32 + (i & 1) * 16 + (i >> 1) * 8, 8), 8)]

    def to_z(k, zq, d):
        device = {"row": zq * 16 + y_at[0] + x_at[d][0] + c, "col": x_at[d][1]}
        return remote(quarter(k, (x + d) & 3), rz.at[(k - 2) * 4 + x], zs, zr, device)

    def to_first(k):
        return remote(acc.at[k], rf.at[k], fs, fr, along_z(away(k)))

    def pick_other(k):
        pick(zo, k, 1 - c)
        to_core(k).start()

    def send_y(k):
        for d in (2, 1, 3):
            to_y(k, d).start()

    def pick_own(k):
        pick(acc, k, c)
        to_core(k).wait_recv()
        acc[k] = acc[k] + rc[k]
        pl.when(k < 2)(lambda: to_first(k).start())
        pl.when((k >= 2) & (k < 7))(lambda: send_y(k))

    def add_y(k):
        all_of(ry.at[k - 2], ys, yr.at[k - 2]).wait_recv()
        mine = block(y)
        acc[k, mine] = (acc[k, mine] + ry[k - 2, 0]) + (ry[k - 2, 1] + ry[k - 2, 2])

    def pass_z(k):
        add_y(k)
        zq = (z + away(k)) & 7
        for d in (2, 1, 3, 0):
            to_z(k, zq, d).start()

    loop(0, 8, pick_other)
    loop(0, 8, pick_own)
    all_of(rf, fs, fr).wait_recv()
    acc[7] = acc[7] + (rf[0] + rf[1])
    send_y(7)
    loop(2, 7, pass_z)
    add_y(7)
    for d in (2, 1, 3):
        to_z(7, z, d).start()
    rz[20 + x] = quarter(7, x)[...]
    all_of(zo, cs, cr.at[0]).wait_send()
    all_of(rf, fs, fr).wait_send()
    all_of(ry, ys, yr.at[0]).wait_send()
    others = all_of(rz.at[pl.ds(0, 23)], zs, zr)
    others.wait_recv()

    def total(i):
        v = [rz[4 * k + i] for k in range(6)] + [rz[4 * k + i + 1] for k in range(6)]
        while len(v) > 1:
            v = [v[j] + v[j + 1] if j + 1 < len(v) else v[j] for j in range(0, len(v), 2)]
        return v[0]

    a0, a1 = total(0), total(2)
    first = jnp.concatenate([a0[:, :64], a1[:, :64]], axis=1)
    second = jnp.concatenate([a0[:, 64:], a1[:, 64:]], axis=1)
    m = jnp.concatenate([first, second], axis=0)
    hi, mid, low = split(m)
    deep = jnp.concatenate([hi, hi, mid, hi, low, mid], axis=0)
    g = jnp.dot(deep.T, jnp.concatenate([hi, mid, hi, low, hi, mid], axis=0), preferred_element_type=F32)
    for e in range(32):
        gs[e] = g[4 * e : 4 * e + 4]

    place = x * 8 + y * 2 + c

    def to_gs(i):
        dy, dx, dc = plane[i]
        e = ((x + dx) & 3) * 8 + ((y + dy) & 3) * 2 + c_at[dc]
        return remote(gs.at[e], gr.at[i], gss, gsr, near(dy, dx, dc))

    to_mate = remote(mx.at[x >> 1], mx.at[x >> 1], xs, xr, near(0, 2, 0))

    def to_gz(d):
        return remote(gz.at[z], gz.at[z], gzs, gzr, near(0, 0, 0, d))

    def to_gf(i):
        return remote(gf.at[place], gf.at[place], gfs, gfr, near(*plane[i]))

    for i in range(31):
        to_gs(i).start()
    mx[x >> 1] = m
    to_mate.start()
    others.wait_send()
    all_of(gr, gss, gsr).wait_recv()
    v = [gr[i] for i in range(31)] + [gs[place]]
    while len(v) > 1:
        v = [v[j] + v[j + 1] for j in range(0, len(v), 2)]
    gz[z] = v[0]
    for d in z_order:
        to_gz(d).start()
    all_of(gr, gss, gsr).wait_send()
    to_mate.wait()
    for i in range(2):
        for j in range(2):
            both_out[128 + 16 * j + 8 * i : 136 + 16 * j + 8 * i, :] = mx[i, 8 * j : 8 * j + 8]
    all_of(gz.at[pl.ds(0, 7)], gzs, gzr).wait_recv()
    gf[place] = (((gz[0] + gz[1]) + (gz[2] + gz[3])) + ((gz[4] + gz[5]) + (gz[6] + gz[7]))) * (1.0 / 4096.0)
    for i in range(31):
        to_gf(i).start()
    all_of(gz.at[pl.ds(0, 7)], gzs, gzr).wait_send()
    all_of(gf.at[pl.ds(0, 31)], gfs, gfr).wait_recv()
    for e in range(32):
        both_out[e * 4 : (e + 1) * 4, :] = gf[e]
    all_of(gf.at[pl.ds(0, 31)], gfs, gfr).wait_send()


def mix(panel, signs, rows):
    vm = pl.BlockSpec(memory_space=pltpu.VMEM)
    hbm = pl.BlockSpec(memory_space=pltpu.HBM)
    V = pltpu.VMEM
    D = pltpu.SemaphoreType.DMA
    return pl.pallas_call(
        mix_kernel,
        out_shape=jax.ShapeDtypeStruct((160, 128), F32),
        in_specs=[hbm, vm],
        out_specs=vm,
        scratch_shapes=[
            V((64, LOCAL), F32),
            V((LOCAL // 128, 128), F32),
            V((4096,), jnp.int32),
            pltpu.SMEM((4096,), jnp.int32),
            V((LOCAL + HALF, 128), F32),
            V((8, 128, 128), F32),
            V((8, 128, 128), F32),
            V((8, 128, 128), F32),
            V((2, 128, 128), F32),
            V((6, 3, 32, 128), F32),
            V((24, 8, 128), F32),
            V((2, 16, 128), F32),
            V((32, 4, 128), F32),
            V((31, 4, 128), F32),
            V((8, 4, 128), F32),
            V((32, 4, 128), F32),
            D((9,)),
            D, D((8,)), D, D, D, D((6,)), D, D, D, D, D, D, D, D, D, D,
        ],
        compiler_params=pltpu.CompilerParams(
            collective_id=0, has_side_effects=True, vmem_limit_bytes=52 << 20
        ),
        name="mix",
    )(panel, jnp.concatenate([signs, rows]))


def rows_const(v, j):
    return jnp.broadcast_to(v[:, j : j + 1], (8, 128))


def factor_kernel(both_ref, basis_ref, tri_ref, a_ref, u_ref, p_ref, q_ref):
    n, width = 128, 32
    col = lax.axis_index("col")
    a_ref[:, :128] = both_ref[:128, :]
    samples = jnp.concatenate([both_ref[128:, :], jnp.zeros((96, 128), F32)], axis=0)
    a_ref[:, 128:] = samples.T
    lane = lax.broadcasted_iota(jnp.int32, (8, 128), 1)
    for panel in range(n // width):
        top = panel * width
        nb = width // 8
        blocks = [
            [a_ref[top + 8 * i : top + 8 * i + 8, 128 * t : 128 * t + 128] for t in range(2)]
            for i in range(nb)
        ]
        for j in range(nb):
            at = top + 8 * j
            for i in range(2):
                p_ref[2 * at + 8 * i : 2 * at + 8 * i + 8, :] = blocks[j][i]
            rows = [[p_ref[pl.ds(2 * at + 8 * i + k, 8, stride=0), :] for i in range(2)] for k in range(8)]
            for k in range(8):
                q_ref[8 * (at + k) : 8 * (at + k) + 8, :] = rows_const(blocks[j][0], at + k)
            d = {(i, k): q_ref[pl.ds(8 * (at + k) + i, 8, stride=0), :] for i in range(8) for k in range(i + 1)}
            below = [[rows_const(blocks[i][0], at + k) for k in range(8)] for i in range(j + 1, nb)]
            for k in range(8):
                r = lax.rsqrt(d[k, k])
                for i in range(k + 1, 8):
                    d[i, k] = d[i, k] * r
                for i in range(k + 1, 8):
                    for q in range(k + 1, i + 1):
                        d[i, q] = d[i, q] - d[i, k] * d[q, k]
                for t in range(2):
                    rows[k][t] = rows[k][t] * r
                    for q in range(k + 1, 8):
                        rows[q][t] = rows[q][t] - d[q, k] * rows[k][t]
                for b in below:
                    b[k] = b[k] * r
                    for q in range(k + 1, 8):
                        b[q] = b[q] - d[q, k] * b[k]
            for k in range(8):
                keep = lane >= at + k
                u_ref[at + k : at + k + 1, :128] = jnp.where(keep, rows[k][0], 0.0)[:1]
                u_ref[at + k : at + k + 1, 128:] = rows[k][1][:1]
            for i in range(j + 1, nb):
                b = below[i - j - 1]
                for t in range(2):
                    v = blocks[i][t]
                    for k in range(8):
                        v = v - b[k] * rows[k][t]
                    blocks[i][t] = v
        if top + width < n:
            rest = top + width
            u = u_ref[top:rest, :]
            hi, mid, low = split(u)
            left = jnp.concatenate([v[:, :128] for v in (hi, hi, mid, hi, low, mid)], axis=0)
            right = jnp.concatenate([hi, mid, hi, low, hi, mid], axis=0)
            upd = jnp.dot(left.T[rest:, :], right, preferred_element_type=F32)
            a_ref[rest:, :] = a_ref[rest:, :] - upd
    half = pl.ds(pl.multiple_of(col * 64, 64), 64)
    tri_ref[...] = u_ref[half, :128]
    basis_ref[...] = u_ref[half, 128:].T[:32]


def factor(both):
    vm = pl.BlockSpec(memory_space=pltpu.VMEM)
    return pl.pallas_call(
        factor_kernel,
        out_shape=(jax.ShapeDtypeStruct((32, 64), F32), jax.ShapeDtypeStruct((64, 128), F32)),
        in_specs=[vm],
        out_specs=(vm, vm),
        scratch_shapes=[pltpu.VMEM((128, 256), F32), pltpu.VMEM((128, 256), F32), pltpu.VMEM((256, 128), F32), pltpu.VMEM((1024, 128), F32)],
        compiler_params=pltpu.CompilerParams(vmem_limit_bytes=16 << 20),
        name="factor",
    )(both)


def shards(tall_panel_array, row_signs, sample_rows):
    basis, upper = factor(mix(tall_panel_array, row_signs, sample_rows))
    return basis.T, upper


def solution(mesh):
    return jax.shard_map(
        shards,
        mesh=mesh,
        in_specs=(P("col", "row"), P("row"), P()),
        out_specs=(P("col", "row"), P("col", None)),
        check_vma=False,
    )
```

```python
import jax
import jax.numpy as jnp
from jax import lax
from jax.experimental import pallas as pl
from jax.experimental.pallas import tpu as pltpu
from jax.sharding import PartitionSpec as P

F32 = jnp.float32
BF16 = jnp.bfloat16
MESH = pl.DeviceIdType.MESH
LO = 256
NU = 32
LOCAL = LO * NU
HALF = LOCAL // 2


def parity(bits):
    bits = bits ^ (bits >> 4)
    bits = bits ^ (bits >> 2)
    bits = bits ^ (bits >> 1)
    return bits & 1


def split(v):
    hi = v.astype(BF16)
    rest = v - hi.astype(F32)
    mid = rest.astype(BF16)
    return hi, mid, (rest - mid.astype(F32)).astype(BF16)


def away(k):
    b = (k + 6) & 7
    return 4 + (b >> 1) * (1 - 2 * (b & 1)) - (b & 1) + ((b + 1) >> 3) - ((k + 1) >> 3)


def mix_kernel(
    x_hbm, ints, both_out,
    xv, sgv, idxv, idx, t, zo, acc, rc, rf, ry, rz, mx, gs, gr, gz, gf,
    in_sem, cs, cr, fs, fr, ys, yr, zs, zr, xs, xr, gss, gsr, gzs, gzr, gfs, gfr,
):
    row, col = lax.axis_index("row"), lax.axis_index("col")
    c = row & 1
    y = (row >> 2) & 3
    z = row >> 4
    x = col * 2 + ((row >> 1) & 1)

    y_at = [((y + d) & 3) * 4 for d in range(4)]
    x_at = [(((x + d) & 1) * 2, ((x + d) & 3) >> 1) for d in range(4)]
    c_at = [c, 1 - c]
    z_at = [((z + d) & 7) * 16 for d in range(8)]

    def near(dy, dx, dc, dz=0):
        return {"row": z_at[dz] + y_at[dy] + x_at[dx][0] + c_at[dc], "col": x_at[dx][1]}

    def along_z(d):
        return {"row": ((z + d) & 7) * 16 + (row & 15), "col": col}

    plane = [(dy, dx, dc) for dy in (2, 1, 3, 0) for dx in (2, 1, 3, 0) for dc in (1, 0) if dy or dx or dc]
    z_order = (4, 3, 5, 2, 6, 1, 7)

    def loop(first, last, body):
        def step(i, carry):
            body(i)
            return carry

        lax.fori_loop(first, last, step, 0)

    place_rows = pltpu.make_async_copy(idxv, idx, in_sem.at[8])

    def fetch(i):
        at = pl.ds(pl.multiple_of(i * 8, 8), 8)
        return pltpu.make_async_copy(x_hbm.at[at], xv.at[at], in_sem.at[i])

    loop(0, 8, lambda i: fetch(i).start())
    picks = (ints[pl.ds(LOCAL, 4096)] & (LOCAL - 1)).reshape(32, 128)
    idxv[...] = (picks | ((pltpu.roll(picks, 112, 1) + HALF) << 14)).reshape(4096)
    place_rows.start()
    sgv[...] = ints[pl.ds(0, LOCAL)].reshape(LOCAL // 128, 128).astype(F32)

    barrier = pltpu.get_barrier_semaphore()
    early = [(0, 0, 1, 0), (0, 0, 0, 1), (0, 0, 0, 7)] + [(d, 0, 0, 0) for d in (2, 1, 3)]
    early += [(0, i, 0, d) for d in (4, 3, 5, 2, 6, 0) for i in range(4) if d or i]
    for at in early:
        pl.semaphore_signal(barrier, inc=1, device_id=near(*at), device_id_type=MESH)
    ri = lax.broadcasted_iota(jnp.int32, (LO, LO), 0)
    ci = lax.broadcasted_iota(jnp.int32, (LO, LO), 1)
    h = ((1 - 2 * parity(ri & ci)).astype(F32) * (1.0 / 1024.0)).astype(BF16)
    h = jnp.concatenate([h, h, h], axis=1)

    def butterfly(i):
        fetch(i).wait()
        rows = pl.ds(pl.multiple_of(i * 8, 8), 8)
        for bt in range(LO // 128):
            v = []
            for u in range(NU):
                at = u * LO + bt * 128
                v.append(xv[rows, at : at + 128] * sgv[at // 128 : at // 128 + 1, :])
            step = 1
            while step < NU:
                for u in range(NU):
                    if not u & step:
                        v[u], v[u + step] = v[u] + v[u + step], v[u] - v[u + step]
                step *= 2
            for u in range(NU):
                at = u * LO + bt * 128
                xv[rows, at : at + 128] = v[u]

    loop(0, 8, butterfly)

    def lower(g):
        parts = []
        for i in range(2):
            for top in (0, NU // 2):
                at = (2 * g + i + top) * LO
                v = xv[:, at : at + LO]
                parts.append(jnp.concatenate(split(v), axis=1))
        w = jnp.concatenate(parts, axis=0)
        o = lax.dot_general(h, w, (((1,), (1,)), ((), ())), preferred_element_type=F32)
        for i in range(2):
            part = o[:, 128 * i : 128 * i + 128]
            at = (2 * g + i) * LO
            t[at : at + LO, :] = part
            t[at + LOCAL : at + LOCAL + LO, :] = part
            t[at + HALF : at + HALF + LO, :] = pltpu.roll(part, 64, 1)

    for g in range(NU // 4):
        lower(g)

    place_rows.wait()
    pl.semaphore_wait(barrier, len(early))

    left = lax.broadcasted_iota(jnp.int32, (8, 128), 1) < 64
    sub = lax.broadcasted_iota(jnp.int32, (8, 128), 0)
    table = t.reshape(LOCAL + HALF, 1, 128)

    def pick(out, k, cq):
        zq = (z + away(k)) & 7

        def body(i, carry):
            q = zq * 16 + i * 2 + cq
            sign = (1 - 2 * parity(row & q)).astype(F32)
            for top in (0, 8):
                v = None
                for j in range(8):
                    both = idx[q * 32 + top + j]
                    a = jnp.broadcast_to(table[both & 16383], (8, 128))
                    b = jnp.broadcast_to(table[both >> 14], (8, 128))
                    r = jnp.where(left, a, b)
                    v = r if v is None else jnp.where(sub == j, r, v)
                out[k, pl.ds(pl.multiple_of(i * 16, 16) + top, 8), :] = v * sign
            return carry

        lax.fori_loop(0, 8, body, 0, unroll=8)

    def remote(src, dst, ss, rs, device):
        return pltpu.make_async_remote_copy(
            src_ref=src, dst_ref=dst, send_sem=ss, recv_sem=rs,
            device_id=device, device_id_type=MESH,
        )

    def all_of(ref, ss, rs):
        return remote(ref, ref, ss, rs, near(0, 0, 1))

    def block(i):
        return pl.ds(pl.multiple_of(i * 32, 32), 32)

    def to_core(k):
        return remote(zo.at[k], rc.at[k], cs, cr.at[k], near(0, 0, 1))

    def to_y(k, d):
        return remote(acc.at[k, block((y + d) & 3)], ry.at[k - 2, d - 1], ys, yr.at[k - 2], near(d, 0, 0))

    def quarter(k, i):
        return acc.at[k, pl.ds(pl.multiple_of(y * 32 + (i & 1) * 16 + (i >> 1) * 8, 8), 8)]

    def to_z(k, zq, d):
        device = {"row": zq * 16 + y_at[0] + x_at[d][0] + c, "col": x_at[d][1]}
        return remote(quarter(k, (x + d) & 3), rz.at[(k - 2) * 4 + x], zs, zr, device)

    def to_first(k):
        return remote(acc.at[k], rf.at[k], fs, fr, along_z(away(k)))

    def pick_other(k):
        pick(zo, k, 1 - c)
        to_core(k).start()

    def send_y(k):
        for d in (2, 1, 3):
            to_y(k, d).start()

    def pick_own(k):
        pick(acc, k, c)
        to_core(k).wait_recv()
        acc[k] = acc[k] + rc[k]
        pl.when(k < 2)(lambda: to_first(k).start())
        pl.when((k >= 2) & (k < 7))(lambda: send_y(k))

    def add_y(k):
        all_of(ry.at[k - 2], ys, yr.at[k - 2]).wait_recv()
        mine = block(y)
        acc[k, mine] = (acc[k, mine] + ry[k - 2, 0]) + (ry[k - 2, 1] + ry[k - 2, 2])

    def pass_z(k):
        add_y(k)
        zq = (z + away(k)) & 7
        for d in (2, 1, 3, 0):
            to_z(k, zq, d).start()

    loop(0, 8, pick_other)
    loop(0, 8, pick_own)
    all_of(rf, fs, fr).wait_recv()
    acc[7] = acc[7] + (rf[0] + rf[1])
    send_y(7)
    loop(2, 7, pass_z)
    add_y(7)
    for d in (2, 1, 3):
        to_z(7, z, d).start()
    rz[20 + x] = quarter(7, x)[...]
    all_of(zo, cs, cr.at[0]).wait_send()
    all_of(rf, fs, fr).wait_send()
    all_of(ry, ys, yr.at[0]).wait_send()
    others = all_of(rz.at[pl.ds(0, 23)], zs, zr)
    others.wait_recv()

    def total(i):
        v = [rz[4 * k + i] for k in range(6)] + [rz[4 * k + i + 1] for k in range(6)]
        while len(v) > 1:
            v = [v[j] + v[j + 1] if j + 1 < len(v) else v[j] for j in range(0, len(v), 2)]
        return v[0]

    a0, a1 = total(0), total(2)
    first = jnp.concatenate([a0[:, :64], a1[:, :64]], axis=1)
    second = jnp.concatenate([a0[:, 64:], a1[:, 64:]], axis=1)
    m = jnp.concatenate([first, second], axis=0)
    hi, mid, low = split(m)
    deep = jnp.concatenate([hi, hi, mid, hi, low, mid], axis=0)
    g = jnp.dot(deep.T, jnp.concatenate([hi, mid, hi, low, hi, mid], axis=0), preferred_element_type=F32)
    for e in range(32):
        gs[e] = g[4 * e : 4 * e + 4]

    place = x * 8 + y * 2 + c

    def to_gs(i):
        dy, dx, dc = plane[i]
        e = ((x + dx) & 3) * 8 + ((y + dy) & 3) * 2 + c_at[dc]
        return remote(gs.at[e], gr.at[i], gss, gsr, near(dy, dx, dc))

    to_mate = remote(mx.at[x >> 1], mx.at[x >> 1], xs, xr, near(0, 2, 0))

    def to_gz(d):
        return remote(gz.at[z], gz.at[z], gzs, gzr, near(0, 0, 0, d))

    def to_gf(i):
        return remote(gf.at[place], gf.at[place], gfs, gfr, near(*plane[i]))

    for i in range(31):
        to_gs(i).start()
    mx[x >> 1] = m
    to_mate.start()
    others.wait_send()
    all_of(gr, gss, gsr).wait_recv()
    v = [gr[i] for i in range(31)] + [gs[place]]
    while len(v) > 1:
        v = [v[j] + v[j + 1] for j in range(0, len(v), 2)]
    gz[z] = v[0]
    for d in z_order:
        to_gz(d).start()
    all_of(gr, gss, gsr).wait_send()
    to_mate.wait()
    for i in range(2):
        for j in range(2):
            both_out[128 + 16 * j + 8 * i : 136 + 16 * j + 8 * i, :] = mx[i, 8 * j : 8 * j + 8]
    all_of(gz.at[pl.ds(0, 7)], gzs, gzr).wait_recv()
    gf[place] = (((gz[0] + gz[1]) + (gz[2] + gz[3])) + ((gz[4] + gz[5]) + (gz[6] + gz[7]))) * (1.0 / 4096.0)
    for i in range(31):
        to_gf(i).start()
    all_of(gz.at[pl.ds(0, 7)], gzs, gzr).wait_send()
    all_of(gf.at[pl.ds(0, 31)], gfs, gfr).wait_recv()
    for e in range(32):
        both_out[e * 4 : (e + 1) * 4, :] = gf[e]
    all_of(gf.at[pl.ds(0, 31)], gfs, gfr).wait_send()


def mix(panel, signs, rows):
    vm = pl.BlockSpec(memory_space=pltpu.VMEM)
    hbm = pl.BlockSpec(memory_space=pltpu.HBM)
    V = pltpu.VMEM
    D = pltpu.SemaphoreType.DMA
    return pl.pallas_call(
        mix_kernel,
        out_shape=jax.ShapeDtypeStruct((160, 128), F32),
        in_specs=[hbm, vm],
        out_specs=vm,
        scratch_shapes=[
            V((64, LOCAL), F32),
            V((LOCAL // 128, 128), F32),
            V((4096,), jnp.int32),
            pltpu.SMEM((4096,), jnp.int32),
            V((LOCAL + HALF, 128), F32),
            V((8, 128, 128), F32),
            V((8, 128, 128), F32),
            V((8, 128, 128), F32),
            V((2, 128, 128), F32),
            V((6, 3, 32, 128), F32),
            V((24, 8, 128), F32),
            V((2, 16, 128), F32),
            V((32, 4, 128), F32),
            V((31, 4, 128), F32),
            V((8, 4, 128), F32),
            V((32, 4, 128), F32),
            D((9,)),
            D, D((8,)), D, D, D, D((6,)), D, D, D, D, D, D, D, D, D, D,
        ],
        compiler_params=pltpu.CompilerParams(
            collective_id=0, has_side_effects=True, vmem_limit_bytes=52 << 20
        ),
        name="mix",
    )(panel, jnp.concatenate([signs, rows]))


def rows_const(v, j):
    return jnp.broadcast_to(v[:, j : j + 1], (8, 128))


def factor_kernel(both_ref, basis_ref, tri_ref, a_ref, u_ref, p_ref, q_ref):
    n, width = 128, 32
    col = lax.axis_index("col")
    a_ref[:, :128] = both_ref[:128, :]
    samples = jnp.concatenate([both_ref[128:, :], jnp.zeros((96, 128), F32)], axis=0)
    a_ref[:, 128:] = samples.T
    lane = lax.broadcasted_iota(jnp.int32, (8, 128), 1)
    for panel in range(n // width):
        top = panel * width
        nb = width // 8
        blocks = [
            [a_ref[top + 8 * i : top + 8 * i + 8, 128 * t : 128 * t + 128] for t in range(2)]
            for i in range(nb)
        ]
        for j in range(nb):
            at = top + 8 * j
            for i in range(2):
                p_ref[2 * at + 8 * i : 2 * at + 8 * i + 8, :] = blocks[j][i]
            rows = [[p_ref[pl.ds(2 * at + 8 * i + k, 8, stride=0), :] for i in range(2)] for k in range(8)]
            for k in range(8):
                q_ref[8 * (at + k) : 8 * (at + k) + 8, :] = rows_const(blocks[j][0], at + k)
            d = {(i, k): q_ref[pl.ds(8 * (at + k) + i, 8, stride=0), :] for i in range(8) for k in range(i + 1)}
            below = [[rows_const(blocks[i][0], at + k) for k in range(8)] for i in range(j + 1, nb)]
            for k in range(8):
                r = lax.rsqrt(d[k, k])
                for i in range(k + 1, 8):
                    d[i, k] = d[i, k] * r
                for i in range(k + 1, 8):
                    for q in range(k + 1, i + 1):
                        d[i, q] = d[i, q] - d[i, k] * d[q, k]
                for t in range(2):
                    rows[k][t] = rows[k][t] * r
                    for q in range(k + 1, 8):
                        rows[q][t] = rows[q][t] - d[q, k] * rows[k][t]
                for b in below:
                    b[k] = b[k] * r
                    for q in range(k + 1, 8):
                        b[q] = b[q] - d[q, k] * b[k]
            for k in range(8):
                keep = lane >= at + k
                u_ref[at + k : at + k + 1, :128] = jnp.where(keep, rows[k][0], 0.0)[:1]
                u_ref[at + k : at + k + 1, 128:] = rows[k][1][:1]
            for i in range(j + 1, nb):
                b = below[i - j - 1]
                for t in range(2):
                    v = blocks[i][t]
                    for k in range(8):
                        v = v - b[k] * rows[k][t]
                    blocks[i][t] = v
        if top + width < n:
            rest = top + width
            u = u_ref[top:rest, :]
            hi, mid, low = split(u)
            left = jnp.concatenate([v[:, :128] for v in (hi, hi, mid, hi, low, mid)], axis=0)
            right = jnp.concatenate([hi, mid, hi, low, hi, mid], axis=0)
            upd = jnp.dot(left.T[rest:, :], right, preferred_element_type=F32)
            a_ref[rest:, :] = a_ref[rest:, :] - upd
    half = pl.ds(pl.multiple_of(col * 64, 64), 64)
    tri_ref[...] = u_ref[half, :128]
    basis_ref[...] = u_ref[half, 128:].T[:32]


def factor(both):
    vm = pl.BlockSpec(memory_space=pltpu.VMEM)
    return pl.pallas_call(
        factor_kernel,
        out_shape=(jax.ShapeDtypeStruct((32, 64), F32), jax.ShapeDtypeStruct((64, 128), F32)),
        in_specs=[vm],
        out_specs=(vm, vm),
        scratch_shapes=[pltpu.VMEM((128, 256), F32), pltpu.VMEM((128, 256), F32), pltpu.VMEM((256, 128), F32), pltpu.VMEM((1024, 128), F32)],
        compiler_params=pltpu.CompilerParams(vmem_limit_bytes=16 << 20),
        name="factor",
    )(both)


def shards(tall_panel_array, row_signs, sample_rows):
    basis, upper = factor(mix(tall_panel_array, row_signs, sample_rows))
    return basis.T, upper


def solution(mesh):
    return jax.shard_map(
        shards,
        mesh=mesh,
        in_specs=(P("col", "row"), P("row"), P()),
        out_specs=(P("col", "row"), P("col", None)),
        check_vma=False,
    )
```

```python
import jax
import jax.numpy as jnp
from jax import lax
from jax.experimental import pallas as pl
from jax.experimental.pallas import tpu as pltpu
from jax.sharding import PartitionSpec as P

F32 = jnp.float32
BF16 = jnp.bfloat16
MESH = pl.DeviceIdType.MESH
LO = 256
NU = 32
LOCAL = LO * NU
HALF = LOCAL // 2


def parity(bits):
    bits = bits ^ (bits >> 4)
    bits = bits ^ (bits >> 2)
    bits = bits ^ (bits >> 1)
    return bits & 1


def split(v):
    hi = v.astype(BF16)
    rest = v - hi.astype(F32)
    mid = rest.astype(BF16)
    return hi, mid, (rest - mid.astype(F32)).astype(BF16)


def away(k):
    b = (k + 6) & 7
    return 4 + (b >> 1) * (1 - 2 * (b & 1)) - (b & 1) + ((b + 1) >> 3) - ((k + 1) >> 3)


def mix_kernel(
    x_hbm, ints, both_out,
    xv, sgv, idxv, idx, t, zo, acc, rc, rf, ry, rz, mx, gs, gr, gz, gf,
    in_sem, cs, cr, fs, fr, ys, yr, zs, zr, xs, xr, gss, gsr, gzs, gzr, gfs, gfr,
):
    row, col = lax.axis_index("row"), lax.axis_index("col")
    c = row & 1
    y = (row >> 2) & 3
    z = row >> 4
    x = col * 2 + ((row >> 1) & 1)

    y_at = [((y + d) & 3) * 4 for d in range(4)]
    x_at = [(((x + d) & 1) * 2, ((x + d) & 3) >> 1) for d in range(4)]
    c_at = [c, 1 - c]
    z_at = [((z + d) & 7) * 16 for d in range(8)]

    def near(dy, dx, dc, dz=0):
        return {"row": z_at[dz] + y_at[dy] + x_at[dx][0] + c_at[dc], "col": x_at[dx][1]}

    def along_z(d):
        return {"row": ((z + d) & 7) * 16 + (row & 15), "col": col}

    plane = [(dy, dx, dc) for dy in (2, 1, 3, 0) for dx in (2, 1, 3, 0) for dc in (1, 0) if dy or dx or dc]
    z_order = (4, 3, 5, 2, 6, 1, 7)

    def loop(first, last, body):
        def step(i, carry):
            body(i)
            return carry

        lax.fori_loop(first, last, step, 0)

    place_rows = pltpu.make_async_copy(idxv, idx, in_sem.at[8])

    def fetch(i):
        at = pl.ds(pl.multiple_of(i * 8, 8), 8)
        return pltpu.make_async_copy(x_hbm.at[at], xv.at[at], in_sem.at[i])

    loop(0, 8, lambda i: fetch(i).start())
    idxv[...] = ints[pl.ds(LOCAL, 4096)] & (LOCAL - 1)
    place_rows.start()
    sgv[...] = ints[pl.ds(0, LOCAL)].reshape(LOCAL // 128, 128).astype(F32)

    barrier = pltpu.get_barrier_semaphore()
    early = [(0, 0, 1, 0), (0, 0, 0, 1), (0, 0, 0, 7)] + [(d, 0, 0, 0) for d in (2, 1, 3)]
    early += [(0, i, 0, d) for d in (4, 3, 5, 2, 6, 0) for i in range(4) if d or i]
    for at in early:
        pl.semaphore_signal(barrier, inc=1, device_id=near(*at), device_id_type=MESH)
    ri = lax.broadcasted_iota(jnp.int32, (LO, LO), 0)
    ci = lax.broadcasted_iota(jnp.int32, (LO, LO), 1)
    h = ((1 - 2 * parity(ri & ci)).astype(F32) * (1.0 / 1024.0)).astype(BF16)
    h = jnp.concatenate([h, h, h], axis=1)

    def butterfly(i):
        fetch(i).wait()
        rows = pl.ds(pl.multiple_of(i * 8, 8), 8)
        for bt in range(LO // 128):
            v = []
            for u in range(NU):
                at = u * LO + bt * 128
                v.append(xv[rows, at : at + 128] * sgv[at // 128 : at // 128 + 1, :])
            step = 1
            while step < NU:
                for u in range(NU):
                    if not u & step:
                        v[u], v[u + step] = v[u] + v[u + step], v[u] - v[u + step]
                step *= 2
            for u in range(NU):
                at = u * LO + bt * 128
                xv[rows, at : at + 128] = v[u]

    loop(0, 8, butterfly)

    def lower(g):
        parts = []
        for i in range(2):
            for top in (0, NU // 2):
                at = (2 * g + i + top) * LO
                v = xv[:, at : at + LO]
                parts.append(jnp.concatenate(split(v), axis=1))
        w = jnp.concatenate(parts, axis=0)
        o = lax.dot_general(h, w, (((1,), (1,)), ((), ())), preferred_element_type=F32)
        for i in range(2):
            part = o[:, 128 * i : 128 * i + 128]
            at = (2 * g + i) * LO
            t[at : at + LO, :] = part
            t[at + LOCAL : at + LOCAL + LO, :] = part
            t[at + HALF : at + HALF + LO, :] = pltpu.roll(part, 64, 1)

    for g in range(NU // 4):
        lower(g)

    place_rows.wait()
    pl.semaphore_wait(barrier, len(early))

    left = lax.broadcasted_iota(jnp.int32, (8, 128), 1) < 64
    sub = lax.broadcasted_iota(jnp.int32, (8, 128), 0)
    table = t.reshape(LOCAL + HALF, 1, 128)

    def pick(out, k, cq):
        zq = (z + away(k)) & 7

        def body(i, carry):
            q = zq * 16 + i * 2 + cq
            sign = (1 - 2 * parity(row & q)).astype(F32)
            for top in (0, 8):
                v = None
                for j in range(8):
                    a = jnp.broadcast_to(table[idx[q * 32 + top + j]], (8, 128))
                    b = jnp.broadcast_to(table[idx[q * 32 + 16 + top + j] + HALF], (8, 128))
                    r = jnp.where(left, a, b)
                    v = r if v is None else jnp.where(sub == j, r, v)
                out[k, pl.ds(pl.multiple_of(i * 16, 16) + top, 8), :] = v * sign
            return carry

        lax.fori_loop(0, 8, body, 0, unroll=8)

    def remote(src, dst, ss, rs, device):
        return pltpu.make_async_remote_copy(
            src_ref=src, dst_ref=dst, send_sem=ss, recv_sem=rs,
            device_id=device, device_id_type=MESH,
        )

    def all_of(ref, ss, rs):
        return remote(ref, ref, ss, rs, near(0, 0, 1))

    def block(i):
        return pl.ds(pl.multiple_of(i * 32, 32), 32)

    def to_core(k):
        return remote(zo.at[k], rc.at[k], cs, cr.at[k], near(0, 0, 1))

    def to_y(k, d):
        return remote(acc.at[k, block((y + d) & 3)], ry.at[k - 2, d - 1], ys, yr.at[k - 2], near(d, 0, 0))

    def quarter(k, i):
        return acc.at[k, pl.ds(pl.multiple_of(y * 32 + (i & 1) * 16 + (i >> 1) * 8, 8), 8)]

    def to_z(k, zq, d):
        device = {"row": zq * 16 + y_at[0] + x_at[d][0] + c, "col": x_at[d][1]}
        return remote(quarter(k, (x + d) & 3), rz.at[(k - 2) * 4 + x], zs, zr, device)

    def to_first(k):
        return remote(acc.at[k], rf.at[k], fs, fr, along_z(away(k)))

    def pick_other(k):
        pick(zo, k, 1 - c)
        to_core(k).start()

    def send_y(k):
        for d in (2, 1, 3):
            to_y(k, d).start()

    def pick_own(k):
        pick(acc, k, c)
        to_core(k).wait_recv()
        acc[k] = acc[k] + rc[k]
        pl.when(k < 2)(lambda: to_first(k).start())
        pl.when((k >= 2) & (k < 7))(lambda: send_y(k))

    def add_y(k):
        all_of(ry.at[k - 2], ys, yr.at[k - 2]).wait_recv()
        mine = block(y)
        acc[k, mine] = (acc[k, mine] + ry[k - 2, 0]) + (ry[k - 2, 1] + ry[k - 2, 2])

    def pass_z(k):
        add_y(k)
        zq = (z + away(k)) & 7
        for d in (2, 1, 3, 0):
            to_z(k, zq, d).start()

    loop(0, 8, pick_other)
    loop(0, 8, pick_own)
    loop(2, 4, pass_z)
    all_of(rf, fs, fr).wait_recv()
    acc[7] = acc[7] + (rf[0] + rf[1])
    send_y(7)
    loop(4, 7, pass_z)
    add_y(7)
    for d in (2, 1, 3):
        to_z(7, z, d).start()
    rz[20 + x] = quarter(7, x)[...]
    all_of(zo, cs, cr.at[0]).wait_send()
    all_of(rf, fs, fr).wait_send()
    all_of(ry, ys, yr.at[0]).wait_send()
    others = all_of(rz.at[pl.ds(0, 23)], zs, zr)
    others.wait_recv()

    def total(i):
        v = [rz[4 * k + i] for k in range(6)] + [rz[4 * k + i + 1] for k in range(6)]
        while len(v) > 1:
            v = [v[j] + v[j + 1] if j + 1 < len(v) else v[j] for j in range(0, len(v), 2)]
        return v[0]

    a0, a1 = total(0), total(2)
    first = jnp.concatenate([a0[:, :64], a1[:, :64]], axis=1)
    second = jnp.concatenate([a0[:, 64:], a1[:, 64:]], axis=1)
    m = jnp.concatenate([first, second], axis=0)
    hi, mid, low = split(m)
    deep = jnp.concatenate([hi, hi, mid, hi, low, mid], axis=0)
    g = jnp.dot(deep.T, jnp.concatenate([hi, mid, hi, low, hi, mid], axis=0), preferred_element_type=F32)
    for e in range(32):
        gs[e] = g[4 * e : 4 * e + 4]

    place = x * 8 + y * 2 + c

    def to_gs(i):
        dy, dx, dc = plane[i]
        e = ((x + dx) & 3) * 8 + ((y + dy) & 3) * 2 + c_at[dc]
        return remote(gs.at[e], gr.at[i], gss, gsr, near(dy, dx, dc))

    to_mate = remote(mx.at[x >> 1], mx.at[x >> 1], xs, xr, near(0, 2, 0))

    def to_gz(d):
        return remote(gz.at[z], gz.at[z], gzs, gzr, near(0, 0, 0, d))

    def to_gf(i):
        return remote(gf.at[place], gf.at[place], gfs, gfr, near(*plane[i]))

    for i in range(31):
        to_gs(i).start()
    mx[x >> 1] = m
    to_mate.start()
    others.wait_send()
    all_of(gr, gss, gsr).wait_recv()
    v = [gr[i] for i in range(31)] + [gs[place]]
    while len(v) > 1:
        v = [v[j] + v[j + 1] for j in range(0, len(v), 2)]
    gz[z] = v[0]
    for d in z_order:
        to_gz(d).start()
    all_of(gr, gss, gsr).wait_send()
    to_mate.wait()
    for i in range(2):
        for j in range(2):
            both_out[128 + 16 * j + 8 * i : 136 + 16 * j + 8 * i, :] = mx[i, 8 * j : 8 * j + 8]
    all_of(gz.at[pl.ds(0, 7)], gzs, gzr).wait_recv()
    gf[place] = (((gz[0] + gz[1]) + (gz[2] + gz[3])) + ((gz[4] + gz[5]) + (gz[6] + gz[7]))) * (1.0 / 4096.0)
    for i in range(31):
        to_gf(i).start()
    all_of(gz.at[pl.ds(0, 7)], gzs, gzr).wait_send()
    all_of(gf.at[pl.ds(0, 31)], gfs, gfr).wait_recv()
    for e in range(32):
        both_out[e * 4 : (e + 1) * 4, :] = gf[e]
    all_of(gf.at[pl.ds(0, 31)], gfs, gfr).wait_send()


def mix(panel, signs, rows):
    vm = pl.BlockSpec(memory_space=pltpu.VMEM)
    hbm = pl.BlockSpec(memory_space=pltpu.HBM)
    V = pltpu.VMEM
    D = pltpu.SemaphoreType.DMA
    return pl.pallas_call(
        mix_kernel,
        out_shape=jax.ShapeDtypeStruct((160, 128), F32),
        in_specs=[hbm, vm],
        out_specs=vm,
        scratch_shapes=[
            V((64, LOCAL), F32),
            V((LOCAL // 128, 128), F32),
            V((4096,), jnp.int32),
            pltpu.SMEM((4096,), jnp.int32),
            V((LOCAL + HALF, 128), F32),
            V((8, 128, 128), F32),
            V((8, 128, 128), F32),
            V((8, 128, 128), F32),
            V((2, 128, 128), F32),
            V((6, 3, 32, 128), F32),
            V((24, 8, 128), F32),
            V((2, 16, 128), F32),
            V((32, 4, 128), F32),
            V((31, 4, 128), F32),
            V((8, 4, 128), F32),
            V((32, 4, 128), F32),
            D((9,)),
            D, D((8,)), D, D, D, D((6,)), D, D, D, D, D, D, D, D, D, D,
        ],
        compiler_params=pltpu.CompilerParams(
            collective_id=0, has_side_effects=True, vmem_limit_bytes=52 << 20
        ),
        name="mix",
    )(panel, jnp.concatenate([signs, rows]))


def rows_const(v, j):
    return jnp.broadcast_to(v[:, j : j + 1], (8, 128))


def factor_kernel(both_ref, basis_ref, tri_ref, a_ref, u_ref, p_ref, q_ref):
    n, width = 128, 32
    col = lax.axis_index("col")
    a_ref[:, :128] = both_ref[:128, :]
    samples = jnp.concatenate([both_ref[128:, :], jnp.zeros((96, 128), F32)], axis=0)
    a_ref[:, 128:] = samples.T
    lane = lax.broadcasted_iota(jnp.int32, (8, 128), 1)
    for panel in range(n // width):
        top = panel * width
        nb = width // 8
        blocks = [
            [a_ref[top + 8 * i : top + 8 * i + 8, 128 * t : 128 * t + 128] for t in range(2)]
            for i in range(nb)
        ]
        for j in range(nb):
            at = top + 8 * j
            for i in range(2):
                p_ref[2 * at + 8 * i : 2 * at + 8 * i + 8, :] = blocks[j][i]
            rows = [[p_ref[pl.ds(2 * at + 8 * i + k, 8, stride=0), :] for i in range(2)] for k in range(8)]
            for k in range(8):
                q_ref[8 * (at + k) : 8 * (at + k) + 8, :] = rows_const(blocks[j][0], at + k)
            d = {(i, k): q_ref[pl.ds(8 * (at + k) + i, 8, stride=0), :] for i in range(8) for k in range(i + 1)}
            below = [[rows_const(blocks[i][0], at + k) for k in range(8)] for i in range(j + 1, nb)]
            for k in range(8):
                r = lax.rsqrt(d[k, k])
                for i in range(k + 1, 8):
                    d[i, k] = d[i, k] * r
                for i in range(k + 1, 8):
                    for q in range(k + 1, i + 1):
                        d[i, q] = d[i, q] - d[i, k] * d[q, k]
                for t in range(2):
                    rows[k][t] = rows[k][t] * r
                    for q in range(k + 1, 8):
                        rows[q][t] = rows[q][t] - d[q, k] * rows[k][t]
                for b in below:
                    b[k] = b[k] * r
                    for q in range(k + 1, 8):
                        b[q] = b[q] - d[q, k] * b[k]
            for k in range(8):
                keep = lane >= at + k
                u_ref[at + k : at + k + 1, :128] = jnp.where(keep, rows[k][0], 0.0)[:1]
                u_ref[at + k : at + k + 1, 128:] = rows[k][1][:1]
            for i in range(j + 1, nb):
                b = below[i - j - 1]
                for t in range(2):
                    v = blocks[i][t]
                    for k in range(8):
                        v = v - b[k] * rows[k][t]
                    blocks[i][t] = v
        if top + width < n:
            rest = top + width
            u = u_ref[top:rest, :]
            hi, mid, low = split(u)
            left = jnp.concatenate([v[:, :128] for v in (hi, hi, mid, hi, low, mid)], axis=0)
            right = jnp.concatenate([hi, mid, hi, low, hi, mid], axis=0)
            upd = jnp.dot(left.T[rest:, :], right, preferred_element_type=F32)
            a_ref[rest:, :] = a_ref[rest:, :] - upd
    half = pl.ds(pl.multiple_of(col * 64, 64), 64)
    tri_ref[...] = u_ref[half, :128]
    basis_ref[...] = u_ref[half, 128:].T[:32]


def factor(both):
    vm = pl.BlockSpec(memory_space=pltpu.VMEM)
    return pl.pallas_call(
        factor_kernel,
        out_shape=(jax.ShapeDtypeStruct((32, 64), F32), jax.ShapeDtypeStruct((64, 128), F32)),
        in_specs=[vm],
        out_specs=(vm, vm),
        scratch_shapes=[pltpu.VMEM((128, 256), F32), pltpu.VMEM((128, 256), F32), pltpu.VMEM((256, 128), F32), pltpu.VMEM((1024, 128), F32)],
        compiler_params=pltpu.CompilerParams(vmem_limit_bytes=16 << 20),
        name="factor",
    )(both)


def shards(tall_panel_array, row_signs, sample_rows):
    basis, upper = factor(mix(tall_panel_array, row_signs, sample_rows))
    return basis.T, upper


def solution(mesh):
    return jax.shard_map(
        shards,
        mesh=mesh,
        in_specs=(P("col", "row"), P("row"), P()),
        out_specs=(P("col", "row"), P("col", None)),
        check_vma=False,
    )
```

```python
import jax
import jax.numpy as jnp
from jax import lax
from jax.experimental import pallas as pl
from jax.experimental.pallas import tpu as pltpu
from jax.sharding import PartitionSpec as P

F32 = jnp.float32
BF16 = jnp.bfloat16
MESH = pl.DeviceIdType.MESH
LO = 256
NU = 32
LOCAL = LO * NU
HALF = LOCAL // 2


def parity(bits):
    bits = bits ^ (bits >> 4)
    bits = bits ^ (bits >> 2)
    bits = bits ^ (bits >> 1)
    return bits & 1


def split(v):
    hi = v.astype(BF16)
    rest = v - hi.astype(F32)
    mid = rest.astype(BF16)
    return hi, mid, (rest - mid.astype(F32)).astype(BF16)


def away(k):
    b = (k + 6) & 7
    return 4 + (b >> 1) * (1 - 2 * (b & 1)) - (b & 1) + ((b + 1) >> 3) - ((k + 1) >> 3)


def mix_kernel(
    x_hbm, ints, both_out,
    xv, sgv, idxv, idx, t, zo, acc, rc, rf, ry, rz, mx, gs, gr, gz, gf,
    in_sem, cs, cr, fs, fr, ys, yr, zs, zr, xs, xr, gss, gsr, gzs, gzr, gfs, gfr,
):
    row, col = lax.axis_index("row"), lax.axis_index("col")
    c = row & 1
    y = (row >> 2) & 3
    z = row >> 4
    x = col * 2 + ((row >> 1) & 1)

    y_at = [((y + d) & 3) * 4 for d in range(4)]
    x_at = [(((x + d) & 1) * 2, ((x + d) & 3) >> 1) for d in range(4)]
    c_at = [c, 1 - c]
    z_at = [((z + d) & 7) * 16 for d in range(8)]

    def near(dy, dx, dc, dz=0):
        return {"row": z_at[dz] + y_at[dy] + x_at[dx][0] + c_at[dc], "col": x_at[dx][1]}

    def along_z(d):
        return {"row": ((z + d) & 7) * 16 + (row & 15), "col": col}

    plane = [(dy, dx, dc) for dy in (2, 1, 3, 0) for dx in (2, 1, 3, 0) for dc in (1, 0) if dy or dx or dc]
    z_order = (4, 3, 5, 2, 6, 1, 7)

    def loop(first, last, body):
        def step(i, carry):
            body(i)
            return carry

        lax.fori_loop(first, last, step, 0)

    place_rows = pltpu.make_async_copy(idxv, idx, in_sem.at[8])

    def fetch(i):
        at = pl.ds(pl.multiple_of(i * 8, 8), 8)
        return pltpu.make_async_copy(x_hbm.at[at], xv.at[at], in_sem.at[i])

    loop(0, 8, lambda i: fetch(i).start())
    idxv[...] = ints[pl.ds(LOCAL, 4096)] & (LOCAL - 1)
    place_rows.start()
    sgv[...] = ints[pl.ds(0, LOCAL)].reshape(LOCAL // 128, 128).astype(F32)

    barrier = pltpu.get_barrier_semaphore()
    early = [(0, 0, 1, 0), (0, 0, 0, 1), (0, 0, 0, 7)] + [(d, 0, 0, 0) for d in (2, 1, 3)]
    early += [(0, i, 0, d) for d in (4, 3, 5, 2, 6, 0) for i in range(4) if d or i]
    for at in early:
        pl.semaphore_signal(barrier, inc=1, device_id=near(*at), device_id_type=MESH)
    ri = lax.broadcasted_iota(jnp.int32, (LO, LO), 0)
    ci = lax.broadcasted_iota(jnp.int32, (LO, LO), 1)
    h = ((1 - 2 * parity(ri & ci)).astype(F32) * (1.0 / 1024.0)).astype(BF16)
    h = jnp.concatenate([h, h, h], axis=1)

    def butterfly(i):
        fetch(i).wait()
        rows = pl.ds(pl.multiple_of(i * 8, 8), 8)
        for bt in range(LO // 128):
            v = []
            for u in range(NU):
                at = u * LO + bt * 128
                v.append(xv[rows, at : at + 128] * sgv[at // 128 : at // 128 + 1, :])
            step = 1
            while step < NU:
                for u in range(NU):
                    if not u & step:
                        v[u], v[u + step] = v[u] + v[u + step], v[u] - v[u + step]
                step *= 2
            for u in range(NU):
                at = u * LO + bt * 128
                xv[rows, at : at + 128] = v[u]

    loop(0, 8, butterfly)

    def lower(g):
        parts = []
        for i in range(2):
            for top in (0, NU // 2):
                at = (2 * g + i + top) * LO
                v = xv[:, at : at + LO]
                parts.append(jnp.concatenate(split(v), axis=1))
        w = jnp.concatenate(parts, axis=0)
        o = lax.dot_general(h, w, (((1,), (1,)), ((), ())), preferred_element_type=F32)
        for i in range(2):
            part = o[:, 128 * i : 128 * i + 128]
            at = (2 * g + i) * LO
            t[at : at + LO, :] = part
            t[at + LOCAL : at + LOCAL + LO, :] = part
            t[at + HALF : at + HALF + LO, :] = pltpu.roll(part, 64, 1)

    for g in range(NU // 4):
        lower(g)

    place_rows.wait()
    pl.semaphore_wait(barrier, len(early))

    left = lax.broadcasted_iota(jnp.int32, (8, 128), 1) < 64
    sub = lax.broadcasted_iota(jnp.int32, (8, 128), 0)
    table = t.reshape(LOCAL + HALF, 1, 128)

    def pick(out, k, cq):
        zq = (z + away(k)) & 7

        def body(i, carry):
            q = zq * 16 + i * 2 + cq
            sign = (1 - 2 * parity(row & q)).astype(F32)
            for top in (0, 8):
                v = None
                for j in range(8):
                    a = jnp.broadcast_to(table[idx[q * 32 + top + j]], (8, 128))
                    b = jnp.broadcast_to(table[idx[q * 32 + 16 + top + j] + HALF], (8, 128))
                    r = jnp.where(left, a, b)
                    v = r if v is None else jnp.where(sub == j, r, v)
                out[k, pl.ds(pl.multiple_of(i * 16, 16) + top, 8), :] = v * sign
            return carry

        lax.fori_loop(0, 8, body, 0, unroll=8)

    def remote(src, dst, ss, rs, device):
        return pltpu.make_async_remote_copy(
            src_ref=src, dst_ref=dst, send_sem=ss, recv_sem=rs,
            device_id=device, device_id_type=MESH,
        )

    def all_of(ref, ss, rs):
        return remote(ref, ref, ss, rs, near(0, 0, 1))

    def block(i):
        return pl.ds(pl.multiple_of(i * 32, 32), 32)

    def to_core(k):
        return remote(zo.at[k], rc.at[k], cs, cr.at[k], near(0, 0, 1))

    def to_y(k, d):
        return remote(acc.at[k, block((y + d) & 3)], ry.at[k - 2, d - 1], ys, yr.at[k - 2], near(d, 0, 0))

    def quarter(k, i):
        return acc.at[k, pl.ds(pl.multiple_of(y * 32 + (i & 1) * 16 + (i >> 1) * 8, 8), 8)]

    def to_z(k, zq, d):
        device = {"row": zq * 16 + y_at[0] + x_at[d][0] + c, "col": x_at[d][1]}
        return remote(quarter(k, (x + d) & 3), rz.at[(k - 2) * 4 + x], zs, zr, device)

    def to_first(k):
        return remote(acc.at[k], rf.at[k], fs, fr, along_z(away(k)))

    def pick_other(k):
        pick(zo, k, 1 - c)
        to_core(k).start()

    def send_y(k):
        for d in (2, 1, 3):
            to_y(k, d).start()

    def pick_own(k):
        pick(acc, k, c)
        to_core(k).wait_recv()
        acc[k] = acc[k] + rc[k]
        pl.when(k < 2)(lambda: to_first(k).start())
        pl.when((k >= 2) & (k < 7))(lambda: send_y(k))

    def add_y(k):
        all_of(ry.at[k - 2], ys, yr.at[k - 2]).wait_recv()
        mine = block(y)
        acc[k, mine] = (acc[k, mine] + ry[k - 2, 0]) + (ry[k - 2, 1] + ry[k - 2, 2])

    def pass_z(k):
        add_y(k)
        zq = (z + away(k)) & 7
        for d in (2, 1, 3, 0):
            to_z(k, zq, d).start()

    loop(0, 8, pick_other)
    loop(0, 8, pick_own)
    all_of(rf, fs, fr).wait_recv()
    acc[7] = acc[7] + (rf[0] + rf[1])
    send_y(7)
    for k in range(2, 7):
        pass_z(k)
    add_y(7)
    for d in (2, 1, 3):
        to_z(7, z, d).start()
    rz[20 + x] = quarter(7, x)[...]
    all_of(zo, cs, cr.at[0]).wait_send()
    all_of(rf, fs, fr).wait_send()
    all_of(ry, ys, yr.at[0]).wait_send()
    others = all_of(rz.at[pl.ds(0, 23)], zs, zr)
    others.wait_recv()

    def total(i):
        v = [rz[4 * k + i] for k in range(6)] + [rz[4 * k + i + 1] for k in range(6)]
        while len(v) > 1:
            v = [v[j] + v[j + 1] if j + 1 < len(v) else v[j] for j in range(0, len(v), 2)]
        return v[0]

    a0, a1 = total(0), total(2)
    first = jnp.concatenate([a0[:, :64], a1[:, :64]], axis=1)
    second = jnp.concatenate([a0[:, 64:], a1[:, 64:]], axis=1)
    m = jnp.concatenate([first, second], axis=0)
    hi, mid, low = split(m)
    deep = jnp.concatenate([hi, hi, mid, hi, low, mid], axis=0)
    g = jnp.dot(deep.T, jnp.concatenate([hi, mid, hi, low, hi, mid], axis=0), preferred_element_type=F32)
    for e in range(32):
        gs[e] = g[4 * e : 4 * e + 4]

    place = x * 8 + y * 2 + c

    def to_gs(i):
        dy, dx, dc = plane[i]
        e = ((x + dx) & 3) * 8 + ((y + dy) & 3) * 2 + c_at[dc]
        return remote(gs.at[e], gr.at[i], gss, gsr, near(dy, dx, dc))

    to_mate = remote(mx.at[x >> 1], mx.at[x >> 1], xs, xr, near(0, 2, 0))

    def to_gz(d):
        return remote(gz.at[z], gz.at[z], gzs, gzr, near(0, 0, 0, d))

    def to_gf(i):
        return remote(gf.at[place], gf.at[place], gfs, gfr, near(*plane[i]))

    for i in range(31):
        to_gs(i).start()
    mx[x >> 1] = m
    to_mate.start()
    others.wait_send()
    all_of(gr, gss, gsr).wait_recv()
    v = [gr[i] for i in range(31)] + [gs[place]]
    while len(v) > 1:
        v = [v[j] + v[j + 1] for j in range(0, len(v), 2)]
    gz[z] = v[0]
    for d in z_order:
        to_gz(d).start()
    all_of(gr, gss, gsr).wait_send()
    to_mate.wait()
    for i in range(2):
        for j in range(2):
            both_out[128 + 16 * j + 8 * i : 136 + 16 * j + 8 * i, :] = mx[i, 8 * j : 8 * j + 8]
    all_of(gz.at[pl.ds(0, 7)], gzs, gzr).wait_recv()
    gf[place] = (((gz[0] + gz[1]) + (gz[2] + gz[3])) + ((gz[4] + gz[5]) + (gz[6] + gz[7]))) * (1.0 / 4096.0)
    for i in range(31):
        to_gf(i).start()
    all_of(gz.at[pl.ds(0, 7)], gzs, gzr).wait_send()
    all_of(gf.at[pl.ds(0, 31)], gfs, gfr).wait_recv()
    for e in range(32):
        both_out[e * 4 : (e + 1) * 4, :] = gf[e]
    all_of(gf.at[pl.ds(0, 31)], gfs, gfr).wait_send()


def mix(panel, signs, rows):
    vm = pl.BlockSpec(memory_space=pltpu.VMEM)
    hbm = pl.BlockSpec(memory_space=pltpu.HBM)
    V = pltpu.VMEM
    D = pltpu.SemaphoreType.DMA
    return pl.pallas_call(
        mix_kernel,
        out_shape=jax.ShapeDtypeStruct((160, 128), F32),
        in_specs=[hbm, vm],
        out_specs=vm,
        scratch_shapes=[
            V((64, LOCAL), F32),
            V((LOCAL // 128, 128), F32),
            V((4096,), jnp.int32),
            pltpu.SMEM((4096,), jnp.int32),
            V((LOCAL + HALF, 128), F32),
            V((8, 128, 128), F32),
            V((8, 128, 128), F32),
            V((8, 128, 128), F32),
            V((2, 128, 128), F32),
            V((6, 3, 32, 128), F32),
            V((24, 8, 128), F32),
            V((2, 16, 128), F32),
            V((32, 4, 128), F32),
            V((31, 4, 128), F32),
            V((8, 4, 128), F32),
            V((32, 4, 128), F32),
            D((9,)),
            D, D((8,)), D, D, D, D((6,)), D, D, D, D, D, D, D, D, D, D,
        ],
        compiler_params=pltpu.CompilerParams(
            collective_id=0, has_side_effects=True, vmem_limit_bytes=52 << 20
        ),
        name="mix",
    )(panel, jnp.concatenate([signs, rows]))


def rows_const(v, j):
    return jnp.broadcast_to(v[:, j : j + 1], (8, 128))


def factor_kernel(both_ref, basis_ref, tri_ref, a_ref, u_ref, p_ref, q_ref):
    n, width = 128, 32
    col = lax.axis_index("col")
    a_ref[:, :128] = both_ref[:128, :]
    samples = jnp.concatenate([both_ref[128:, :], jnp.zeros((96, 128), F32)], axis=0)
    a_ref[:, 128:] = samples.T
    lane = lax.broadcasted_iota(jnp.int32, (8, 128), 1)
    for panel in range(n // width):
        top = panel * width
        nb = width // 8
        blocks = [
            [a_ref[top + 8 * i : top + 8 * i + 8, 128 * t : 128 * t + 128] for t in range(2)]
            for i in range(nb)
        ]
        for j in range(nb):
            at = top + 8 * j
            for i in range(2):
                p_ref[2 * at + 8 * i : 2 * at + 8 * i + 8, :] = blocks[j][i]
            rows = [[p_ref[pl.ds(2 * at + 8 * i + k, 8, stride=0), :] for i in range(2)] for k in range(8)]
            for k in range(8):
                q_ref[8 * (at + k) : 8 * (at + k) + 8, :] = rows_const(blocks[j][0], at + k)
            d = {(i, k): q_ref[pl.ds(8 * (at + k) + i, 8, stride=0), :] for i in range(8) for k in range(i + 1)}
            below = [[rows_const(blocks[i][0], at + k) for k in range(8)] for i in range(j + 1, nb)]
            for k in range(8):
                r = lax.rsqrt(d[k, k])
                for i in range(k + 1, 8):
                    d[i, k] = d[i, k] * r
                for i in range(k + 1, 8):
                    for q in range(k + 1, i + 1):
                        d[i, q] = d[i, q] - d[i, k] * d[q, k]
                for t in range(2):
                    rows[k][t] = rows[k][t] * r
                    for q in range(k + 1, 8):
                        rows[q][t] = rows[q][t] - d[q, k] * rows[k][t]
                for b in below:
                    b[k] = b[k] * r
                    for q in range(k + 1, 8):
                        b[q] = b[q] - d[q, k] * b[k]
            for k in range(8):
                keep = lane >= at + k
                u_ref[at + k : at + k + 1, :128] = jnp.where(keep, rows[k][0], 0.0)[:1]
                u_ref[at + k : at + k + 1, 128:] = rows[k][1][:1]
            for i in range(j + 1, nb):
                b = below[i - j - 1]
                for t in range(2):
                    v = blocks[i][t]
                    for k in range(8):
                        v = v - b[k] * rows[k][t]
                    blocks[i][t] = v
        if top + width < n:
            rest = top + width
            u = u_ref[top:rest, :]
            hi, mid, low = split(u)
            left = jnp.concatenate([v[:, :128] for v in (hi, hi, mid, hi, low, mid)], axis=0)
            right = jnp.concatenate([hi, mid, hi, low, hi, mid], axis=0)
            upd = jnp.dot(left.T[rest:, :], right, preferred_element_type=F32)
            a_ref[rest:, :] = a_ref[rest:, :] - upd
    half = pl.ds(pl.multiple_of(col * 64, 64), 64)
    tri_ref[...] = u_ref[half, :128]
    basis_ref[...] = u_ref[half, 128:].T[:32]


def factor(both):
    vm = pl.BlockSpec(memory_space=pltpu.VMEM)
    return pl.pallas_call(
        factor_kernel,
        out_shape=(jax.ShapeDtypeStruct((32, 64), F32), jax.ShapeDtypeStruct((64, 128), F32)),
        in_specs=[vm],
        out_specs=(vm, vm),
        scratch_shapes=[pltpu.VMEM((128, 256), F32), pltpu.VMEM((128, 256), F32), pltpu.VMEM((256, 128), F32), pltpu.VMEM((1024, 128), F32)],
        compiler_params=pltpu.CompilerParams(vmem_limit_bytes=16 << 20),
        name="factor",
    )(both)


def shards(tall_panel_array, row_signs, sample_rows):
    basis, upper = factor(mix(tall_panel_array, row_signs, sample_rows))
    return basis.T, upper


def solution(mesh):
    return jax.shard_map(
        shards,
        mesh=mesh,
        in_specs=(P("col", "row"), P("row"), P()),
        out_specs=(P("col", "row"), P("col", None)),
        check_vma=False,
    )
```
